32 devices in a mesh: dp: 16 (over z, x, core), blk: 2 (over y).
Axes of the slice: x: 2, y: 2, z: 4, core: 2. Of those that a mesh axis runs over, the one named last changes fastest.
Arguments:
- tokens: bfloat16 [16, 2, 2048, 1152], P('dp', None, 'blk'), may hold values from -6 to 6
- cotangent: bfloat16 [16, 2, 2048, 1152], P('dp', None, 'blk'), may hold values from -6 to 6
- condition: bfloat16 [16, 2, 8, 1152], P('dp'), may hold values from -6 to 6
- lengths: int32 [16, 2, 8], P('dp'), may hold values from 0 to 1024, as said below
- adaptive_weight: bfloat16 [1152, 6912], P('dp', 'blk'), may hold values from -0.09375 to 0.09375
- joint_weight: bfloat16 [1152, 3456], P('dp', 'blk'), may hold values from -0.1875 to 0.1875
- output_weight: bfloat16 [1152, 1152], P('dp', 'blk'), may hold values from -0.75 to 0.75
- up_weight: bfloat16 [1152, 4608], P('dp', 'blk'), may hold values from -0.1875 to 0.1875
- down_weight: bfloat16 [4608, 1152], P('dp', 'blk'), may hold values from -0.09375 to 0.09375
- adaptive_bias: bfloat16 [6912], P('blk'), may hold values from -1.5 to 1.5
- query_bias: bfloat16 [1152], P('blk'), may hold values from -3 to 3
- value_bias: bfloat16 [1152], P('blk'), may hold values from -3 to 3
- output_bias: bfloat16 [1152], P('blk'), may hold values from -3 to 3
- up_bias: bfloat16 [4608], P('blk'), may hold values from -3 to 3
- down_bias: bfloat16 [1152], P('blk'), may hold values from -3 to 3
Outputs:
- block_output: float32 [16, 2, 2048, 1152], P('dp', None, 'blk')
- tokens_grad: float32 [16, 2, 2048, 1152], P('dp', None, 'blk')
- condition_grad: float32 [16, 2, 8, 1152], P('dp')
- adaptive_weight_grad: float32 [1152, 6912], P('dp', 'blk')
- joint_weight_grad: float32 [1152, 3456], P('dp', 'blk')
- output_weight_grad: float32 [1152, 1152], P('dp', 'blk')
- up_weight_grad: float32 [1152, 4608], P('dp', 'blk')
- down_weight_grad: float32 [4608, 1152], P('dp', 'blk')
- adaptive_bias_grad: float32 [6912], P('blk')
- query_bias_grad: float32 [1152], P('blk')
- value_bias_grad: float32 [1152], P('blk')
- output_bias_grad: float32 [1152], P('blk')
- up_bias_grad: float32 [4608], P('blk')
- down_bias_grad: float32 [1152], P('blk')
The draws below stay inside these ranges and needn't reach their ends.
Inputs may be any that keep to these rules, and one draw needn't show every extreme that they name: `lengths`: every entry is 0, 256 or 1024; in each pack the nonzero entries come first and add up to 2048, and each pack holds at least one image of 1024 tokens and at least one empty slot.
All inputs are finite; a program needn't handle non-finite values.
Results may differ from the reference program's by a relative error of at most 0.025.
Values may be sent and summed in bfloat16 or wider, within the bound.
A program may use at most 576 MiB of HBM per device.

```python
import jax
import jax.numpy as jnp
from jax import lax

D = 1152
HEADS = 16
HD = 72
FF = 4608
LONG = 1024
SHORT = 256
MICRO = 2
PACK = 2048
ROWS = 1024
IMGS = 8
N_DP = 16
N_BLK = 2


def draw_lengths(key, part):
    key = jax.random.fold_in(key, 11)
    packs = N_DP * MICRO
    most_long = PACK // LONG
    first_key, second_key = jax.random.split(key)
    longs = jax.random.randint(first_key, (packs, 1), 1, most_long + 1).astype(jnp.int32)
    used = longs + (PACK - longs * LONG) // SHORT
    slot = jnp.arange(IMGS, dtype=jnp.int32)[None, :]
    noise = jax.random.randint(second_key, (packs, IMGS), 0, 1 << 20).astype(jnp.int32)
    scores = jnp.where(slot < used, noise * IMGS + slot, (1 << 30) + slot)
    rank = jnp.argsort(jnp.argsort(scores, axis=1), axis=1).astype(jnp.int32)
    sizes = jnp.where(rank < longs, LONG, SHORT)
    length = jnp.where(slot < used, sizes, 0)
    return length.reshape(N_DP, MICRO, IMGS).astype(jnp.int32)


def steps_of(stream_key, extent, cuts, smallest, top_value):
    def one(dim, blocks):
        steps = jax.random.uniform(jax.random.fold_in(jax.random.fold_in(stream_key, 6), dim), (blocks,), jnp.float32, smallest / len(cuts), top_value / len(cuts))
        return jnp.repeat(jnp.exp(steps), extent[dim] // blocks).reshape((-1,) + (1,) * (len(extent) - dim - 1))

    level = one(*cuts[0])
    for cut in cuts[1:]:
        level = level * one(*cut)
    return level


def centred(rng, shape, spread, limit, shards=(), kind=jnp.bfloat16):
    values = jax.random.normal(rng, shape, jnp.float32) * spread
    if len(shards) > 0:
        values = steps_of(rng, shape, shards, -0.22, 0.18) * values
    return jnp.clip(values, min=-limit, max=limit).astype(kind)


def setup_inputs(seed: int = 0) -> dict:
    key_of = jax.random.split(jax.random.key(seed), 16)
    tokens = centred(key_of[0], (N_DP, MICRO, PACK, D), 1.0, 6.0, ((0, 16), (2, 2)))
    cotangent = centred(key_of[1], (N_DP, MICRO, PACK, D), 1.0, 6.0, ((0, 16), (2, 2)))
    condition = centred(key_of[2], (N_DP, MICRO, IMGS, D), 1.0, 6.0, ((0, 16),))
    lengths = draw_lengths(jax.random.fold_in(key_of[15], 71), 0)
    adaptive_weight = centred(key_of[4], (D, 6 * D), (4 * D) ** -0.5, 0.09375, ((0, 16), (1, 2)))
    joint_weight = centred(key_of[5], (D, 3 * D), D ** -0.5, 0.1875, ((0, 16), (1, 2)))
    output_weight = centred(key_of[6], (D, D), (D // 16) ** -0.5, 0.75, ((0, 16), (1, 2)))
    up_weight = centred(key_of[7], (D, FF), D ** -0.5, 0.1875, ((0, 16), (1, 2)))
    down_weight = centred(key_of[8], (FF, D), FF ** -0.5, 0.09375, ((0, 16), (1, 2)))
    adaptive_bias = centred(key_of[9], (6 * D,), 0.25, 1.5, ((0, 2),))
    query_bias = centred(key_of[10], (D,), 0.5, 3.0, ((0, 2),))
    value_bias = centred(key_of[11], (D,), 0.5, 3.0, ((0, 2),))
    output_bias = centred(key_of[12], (D,), 0.5, 3.0, ((0, 2),))
    up_bias = centred(key_of[13], (FF,), 0.5, 3.0, ((0, 2),))
    down_bias = centred(key_of[14], (D,), 0.5, 3.0, ((0, 2),))
    return dict(tokens=tokens, cotangent=cotangent, condition=condition, lengths=lengths, adaptive_weight=adaptive_weight, joint_weight=joint_weight, output_weight=output_weight, up_weight=up_weight, down_weight=down_weight, adaptive_bias=adaptive_bias, query_bias=query_bias, value_bias=value_bias, output_bias=output_bias, up_bias=up_bias, down_bias=down_bias)


@jax.custom_vjp
def low(v):
    return lax.optimization_barrier(v.astype(jnp.bfloat16)).astype(jnp.float32)

@jax.custom_vjp
def low_back(v):
    return v

def low_keep(v):
    return (low(v), None)

def low_pass(kept, grad):
    return (grad,)

def back_keep(v):
    return (v, None)

def back_low(kept, grad):
    return (low(grad),)
low.defvjp(low_keep, low_pass)
low_back.defvjp(back_keep, back_low)
EPSILON = 1e-06
GELU_SCALE = 0.7978845608028654
HIGHEST = lax.Precision.HIGHEST

def product(left, right):
    return jnp.dot(left, right, precision=HIGHEST, preferred_element_type=jnp.float32)

def normalize(values):
    center = values - lax.optimization_barrier(jnp.mean(values, axis=-1, keepdims=True))
    return center * lax.rsqrt(lax.optimization_barrier(jnp.mean(center * center, axis=-1, keepdims=True)) + EPSILON)

def gelu_tanh(values):
    return 0.5 * values * (1.0 + jnp.tanh(GELU_SCALE * (values + 0.044715 * values * values * values)))

def membership(lengths):
    strip = (lengths // N_BLK).astype(jnp.int32)
    ends = jnp.cumsum(strip).astype(jnp.int32)
    starts = ends - strip
    place = (jnp.arange(PACK, dtype=jnp.int32) % ROWS)[:, None]
    inside = (place >= starts[None, :]) & (place < ends[None, :])
    return inside.astype(jnp.float32)

def attention(query, keys, values, member):
    scale = HD ** (-0.5)
    block = min(512, PACK)
    count = PACK // block
    query_blocks = query.reshape(count, block, HEADS, HD)
    member_blocks = member.reshape(count, block, IMGS)
    key_heads = keys.reshape(PACK, HEADS, HD)
    value_heads = values.reshape(PACK, HEADS, HD)

    def one_block(pair):
        part_query, part_member = pair
        scores = jnp.einsum('qhd,khd->hqk', part_query, key_heads, precision=HIGHEST) * scale
        allowed = product(part_member, member.T) > 0.5
        scores = low_back(jnp.where(allowed[None], scores, -1e+30))
        top = lax.optimization_barrier(jnp.max(scores, axis=-1, keepdims=True))
        expo = jnp.exp(scores - top)
        weights = low(expo / lax.optimization_barrier(jnp.sum(expo, axis=-1, keepdims=True)))
        return jnp.einsum('hqk,khd->qhd', weights, value_heads, precision=HIGHEST)
    return lax.map(jax.checkpoint(one_block), (query_blocks, member_blocks)).reshape(PACK, D)

def layer(weights, inputs, condition_rows, member):
    adaptive_matrix, joint_matrix, output_matrix, up_matrix, down_matrix, adaptive_vector, query_vector, value_vector, output_vector, up_vector, down_vector = weights
    cond_act = low(jax.nn.silu(condition_rows))
    modulation = product(cond_act, adaptive_matrix) + adaptive_vector
    per_token = product(member, modulation)
    shift_one, scale_one, gate_one, shift_two, scale_two, gate_two = jnp.split(per_token, 6, axis=1)
    hidden_one = low(normalize(inputs) * (1.0 + scale_one) + shift_one)
    projected = product(hidden_one, joint_matrix)
    query = low_back(low(projected[:, :D] + query_vector))
    keys = low_back(low(projected[:, D:2 * D]))
    values = low_back(low(projected[:, 2 * D:] + value_vector))
    attended = low_back(low(attention(query, keys, values, member)))
    branch_one = low_back(product(attended, output_matrix) + output_vector)
    middle = inputs + gate_one * branch_one
    hidden_two = low(normalize(middle) * (1.0 + scale_two) + shift_two)
    pre_act = low_back(product(hidden_two, up_matrix) + up_vector)
    activated = low(gelu_tanh(pre_act))
    branch_two = low_back(product(activated, down_matrix) + down_vector)
    return middle + gate_two * branch_two

def reference(tokens, cotangent, condition, lengths, adaptive_weight, joint_weight, output_weight, up_weight, down_weight, adaptive_bias, query_bias, value_bias, output_bias, up_bias, down_bias):
    weights = tuple((item.astype(jnp.float32) for item in (adaptive_weight, joint_weight, output_weight, up_weight, down_weight, adaptive_bias, query_bias, value_bias, output_bias, up_bias, down_bias)))
    packs = N_DP * MICRO
    flat_tokens = tokens.astype(jnp.float32).reshape(packs, PACK, D)
    flat_cotangent = cotangent.astype(jnp.float32).reshape(packs, PACK, D)
    flat_condition = condition.astype(jnp.float32).reshape(packs, IMGS, D)
    flat_lengths = lengths.reshape(packs, IMGS)

    def one_pack(totals, item):
        pack_tokens, pack_cotangent, pack_condition, pack_lengths = item
        member = membership(pack_lengths)

        def forward(layer_weights, inputs, condition_rows):
            return layer(layer_weights, inputs, condition_rows, member)
        result, pull = jax.vjp(forward, weights, pack_tokens, pack_condition)
        grad_weights, grad_tokens, grad_condition = pull(pack_cotangent)
        totals = tuple((first + second for first, second in zip(totals, grad_weights)))
        return (totals, (result, grad_tokens, grad_condition))
    start = tuple((jnp.zeros_like(item) for item in weights))
    totals, (results, grad_tokens, grad_condition) = lax.scan(one_pack, start, (flat_tokens, flat_cotangent, flat_condition, flat_lengths))
    return (results.reshape(N_DP, MICRO, PACK, D), grad_tokens.reshape(N_DP, MICRO, PACK, D), grad_condition.reshape(N_DP, MICRO, IMGS, D), totals[0], totals[1], totals[2], totals[3], totals[4], totals[5], totals[6], totals[7], totals[8], totals[9], totals[10])
```

```python
import functools

import jax
import jax.numpy as jnp
from jax import lax
from jax.experimental import pallas as pl
from jax.experimental.pallas import tpu as pltpu
from jax.sharding import PartitionSpec as P

HEADS = 16


EPSILON = 1e-06
GELU_SCALE = 0.7978845608028654
HIGHEST = lax.Precision.HIGHEST
FLOAT = jnp.float32
HALF = jnp.bfloat16


def matmul(left, right):
    return jnp.dot(left, right, preferred_element_type=FLOAT)


def left_outer(left, right):
    return lax.dot_general(left, right, (((0,), (0,)), ((), ())), preferred_element_type=FLOAT)


def right_outer(left, right):
    return lax.dot_general(left, right, (((1,), (1,)), ((), ())), preferred_element_type=FLOAT)


def normalize(values):
    center = values - jnp.mean(values, axis=-1, keepdims=True)
    inverse = lax.rsqrt(jnp.mean(center * center, axis=-1, keepdims=True) + EPSILON)
    return (center * inverse, inverse)


def norm_backward(normed, inverse, grad):
    mean_grad = jnp.mean(grad, axis=-1, keepdims=True)
    mean_cross = jnp.mean(grad * normed, axis=-1, keepdims=True)
    return inverse * (grad - mean_grad - normed * mean_cross)


def gelu_tanh(values):
    return (
        0.5 * values * (1.0 + jnp.tanh(GELU_SCALE * (values + 0.044715 * values * values * values)))
    )


def gelu_slope(values):
    bend = jnp.tanh(GELU_SCALE * (values + 0.044715 * values * values * values))
    return 0.5 * (1.0 + bend) + 0.5 * values * (1.0 - bend * bend) * GELU_SCALE * (
        1.0 + 3.0 * 0.044715 * values * values
    )


def block_size():
    return 512


def block_scores(query_heads, key_part, query_slots, slot_part, scale):
    scores = jnp.einsum("qhd,khd->hqk", query_heads, key_part, preferred_element_type=FLOAT) * scale
    allowed = query_slots[:, None] == slot_part[None, :]
    return jnp.where(allowed[None], scores, -1e30)


def split_blocks(key_all, value_all, key_slots):
    total, width = key_all.shape
    size = block_size()
    count = total // size
    shape = (count, size, HEADS, width // HEADS)
    return (key_all.reshape(shape), value_all.reshape(shape), key_slots.reshape(count, size))


def attend_forward(query, key_all, value_all, query_slots, key_slots, scale):
    rows, width = query.shape
    query_heads = query.reshape(rows, HEADS, width // HEADS)
    key_blocks, value_blocks, slot_blocks = split_blocks(key_all, value_all, key_slots)

    def statistics(carry, item):
        top, mass = carry
        key_part, slot_part = item
        scores = block_scores(query_heads, key_part, query_slots, slot_part, scale)
        new_top = jnp.maximum(top, jnp.max(scores, axis=-1))
        mass = mass * jnp.exp(top - new_top) + jnp.sum(
            jnp.exp(scores - new_top[..., None]), axis=-1
        )
        return ((new_top, mass), None)

    start = (jnp.full((HEADS, rows), -1e30, FLOAT), jnp.zeros((HEADS, rows), FLOAT))
    (top, mass), unused = lax.scan(statistics, start, (key_blocks, slot_blocks))
    log_total = top + jnp.log(mass)

    def accumulate(running, item):
        key_part, value_part, slot_part = item
        scores = block_scores(query_heads, key_part, query_slots, slot_part, scale)
        weights = jnp.exp(scores - log_total[..., None]).astype(HALF)
        return (
            running + jnp.einsum("hqk,khd->qhd", weights, value_part, preferred_element_type=FLOAT),
            None,
        )

    empty = jnp.zeros((rows, HEADS, width // HEADS), FLOAT)
    attended, unused = lax.scan(accumulate, empty, (key_blocks, value_blocks, slot_blocks))
    return (log_total, attended.reshape(rows, width))


def attention_delta(d_attended, attended):
    rows, width = attended.shape
    grad_heads = d_attended.reshape(rows, HEADS, width // HEADS).astype(FLOAT)
    return jnp.einsum("qhd,qhd->hq", grad_heads, attended.reshape(rows, HEADS, width // HEADS))


def attend_backward(
    query, key_all, value_all, query_slots, key_slots, log_total, delta, d_attended, scale
):
    rows, width = query.shape
    total = key_all.shape[0]
    query_heads = query.reshape(rows, HEADS, width // HEADS)
    grad_heads = d_attended.reshape(rows, HEADS, width // HEADS)
    key_blocks, value_blocks, slot_blocks = split_blocks(key_all, value_all, key_slots)

    def one_block(d_query, item):
        key_part, value_part, slot_part = item
        scores = block_scores(query_heads, key_part, query_slots, slot_part, scale)
        weights = jnp.exp(scores - log_total[..., None])
        d_weights = jnp.einsum("qhd,khd->hqk", grad_heads, value_part, preferred_element_type=FLOAT)
        d_scores = (weights * (d_weights - delta[..., None])).astype(HALF)
        d_query = (
            d_query
            + jnp.einsum("hqk,khd->qhd", d_scores, key_part, preferred_element_type=FLOAT) * scale
        )
        d_value_part = jnp.einsum(
            "hqk,qhd->khd", weights.astype(HALF), grad_heads, preferred_element_type=FLOAT
        )
        d_key_part = (
            jnp.einsum("hqk,qhd->khd", d_scores, query_heads, preferred_element_type=FLOAT) * scale
        )
        return (d_query, (d_key_part, d_value_part))

    empty = jnp.zeros((rows, HEADS, width // HEADS), FLOAT)
    d_query, key_parts = lax.scan(one_block, empty, (key_blocks, value_blocks, slot_blocks))
    d_keys, d_values = key_parts
    return (
        d_query.reshape(rows, width),
        d_keys.reshape(total, width),
        d_values.reshape(total, width),
    )


def run_pack(full, tokens_in, cotangent_in, condition_in, lengths_in, blocks, first_block):
    (
        adaptive_matrix,
        joint_matrix,
        output_matrix,
        up_matrix,
        down_matrix,
        adaptive_vector,
        query_vector,
        value_vector,
        output_vector,
        up_vector,
        down_vector,
    ) = full
    rows, width = tokens_in.shape
    scale = (width // HEADS) ** (-0.5)
    inputs = tokens_in.astype(FLOAT)
    strip = lengths_in // blocks
    ends = jnp.cumsum(strip)
    starts = ends - strip
    place = jnp.arange(rows, dtype=jnp.int32)[:, None]
    inside = (place >= starts[None, :]) & (place < ends[None, :])
    member = inside.astype(FLOAT)
    slot_ids = jnp.sum(
        inside.astype(jnp.int32) * jnp.arange(strip.shape[0], dtype=jnp.int32)[None, :], axis=1
    )
    key_slots = jnp.tile(slot_ids, blocks)
    condition_full = condition_in.astype(FLOAT)
    cond_act = jax.nn.silu(condition_full).astype(HALF)
    modulation = matmul(cond_act, adaptive_matrix) + adaptive_vector.astype(FLOAT)
    per_token = jnp.dot(member, modulation, precision=HIGHEST, preferred_element_type=FLOAT)
    shift_one, scale_one, gate_one, shift_two, scale_two, gate_two = jnp.split(per_token, 6, axis=1)
    normed_one, inverse_one = normalize(inputs)
    hidden_one = (normed_one * (1.0 + scale_one) + shift_one).astype(HALF)
    projected = matmul(hidden_one, joint_matrix)
    query = (projected[:, :width] + query_vector.astype(FLOAT)).astype(HALF)
    keys = projected[:, width : 2 * width].astype(HALF)
    values = (projected[:, 2 * width :] + value_vector.astype(FLOAT)).astype(HALF)
    key_all, value_all = (
        lax.all_gather(keys, "blk", axis=0, tiled=True),
        lax.all_gather(values, "blk", axis=0, tiled=True),
    )
    log_total, attended = attend_forward(query, key_all, value_all, slot_ids, key_slots, scale)
    attended_half = attended.astype(HALF)
    branch_one = matmul(attended_half, output_matrix) + output_vector.astype(FLOAT)
    middle = inputs + gate_one * branch_one
    normed_two, inverse_two = normalize(middle)
    hidden_two = (normed_two * (1.0 + scale_two) + shift_two).astype(HALF)
    pre_act = matmul(hidden_two, up_matrix) + up_vector.astype(FLOAT)
    activated = gelu_tanh(pre_act).astype(HALF)
    branch_two = matmul(activated, down_matrix) + down_vector.astype(FLOAT)
    result = middle + gate_two * branch_two
    upstream = cotangent_in.astype(FLOAT)
    d_gate_two = upstream * branch_two
    d_branch_two = (upstream * gate_two).astype(HALF)
    d_pre = (right_outer(d_branch_two, down_matrix) * gelu_slope(pre_act)).astype(HALF)
    d_hidden_two = right_outer(d_pre, up_matrix)
    d_scale_two = d_hidden_two * normed_two
    d_middle = upstream + norm_backward(normed_two, inverse_two, d_hidden_two * (1.0 + scale_two))
    d_gate_one = d_middle * branch_one
    d_branch_one = (d_middle * gate_one).astype(HALF)
    d_attended = right_outer(d_branch_one, output_matrix).astype(HALF)
    delta = attention_delta(d_attended, attended)
    d_query_full, d_key_all, d_value_all = attend_backward(
        query, key_all, value_all, slot_ids, key_slots, log_total, delta, d_attended, scale
    )
    d_key_full, d_value_full = (
        lax.psum_scatter(
            d_key_all.astype(jnp.bfloat16), "blk", scatter_dimension=0, tiled=True
        ).astype(jnp.float32),
        lax.psum_scatter(
            d_value_all.astype(jnp.bfloat16), "blk", scatter_dimension=0, tiled=True
        ).astype(jnp.float32),
    )
    d_query = d_query_full.astype(HALF)
    d_keys = d_key_full.astype(HALF)
    d_values = d_value_full.astype(HALF)
    d_projected = jnp.concatenate([d_query, d_keys, d_values], axis=1)
    d_hidden_one = right_outer(d_projected, joint_matrix)
    d_scale_one = d_hidden_one * normed_one
    d_inputs = d_middle + norm_backward(normed_one, inverse_one, d_hidden_one * (1.0 + scale_one))
    d_per_token = jnp.concatenate(
        [d_hidden_one, d_scale_one, d_gate_one, d_hidden_two, d_scale_two, d_gate_two], axis=1
    )
    d_mod_local = lax.dot_general(
        member,
        d_per_token,
        (((0,), (0,)), ((), ())),
        precision=HIGHEST,
        preferred_element_type=FLOAT,
    )
    d_modulation = lax.psum(d_mod_local.astype(jnp.bfloat16), "blk").astype(jnp.float32)
    sigmoid_cond = jax.nn.sigmoid(condition_full)
    adaptive_float = adaptive_matrix.astype(FLOAT)
    d_condition = (
        lax.dot_general(
            d_modulation,
            adaptive_float,
            (((1,), (1,)), ((), ())),
            precision=HIGHEST,
            preferred_element_type=FLOAT,
        )
        * sigmoid_cond
        * (1.0 + condition_full * (1.0 - sigmoid_cond))
    )
    adaptive_grad = lax.dot_general(
        cond_act.astype(FLOAT),
        d_modulation,
        (((0,), (0,)), ((), ())),
        precision=HIGHEST,
        preferred_element_type=FLOAT,
    )
    local = (
        adaptive_grad * first_block,
        left_outer(hidden_one, d_projected),
        left_outer(attended_half, d_branch_one),
        left_outer(hidden_two, d_pre),
        left_outer(activated, d_branch_two),
        jnp.sum(d_modulation, axis=0) * first_block,
        jnp.sum(d_query.astype(FLOAT), axis=0),
        jnp.sum(d_values.astype(FLOAT), axis=0),
        jnp.sum(d_branch_one.astype(FLOAT), axis=0),
        jnp.sum(d_pre.astype(FLOAT), axis=0),
        jnp.sum(d_branch_two.astype(FLOAT), axis=0),
    )
    return (result, d_inputs, d_condition, local)


def general_body(
    tokens,
    cotangent,
    condition,
    lengths,
    adaptive_weight,
    joint_weight,
    output_weight,
    up_weight,
    down_weight,
    adaptive_bias,
    query_bias,
    value_bias,
    output_bias,
    up_bias,
    down_bias,
):
    micro = tokens.shape[1]
    blocks = lax.axis_size("blk")
    first_block = jnp.where(lax.axis_index("blk") == 0, 1.0, 0.0).astype(FLOAT)
    results = []
    token_grads = []
    condition_grads = []
    sums = None
    for step in range(micro):
        columns = (
            lax.all_gather(adaptive_weight, "blk", axis=1, tiled=True),
            lax.all_gather(joint_weight, "blk", axis=1, tiled=True),
            lax.all_gather(output_weight, "blk", axis=1, tiled=True),
            lax.all_gather(up_weight, "blk", axis=1, tiled=True),
            lax.all_gather(down_weight, "blk", axis=1, tiled=True),
            lax.all_gather(adaptive_bias, "blk", axis=0, tiled=True),
            lax.all_gather(query_bias, "blk", axis=0, tiled=True),
            lax.all_gather(value_bias, "blk", axis=0, tiled=True),
            lax.all_gather(output_bias, "blk", axis=0, tiled=True),
            lax.all_gather(up_bias, "blk", axis=0, tiled=True),
            lax.all_gather(down_bias, "blk", axis=0, tiled=True),
        )
        whole = (
            lax.all_gather(columns[0], "dp", axis=0, tiled=True),
            lax.all_gather(columns[1], "dp", axis=0, tiled=True),
            lax.all_gather(columns[2], "dp", axis=0, tiled=True),
            lax.all_gather(columns[3], "dp", axis=0, tiled=True),
            lax.all_gather(columns[4], "dp", axis=0, tiled=True),
        )
        full = tuple(whole) + tuple(columns[5:])
        result, d_inputs, d_condition, local = run_pack(
            full,
            tokens[0, step],
            cotangent[0, step],
            condition[0, step],
            lengths[0, step],
            blocks,
            first_block,
        )
        results.append(result)
        token_grads.append(d_inputs)
        condition_grads.append(d_condition)
        shares = (
            lax.psum_scatter(
                lax.psum_scatter(
                    local[0].astype(jnp.bfloat16), "dp", scatter_dimension=0, tiled=True
                ),
                "blk",
                scatter_dimension=1,
                tiled=True,
            ).astype(jnp.float32),
            lax.psum_scatter(
                lax.psum_scatter(
                    local[1].astype(jnp.bfloat16), "dp", scatter_dimension=0, tiled=True
                ),
                "blk",
                scatter_dimension=1,
                tiled=True,
            ).astype(jnp.float32),
            lax.psum_scatter(
                lax.psum_scatter(
                    local[2].astype(jnp.bfloat16), "dp", scatter_dimension=0, tiled=True
                ),
                "blk",
                scatter_dimension=1,
                tiled=True,
            ).astype(jnp.float32),
            lax.psum_scatter(
                lax.psum_scatter(
                    local[3].astype(jnp.bfloat16), "dp", scatter_dimension=0, tiled=True
                ),
                "blk",
                scatter_dimension=1,
                tiled=True,
            ).astype(jnp.float32),
            lax.psum_scatter(
                lax.psum_scatter(
                    local[4].astype(jnp.bfloat16), "dp", scatter_dimension=0, tiled=True
                ),
                "blk",
                scatter_dimension=1,
                tiled=True,
            ).astype(jnp.float32),
            lax.psum_scatter(
                lax.psum(local[5].astype(jnp.bfloat16), "dp"),
                "blk",
                scatter_dimension=0,
                tiled=True,
            ).astype(jnp.float32),
            lax.psum_scatter(
                lax.psum(local[6].astype(jnp.bfloat16), "dp"),
                "blk",
                scatter_dimension=0,
                tiled=True,
            ).astype(jnp.float32),
            lax.psum_scatter(
                lax.psum(local[7].astype(jnp.bfloat16), "dp"),
                "blk",
                scatter_dimension=0,
                tiled=True,
            ).astype(jnp.float32),
            lax.psum_scatter(
                lax.psum(local[8].astype(jnp.bfloat16), "dp"),
                "blk",
                scatter_dimension=0,
                tiled=True,
            ).astype(jnp.float32),
            lax.psum_scatter(
                lax.psum(local[9].astype(jnp.bfloat16), "dp"),
                "blk",
                scatter_dimension=0,
                tiled=True,
            ).astype(jnp.float32),
            lax.psum_scatter(
                lax.psum(local[10].astype(jnp.bfloat16), "dp"),
                "blk",
                scatter_dimension=0,
                tiled=True,
            ).astype(jnp.float32),
        )
        sums = (
            shares
            if sums is None
            else tuple((first + second for first, second in zip(sums, shares)))
        )
    block_output = jnp.stack(results, axis=0)[None]
    tokens_grad = jnp.stack(token_grads, axis=0)[None]
    condition_grad = jnp.stack(condition_grads, axis=0)[None]
    return (
        block_output,
        tokens_grad,
        condition_grad,
        sums[0],
        sums[1],
        sums[2],
        sums[3],
        sums[4],
        sums[5],
        sums[6],
        sums[7],
        sums[8],
        sums[9],
        sums[10],
    )


HEAD = 72
WINDOW = 256
EXPONENT = HEAD**-0.5 * 1.4426950408889634


def head_window(head, width):
    start = jnp.minimum(lax.div(head * HEAD, 128) * 128, width - WINDOW)
    return pl.ds(pl.multiple_of(start, 128), WINDOW), head * HEAD - start


def head_lanes(offset, rows):
    lane = lax.broadcasted_iota(jnp.int32, (rows, WINDOW), 1)
    return (lane >= offset) & (lane < offset + HEAD)


def for_images(info, unit, image):
    @pl.when(info[8 + unit] == 1)
    def _():
        image(info[unit], 512, 256)

    @pl.when(info[8 + unit] == 0)
    def _():
        def step(index, carry):
            image(info[unit + index], 128, 128)
            return carry

        lax.fori_loop(0, 4, step, 0)


def image_rows(start, strip, half, index, block):
    place = index * block
    place = start + (place if place < strip else half + place - strip)
    return pl.ds(pl.multiple_of(place, 128), block)


def both_strips(ref, start, strip, half, window):
    return jnp.concatenate(
        [ref[pl.ds(start, strip), window], ref[pl.ds(half + start, strip), window]], axis=0
    )


def attend_forward_kernel(info, q_ref, k_ref, v_ref, o_ref, total_ref, *, group):
    half, width = q_ref.shape[0] // 2, q_ref.shape[1]

    def image(start, strip, block):
        start = pl.multiple_of(start, 128)
        work = []
        for member in range(group):
            head = pl.program_id(1) * group + member
            window, offset = head_window(head, width)
            keys = both_strips(k_ref, start, strip, half, window)
            keys = jnp.where(head_lanes(offset, 2 * strip), keys, jnp.zeros_like(keys))
            values = both_strips(v_ref, start, strip, half, window).T
            for index in range(2 * strip // block):
                rows = image_rows(start, strip, half, index, block)
                work.append((head, window, offset, keys, values, rows))

        def scores_of(item):
            return right_outer(item[3], q_ref[item[5], item[1]])

        coming = scores_of(work[0])
        for index, item in enumerate(work):
            head, window, offset, keys, values, rows = item
            scores = coming
            if index + 1 < len(work):
                coming = scores_of(work[index + 1])
            top = jnp.max(scores, axis=0, keepdims=True)
            expo = jnp.exp2((scores - top) * EXPONENT)
            mass = jnp.sum(expo, axis=0, keepdims=True)
            out = (matmul(values, expo.astype(HALF)) * (1.0 / mass)).T.astype(HALF)
            o_ref[rows, window] = jnp.where(head_lanes(offset, block), out, o_ref[rows, window])
            total_ref[head, :, rows] = top * EXPONENT + jnp.log2(mass)

    for_images(info, pl.program_id(0), image)


def attend_backward_kernel(
    info, q_ref, k_ref, v_ref, do_ref, total_ref, dq_ref, dk_ref, dv_ref, *, group
):
    half, width = q_ref.shape[0] // 2, q_ref.shape[1]
    scale = HEAD**-0.5

    def image(start, strip, block):
        start = pl.multiple_of(start, 128)
        work = []
        sums = {}
        for member in range(group):
            head = pl.program_id(1) * group + member
            window, offset = head_window(head, width)
            keys = both_strips(k_ref, start, strip, half, window)
            values = both_strips(v_ref, start, strip, half, window)
            inside = head_lanes(offset, 2 * strip)
            head_keys = jnp.where(inside, keys, jnp.zeros_like(keys))
            head_values = jnp.where(inside, values, jnp.zeros_like(values))
            turned = keys.T
            for index in range(2 * strip // block):
                rows = image_rows(start, strip, half, index, block)
                work.append((head, window, offset, head_keys, head_values, turned, rows))

        def begin(item):
            head, window, offset, keys, values, turned, rows = item
            return (
                right_outer(keys, q_ref[rows, window]),
                right_outer(values, do_ref[rows, window]),
            )

        def middle(item, scores, d_weights):
            weights = jnp.exp2(scores * EXPONENT - total_ref[item[0], :, item[6]])
            product = weights * d_weights
            delta = jnp.sum(product, axis=0, keepdims=True)
            return weights.astype(HALF), (product - weights * delta).astype(HALF)

        def finish(item, weights, d_scores):
            head, window, offset, keys, values, turned, rows = item
            d_keys = matmul(d_scores, q_ref[rows, window])
            d_values = matmul(weights, do_ref[rows, window])
            d_query = (matmul(turned, d_scores).T * scale).astype(HALF)
            dq_ref[rows, window] = jnp.where(
                head_lanes(offset, block), d_query, dq_ref[rows, window]
            )
            if id(keys) in sums:
                d_keys, d_values = sums[id(keys)][0] + d_keys, sums[id(keys)][1] + d_values
            sums[id(keys)] = (d_keys, d_values)

        coming = begin(work[0])
        late = None
        for index, item in enumerate(work):
            now = coming
            if index + 1 < len(work):
                coming = begin(work[index + 1])
            if late is not None:
                finish(*late)
            late = (item,) + middle(item, *now)
        finish(*late)
        for item in work[:: 2 * strip // block]:
            head, window, offset, keys = item[:4]
            d_keys, d_values = sums[id(keys)]
            lanes = head_lanes(offset, strip)
            for ref, value in (
                (dk_ref, (d_keys * scale).astype(HALF)),
                (dv_ref, d_values.astype(HALF)),
            ):
                for first, part in ((start, value[:strip]), (half + start, value[strip:])):
                    rows = pl.ds(pl.multiple_of(first, 128), strip)
                    ref[rows, window] = jnp.where(lanes, part, ref[rows, window])

    for_images(info, pl.program_id(0), image)


def attention_call(kernel, name, info, arrays, outputs, group, flops):
    def whole(array):
        return pl.BlockSpec(
            array.shape,
            lambda unit, head, info: (0,) * len(array.shape),
            pipeline_mode=pl.Buffered(1),
        )

    return pl.pallas_call(
        functools.partial(kernel, group=group),
        grid_spec=pltpu.PrefetchScalarGridSpec(
            num_scalar_prefetch=1,
            grid=(2, HEADS // group),
            in_specs=[whole(array) for array in arrays],
            out_specs=[whole(array) for array in outputs],
        ),
        out_shape=outputs,
        compiler_params=pltpu.CompilerParams(vmem_limit_bytes=60 * 2**20),
        cost_estimate=pl.CostEstimate(
            flops=flops, bytes_accessed=30 * 2**20, transcendentals=HEADS * 2**21
        ),
        name=name,
    )(info, *arrays)


def attend_pack(info, query, keys, values):
    rows, width = query.shape
    outputs = [
        jax.ShapeDtypeStruct((rows, width), HALF),
        jax.ShapeDtypeStruct((HEADS, 1, rows), FLOAT),
    ]
    return attention_call(
        attend_forward_kernel, "attend", info, [query, keys, values], outputs, 4, 70 * 10**9
    )


def attend_pack_backward(info, query, keys, values, grad, total):
    outputs = [jax.ShapeDtypeStruct(query.shape, HALF)] * 3
    arrays = [query, keys, values, grad, total]
    return attention_call(
        attend_backward_kernel, "attend_backward", info, arrays, outputs, 2, 140 * 10**9
    )


BLOCK = 256
PART = 128
STRIP = 32


def resident(array):
    return pl.BlockSpec(
        array.shape, lambda *step: (0,) * len(array.shape), pipeline_mode=pl.Buffered(1)
    )


def by_rows(array):
    size = BLOCK if len(array.shape) == 2 else BLOCK // PART
    zeros = (0,) * (len(array.shape) - 1)
    return pl.BlockSpec((size,) + array.shape[1:], lambda step: (step,) + zeros)


def dense_call(kernel, name, inputs, outputs, scratch=(), flops=0):
    rows = 2048
    size = sum(array.size * array.dtype.itemsize for array, _ in inputs + outputs)
    return pl.pallas_call(
        kernel,
        grid=(rows // BLOCK,),
        in_specs=[spec for _, spec in inputs],
        out_specs=[spec for _, spec in outputs],
        out_shape=[shape for shape, _ in outputs],
        scratch_shapes=list(scratch),
        compiler_params=pltpu.CompilerParams(vmem_limit_bytes=60 * 2**20),
        cost_estimate=pl.CostEstimate(flops=flops, bytes_accessed=size, transcendentals=0),
        name=name,
    )(*[array for array, _ in inputs])


def shape_of(*dims, kind=None):
    return jax.ShapeDtypeStruct(dims, kind or FLOAT)


def strips():
    return [
        (pl.ds(begin, STRIP), begin // PART, begin % PART == 0) for begin in range(0, BLOCK, STRIP)
    ]


def row_norm(values):
    center = values - jnp.mean(values, axis=1, keepdims=True)
    inverse = lax.rsqrt(jnp.mean(center * center, axis=1, keepdims=True) + EPSILON)
    return center * inverse, inverse


def fold(values):
    return jnp.sum(values.reshape(-1, 8, values.shape[1]), axis=0)


class Sums:
    def __init__(self):
        self.held = {}

    def add(self, ref, part, first, values):
        folded = fold(values)
        key = id(ref), part
        if not first:
            folded = self.held[key][1] + folded
        self.held[key] = (ref, folded)

    def store(self):
        for (_, part), (ref, value) in self.held.items():
            ref[part] = jnp.sum(value, axis=0, keepdims=True)


TILE_ROWS = 32
TILE_COLUMNS = 256


def tiles(rows, columns):
    return [
        (row, column)
        for row in range(0, rows, TILE_ROWS)
        for column in range(0, columns, TILE_COLUMNS)
    ]


def up_kernel(x_ref, w_ref, bias_ref, act_ref, slope_ref, *, chunk):
    x = x_ref[...]
    halves, _, columns = w_ref.shape
    work = [(half, begin) for half in range(halves) for begin in range(0, columns, chunk)]

    def product(item):
        return matmul(x, w_ref[item[0], :, pl.ds(item[1], chunk)])

    coming = product(work[0])
    for index, (half, begin) in enumerate(work):
        now = coming
        if index + 1 < len(work):
            coming = product(work[index + 1])
        for row, column in tiles(BLOCK, chunk):
            rows = pl.ds(row, TILE_ROWS)
            place = pl.ds(half * columns + begin + column, TILE_COLUMNS)
            value = now[row : row + TILE_ROWS, column : column + TILE_COLUMNS] + bias_ref[:, place]
            square = value * value
            gate = 0.5 + 0.5 * jnp.tanh(
                value * (GELU_SCALE + (GELU_SCALE * 0.044715) * square)
            )
            active = value * gate
            bend = 2.0 * GELU_SCALE + (6.0 * GELU_SCALE * 0.044715) * square
            act_ref[rows, place] = active.astype(HALF)
            slope_ref[rows, place] = (gate + active * (1.0 - gate) * bend).astype(HALF)


def up_call(hidden, weight, bias, chunk=768):
    rows, width = hidden.shape
    wide = 2 * weight.shape[2]
    out = shape_of(rows, wide, kind=HALF)
    return dense_call(
        functools.partial(up_kernel, chunk=chunk),
        "up",
        [(hidden, by_rows(hidden)), (weight, resident(weight)), (bias, resident(bias))],
        [(out, by_rows(out)), (out, by_rows(out))],
        flops=2 * rows * width * wide,
    )


def down_grad_kernel(cot_ref, gate_ref, slope_ref, w_ref, d_branch_ref, d_pre_ref, sum_ref, wide_ref, *, chunk):
    for rows, part, _ in strips():
        d_branch_ref[rows, :] = (cot_ref[rows, :].astype(FLOAT) * gate_ref[part]).astype(HALF)
    x = d_branch_ref[...]
    sum_ref[0] = jnp.sum(fold(x.astype(FLOAT)), axis=0, keepdims=True)
    wide = w_ref.shape[0]
    work = list(range(0, wide, chunk))

    def product(begin):
        return right_outer(x, w_ref[pl.ds(begin, chunk), :])

    coming = product(work[0])
    for index, begin in enumerate(work):
        now = coming
        if index + 1 < len(work):
            coming = product(work[index + 1])
        for column in range(0, chunk, TILE_COLUMNS):
            place = pl.ds(begin + column, TILE_COLUMNS)
            total = None
            for row in range(0, BLOCK, TILE_ROWS):
                rows = pl.ds(row, TILE_ROWS)
                value = now[row : row + TILE_ROWS, column : column + TILE_COLUMNS]
                value = (value * slope_ref[rows, place].astype(FLOAT)).astype(HALF)
                d_pre_ref[rows, place] = value
                folded = fold(value.astype(FLOAT))
                total = folded if total is None else total + folded
            wide_ref[0, :, place] = jnp.sum(total, axis=0, keepdims=True)


def down_grad_call(cotangent, gate, slope, weight, chunk=768):
    rows, width = cotangent.shape
    wide = weight.shape[0]
    steps = rows // BLOCK
    d_branch, d_pre = shape_of(rows, width, kind=HALF), shape_of(rows, wide, kind=HALF)
    total, wide_total = shape_of(steps, 1, width), shape_of(steps, 1, wide)

    def per_step(shape):
        return pl.BlockSpec((1,) + shape.shape[1:], lambda step: (step, 0, 0))

    return dense_call(
        functools.partial(down_grad_kernel, chunk=chunk),
        "down_grad",
        [
            (cotangent, by_rows(cotangent)),
            (gate, by_rows(gate)),
            (slope, by_rows(slope)),
            (weight, resident(weight)),
        ],
        [
            (d_branch, by_rows(d_branch)),
            (d_pre, by_rows(d_pre)),
            (total, per_step(total)),
            (wide_total, per_step(wide_total)),
        ],
        flops=2 * rows * width * wide,
    )


def project_kernel(x_ref, shift_ref, scale_ref, w_ref, bias_ref, hidden_ref, q_ref, k_ref, v_ref):
    for rows, part, _ in strips():
        normed, _ = row_norm(x_ref[rows, :].astype(FLOAT))
        hidden_ref[rows, :] = (normed * (1.0 + scale_ref[part]) + shift_ref[part]).astype(HALF)
    hidden = hidden_ref[...]
    width = hidden.shape[1]
    for index, ref in enumerate((q_ref, k_ref, v_ref)):
        place = pl.ds(index * width, width)
        ref[...] = (matmul(hidden, w_ref[:, place]) + bias_ref[:, place]).astype(HALF)


def project_call(tokens, shift, scale, weight, bias):
    rows, width = tokens.shape
    out = shape_of(rows, width, kind=HALF)
    return dense_call(
        project_kernel,
        "project",
        [
            (tokens, by_rows(tokens)),
            (shift, by_rows(shift)),
            (scale, by_rows(scale)),
            (weight, resident(weight)),
            (bias, resident(bias)),
        ],
        [(out, by_rows(out))] * 4,
        flops=6 * rows * width * width,
    )


def mix_kernel(
    attended_ref, x_ref, gate_ref, shift_ref, scale_ref, w_ref, bias_ref, branch_ref, hidden_ref
):
    branch_ref[...] = matmul(attended_ref[...], w_ref[...]) + bias_ref[...]
    for rows, part, _ in strips():
        middle = x_ref[rows, :].astype(FLOAT) + gate_ref[part] * branch_ref[rows, :]
        normed, _ = row_norm(middle)
        hidden_ref[rows, :] = (normed * (1.0 + scale_ref[part]) + shift_ref[part]).astype(HALF)


def mix_call(attended, tokens, gate, shift, scale, weight, bias):
    rows, width = tokens.shape
    branch, hidden = shape_of(rows, width), shape_of(rows, width, kind=HALF)
    return dense_call(
        mix_kernel,
        "mix",
        [
            (attended, by_rows(attended)),
            (tokens, by_rows(tokens)),
            (gate, by_rows(gate)),
            (shift, by_rows(shift)),
            (scale, by_rows(scale)),
            (weight, resident(weight)),
            (bias, resident(bias)),
        ],
        [(branch, by_rows(branch)), (hidden, by_rows(hidden))],
        flops=2 * rows * width * width,
    )


def finish_kernel(
    act_ref, x_ref, branch_ref, cot_ref, gate_one_ref, gate_two_ref, w_ref, bias_ref,
    own_ref, other_ref, sum_ref, branch_two,
):
    branch_two[...] = matmul(act_ref[...], w_ref[...]) + bias_ref[...]
    step = pl.program_id(0)
    sums = Sums()
    for rows, part, first in strips():
        middle = x_ref[rows, :].astype(FLOAT) + gate_one_ref[part] * branch_ref[rows, :]
        two = branch_two[rows, :]
        sums.add(sum_ref, part, first, cot_ref[rows, :].astype(FLOAT) * two)
        branch_two[rows, :] = middle + gate_two_ref[part] * two
    sums.store()
    store_strip(step, branch_two, own_ref, other_ref)


def store_strip(step, value_ref, own_ref, other_ref):
    half = pl.num_programs(0) // 2

    @pl.when(step < half)
    def _():
        own_ref[...] = value_ref[...]

    @pl.when(step >= half)
    def _():
        other_ref[...] = value_ref[...].astype(HALF)


def strip_specs(rows, width):
    half = rows // BLOCK // 2
    own, other = shape_of(rows // 2, width), shape_of(rows // 2, width, kind=HALF)
    return [
        (own, pl.BlockSpec((BLOCK, width), lambda step: (jnp.minimum(step, half - 1), 0))),
        (other, pl.BlockSpec((BLOCK, width), lambda step: (jnp.maximum(step - half, 0), 0))),
    ]


def finish_call(active, tokens, branch, cotangent, gate_one, gate_two, weight, bias):
    rows, width = tokens.shape
    sums = shape_of(rows // PART, 1, width)
    return dense_call(
        finish_kernel,
        "finish",
        [
            (active, by_rows(active)),
            (tokens, by_rows(tokens)),
            (branch, by_rows(branch)),
            (cotangent, by_rows(cotangent)),
            (gate_one, by_rows(gate_one)),
            (gate_two, by_rows(gate_two)),
            (weight, resident(weight)),
            (bias, resident(bias)),
        ],
        strip_specs(rows, width) + [(sums, by_rows(sums))],
        scratch=[pltpu.VMEM((BLOCK, width), FLOAT)],
        flops=2 * rows * active.shape[1] * width,
    )


def norm_pull(normed, inverse, grad):
    mean_grad = jnp.mean(grad, axis=1, keepdims=True)
    mean_cross = jnp.mean(grad * normed, axis=1, keepdims=True)
    return inverse * (grad - mean_grad - normed * mean_cross)


def mix_grad_kernel(
    d_pre_ref, x_ref, branch_ref, cot_ref, gate_ref, scale_ref, up_ref, out_ref,
    d_middle_ref, d_branch_ref, d_attended_ref, shift_sum, scale_sum, gate_sum, bias_sum, hidden,
):
    columns = up_ref.shape[2]
    hidden[...] = right_outer(d_pre_ref[:, :columns], up_ref[0]) + right_outer(
        d_pre_ref[:, columns:], up_ref[1]
    )
    sums = Sums()
    for rows, part, first in strips():
        branch, grad = branch_ref[rows, :], hidden[rows, :]
        gate = gate_ref[part]
        normed, inverse = row_norm(x_ref[rows, :].astype(FLOAT) + gate * branch)
        sums.add(shift_sum, part, first, grad)
        sums.add(scale_sum, part, first, grad * normed)
        d_middle = cot_ref[rows, :].astype(FLOAT) + norm_pull(
            normed, inverse, grad * (1.0 + scale_ref[part])
        )
        d_middle_ref[rows, :] = d_middle
        sums.add(gate_sum, part, first, d_middle * branch)
        d_branch = (d_middle * gate).astype(HALF)
        d_branch_ref[rows, :] = d_branch
        sums.add(bias_sum, part, first, d_branch.astype(FLOAT))
    sums.store()
    d_attended_ref[...] = right_outer(d_branch_ref[...], out_ref[...]).astype(HALF)


def mix_grad_call(d_pre, tokens, branch, cotangent, gate, scale, up, out):
    rows, width = tokens.shape
    half, sums = shape_of(rows, width, kind=HALF), shape_of(rows // PART, 1, width)
    d_middle = shape_of(rows, width)
    return dense_call(
        mix_grad_kernel,
        "mix_grad",
        [
            (d_pre, by_rows(d_pre)),
            (tokens, by_rows(tokens)),
            (branch, by_rows(branch)),
            (cotangent, by_rows(cotangent)),
            (gate, by_rows(gate)),
            (scale, by_rows(scale)),
            (up, resident(up)),
            (out, resident(out)),
        ],
        [(d_middle, by_rows(d_middle)), (half, by_rows(half)), (half, by_rows(half))]
        + [(sums, by_rows(sums))] * 4,
        scratch=[pltpu.VMEM((BLOCK, width), FLOAT)],
        flops=2 * rows * width * (d_pre.shape[1] + width),
    )


def project_grad_kernel(
    dq_ref, dk_ref, dv_ref, x_ref, d_middle_ref, scale_ref, w_ref,
    own_ref, other_ref, shift_sum, scale_sum, query_sum, value_sum, hidden,
):
    grads = jnp.concatenate([dq_ref[...], dk_ref[...], dv_ref[...]], axis=1)
    hidden[...] = right_outer(grads, w_ref[...])
    sums = Sums()
    for rows, part, first in strips():
        grad = hidden[rows, :]
        normed, inverse = row_norm(x_ref[rows, :].astype(FLOAT))
        sums.add(shift_sum, part, first, grad)
        sums.add(scale_sum, part, first, grad * normed)
        sums.add(query_sum, part, first, dq_ref[rows, :].astype(FLOAT))
        sums.add(value_sum, part, first, dv_ref[rows, :].astype(FLOAT))
        hidden[rows, :] = d_middle_ref[rows, :] + norm_pull(
            normed, inverse, grad * (1.0 + scale_ref[part])
        )
    sums.store()
    store_strip(pl.program_id(0), hidden, own_ref, other_ref)


def project_grad_call(d_query, d_keys, d_values, tokens, d_middle, scale, weight):
    rows, width = tokens.shape
    sums = shape_of(rows // PART, 1, width)
    return dense_call(
        project_grad_kernel,
        "project_grad",
        [
            (d_query, by_rows(d_query)),
            (d_keys, by_rows(d_keys)),
            (d_values, by_rows(d_values)),
            (tokens, by_rows(tokens)),
            (d_middle, by_rows(d_middle)),
            (scale, by_rows(scale)),
            (weight, resident(weight)),
        ],
        strip_specs(rows, width) + [(sums, by_rows(sums))] * 4,
        scratch=[pltpu.VMEM((BLOCK, width), FLOAT)],
        flops=6 * rows * width * width,
    )


MESH = pl.DeviceIdType.MESH


class Place:
    def __init__(self):
        me = lax.axis_index("dp")
        self.me, self.y = me, lax.axis_index("blk")
        self.z, self.x, self.core = me // 4, (me // 2) % 2, me % 2

    def at(self, z_step, x_step, core_step):
        z = (self.z + 4 - z_step) % 4
        return z * 4 + ((self.x + x_step) % 2) * 2 + (self.core + core_step) % 2

    def half(self, y_step):
        return (self.y + y_step) % 2

    def partner(self, kind):
        if kind == "y":
            return {"blk": 1 - self.y}
        if kind == "z":
            return {"dp": (self.me + 4) % 16}
        if kind == "back":
            return {"dp": (self.me + 12) % 16}
        if kind == "x":
            return {"dp": self.at(0, 1, 0)}
        return {"dp": self.at(0, 0, 1)}

    def greet(self):
        barrier = pltpu.get_barrier_semaphore()
        for kind in ("y", "z", "back", "x", "core"):
            pl.semaphore_signal(
                barrier, inc=1, device_id=self.partner(kind), device_id_type=MESH
            )
        pl.semaphore_wait(barrier, 5)


class Copies:
    def __init__(self, place, send_sems, recv_sems):
        self.place, self.send_sems, self.recv_sems = place, send_sems, recv_sems
        self.made = {}

    def send(self, key, source, target):
        index = len(self.made)
        copy = pltpu.make_async_remote_copy(
            src_ref=source,
            dst_ref=target,
            send_sem=self.send_sems.at[index],
            recv_sem=self.recv_sems.at[index],
            device_id=self.place.partner(key[0]),
            device_id_type=MESH,
        )
        self.made[key] = copy
        copy.start()

    def receive(self, key):
        self.made[key].wait_recv()

    def finish(self):
        for copy in self.made.values():
            copy.wait_send()


def head_kernel(
    shard_ref,
    condition_ref,
    adaptive_ref,
    bias_ref,
    tokens_ref,
    whole_ref,
    modulation_ref,
    act_ref,
    other_ref,
    conditions,
    parts,
    from_core,
    from_x,
    from_z,
    share,
    from_y,
    local_sem,
    send_sems,
    recv_sems,
):
    place = Place()
    copies = Copies(place, send_sems, recv_sems)
    place.greet()

    own = pltpu.make_async_copy(
        shard_ref, whole_ref.at[place.half(0), place.me], local_sem.at[0]
    )
    own.start()
    conditions[place.me] = condition_ref[...]

    def condition(kind, z_step, x_step):
        slot = conditions.at[place.at(z_step, x_step, 0)]
        copies.send((kind, "condition", z_step, x_step), slot, slot)

    def weight(kind, y_step, z_step, x_step):
        slot = whole_ref.at[place.half(y_step), place.at(z_step, x_step, 0)]
        mine = y_step == 0 and z_step == 0 and x_step == 0
        copies.send((kind, "weight", y_step, z_step, x_step), shard_ref if mine else slot, slot)

    def forward_condition(z_step):
        for x_step in range(2):
            copies.receive(("z", "condition", z_step - 1, x_step))
            if z_step < 3:
                condition("z", z_step, x_step)
            condition("core", z_step, x_step)

    def forward(z_step, y_step):
        copies.receive(("z", "weight", y_step, z_step - 1, 0))
        if z_step < 3:
            weight("z", y_step, z_step, 0)
        weight("x", y_step, z_step, 0)
        weight("core", y_step, z_step, 0)

    condition("x", 0, 0)
    condition("z", 0, 0)
    condition("core", 0, 0)
    weight("y", 0, 0, 0)
    weight("z", 0, 0, 0)
    weight("x", 0, 0, 0)
    weight("core", 0, 0, 0)
    copies.send(("y", "tokens"), tokens_ref.at[place.half(1)], other_ref)
    copies.receive(("x", "condition", 0, 0))
    condition("z", 0, 1)
    condition("core", 0, 1)
    forward_condition(1)
    copies.receive(("y", "weight", 0, 0, 0))
    weight("z", 1, 0, 0)
    weight("x", 1, 0, 0)
    weight("core", 1, 0, 0)
    forward_condition(2)
    forward(1, 0)
    forward_condition(3)
    forward(1, 1)
    for z_step in range(4):
        for x_step in range(2):
            copies.receive(("core", "condition", z_step, x_step))

    adaptive = adaptive_ref[...]
    count, rows = conditions.shape[0], conditions.shape[2]
    for index in range(count):
        values = conditions[index, place.me].astype(FLOAT)
        act_ref[index] = (values / (1.0 + jnp.exp(-values))).astype(HALF)

    def products(z_step, core_step):
        for x_step in range(2):
            target = place.at((4 - z_step) % 4, x_step, core_step)
            product = matmul(act_ref[target], adaptive)
            parts[core_step, z_step, x_step] = product.astype(HALF)

    def add(first, second):
        return first.astype(FLOAT) + second.astype(FLOAT)

    for z_step in (3, 2, 1, 0):
        products(z_step, 1)
        copies.send(("core", "part", z_step), parts.at[1, z_step], from_core.at[z_step])
    forward(2, 0)
    for z_step in (3, 2, 1, 0):
        products(z_step, 0)
    forward(2, 1)
    for z_step in (3, 2, 1, 0):
        copies.receive(("core", "part", z_step))
        total = add(parts[0, z_step], from_core[z_step])
        if z_step < 3:
            copies.receive(("z", "part", z_step + 1))
            total = total + from_z[z_step].astype(FLOAT)
        parts[0, z_step] = total.astype(HALF)
        if z_step > 0:
            copies.send(("z", "part", z_step), parts.at[0, z_step], from_z.at[z_step - 1])
        if z_step == 2:
            forward(3, 0)
        if z_step == 1:
            forward(3, 1)
    copies.send(("x", "part"), parts.at[0, 0, 1], from_x)

    def last(z_step):
        for y_step in range(2):
            copies.receive(("x", "weight", y_step, z_step, 0))
            weight("core", y_step, z_step, 1)

    last(0)
    last(1)
    images = rows // 2
    copies.receive(("x", "part"))
    total = add(parts[0, 0, 0], from_x[...]) + bias_ref[...]
    share[0] = total[:images]
    share[1] = total[images:]
    copies.send(("y", "part"), share.at[place.half(1)], from_y)
    modulation_ref[place.half(0)] = share[place.half(0)]
    last(2)
    last(3)
    copies.receive(("y", "part"))
    modulation_ref[place.half(1)] = from_y[...]
    for z_step in range(4):
        for x_step in range(2):
            for y_step in range(2):
                copies.receive(("core", "weight", y_step, z_step, x_step))
    copies.receive(("y", "tokens"))
    own.wait()
    copies.finish()


def head(shard, condition, adaptive_weight, adaptive_bias, tokens):
    micro, images, width = condition.shape
    features = adaptive_weight.shape[0]
    rows = micro * images
    condition = condition.reshape(rows, width // features, features).transpose(1, 0, 2)
    columns = adaptive_weight.shape[1]
    count = 16
    vmem = pl.BlockSpec(memory_space=pltpu.VMEM)
    anywhere = pl.BlockSpec(memory_space=pl.ANY)
    return pl.pallas_call(
        head_kernel,
        out_shape=[
            jax.ShapeDtypeStruct((2, count) + shard.shape, HALF),
            jax.ShapeDtypeStruct((2, images, columns), FLOAT),
            jax.ShapeDtypeStruct((count, rows, features), HALF),
            jax.ShapeDtypeStruct(tokens.shape[1:], HALF),
        ],
        in_specs=[anywhere, vmem, vmem, vmem, anywhere],
        out_specs=[anywhere, vmem, vmem, anywhere],
        scratch_shapes=[
            pltpu.VMEM((count,) + condition.shape, HALF),
            pltpu.VMEM((2, 4, 2, rows, columns), HALF),
            pltpu.VMEM((4, 2, rows, columns), HALF),
            pltpu.VMEM((rows, columns), HALF),
            pltpu.VMEM((3, 2, rows, columns), HALF),
            pltpu.VMEM((2, images, columns), FLOAT),
            pltpu.VMEM((images, columns), FLOAT),
            pltpu.SemaphoreType.DMA((1,)),
            pltpu.SemaphoreType.DMA((64,)),
            pltpu.SemaphoreType.DMA((64,)),
        ],
        compiler_params=pltpu.CompilerParams(
            collective_id=1, has_side_effects=True, vmem_limit_bytes=48 * 2**20
        ),
        cost_estimate=pl.CostEstimate(flops=0, bytes_accessed=200 * 2**20, transcendentals=0),
        name="head",
    )(shard, condition, adaptive_weight, adaptive_bias.astype(FLOAT)[None], tokens)


def tail_kernel(
    grad_ref,
    half_ref,
    vector_ref,
    strip_ref,
    share_ref,
    all_ref,
    total_ref,
    other_ref,
    own,
    from_core,
    from_x,
    from_z,
    from_y,
    pair,
    pair_from_y,
    vector,
    vector_from,
    vector_z,
    local_sems,
    send_sems,
    recv_sems,
):
    place = Place()
    copies = Copies(place, send_sems, recv_sems)
    place.greet()

    def grad(y_step, z_step, x_step, core_step):
        return grad_ref.at[place.half(y_step), place.at((4 - z_step) % 4, x_step, core_step)]

    def modulation(kind, z_step, x_step):
        slot = all_ref.at[place.at(z_step, x_step, 0)]
        copies.send((kind, "modulation", z_step, x_step), slot, slot)

    copies.send(("y", "half"), half_ref.at[place.half(1)], pair_from_y)
    copies.send(("core", "vector"), vector_ref, vector_from.at[0])
    order = [(z_step, y_step) for z_step in (3, 2, 1, 0) for y_step in (1, 0)]
    loads = {}
    for x_step in (1, 0):
        for z_step, y_step in order:
            copies.send(
                ("core", x_step, z_step, y_step),
                grad(y_step, z_step, x_step, 1),
                from_core.at[x_step, z_step, y_step],
            )
            load = pltpu.make_async_copy(
                grad(y_step, z_step, x_step, 0),
                own.at[x_step, z_step, y_step],
                local_sems.at[len(loads)],
            )
            load.start()
            loads[x_step, z_step, y_step] = load

    copies.receive(("core", "vector"))
    vector[0] = vector_ref[...] + vector_from[0]
    copies.send(("x", "vector"), vector.at[0], vector_from.at[1])
    pair[place.half(0)] = half_ref[place.half(0)]
    copies.receive(("y", "half"))
    pair[place.half(1)] = pair_from_y[...]
    all_ref[place.me] = pair[...].reshape(all_ref.shape[1:]).astype(HALF)
    modulation("x", 0, 0)
    modulation("z", 0, 0)
    modulation("core", 0, 0)

    def summed(x_step, z_step, y_step):
        loads[x_step, z_step, y_step].wait()
        copies.receive(("core", x_step, z_step, y_step))
        first = own[x_step, z_step, y_step].astype(FLOAT)
        return first + from_core[x_step, z_step, y_step].astype(FLOAT)

    def send_x(z_step):
        for y_step in (1, 0):
            own[1, z_step, y_step] = summed(1, z_step, y_step).astype(HALF)
            copies.send(
                ("x", z_step, y_step), own.at[1, z_step, y_step], from_x.at[z_step, y_step]
            )

    def forward_modulation(z_step):
        for x_step in range(2):
            copies.receive(("z", "modulation", z_step - 1, x_step))
            if z_step < 3:
                modulation("z", z_step, x_step)
            modulation("core", z_step, x_step)

    def vector_ring(z_step):
        slot = vector_z.at[(place.z + 4 - z_step) % 4]
        copies.send(("z", "vector", z_step), slot, slot)

    send_x(3)
    copies.receive(("x", "vector"))
    vector[1] = vector[0] + vector_from[1]
    copies.send(("y", "vector"), vector.at[1], vector_from.at[2])
    copies.send(("y", "strip"), strip_ref, other_ref)
    copies.receive(("x", "modulation", 0, 0))
    modulation("z", 0, 1)
    modulation("core", 0, 1)
    send_x(2)
    copies.receive(("y", "vector"))
    vector_z[place.z] = vector[1] + vector_from[2]
    vector_ring(0)
    forward_modulation(1)
    send_x(1)
    copies.receive(("z", "vector", 0))
    vector_ring(1)
    forward_modulation(2)
    send_x(0)
    copies.receive(("z", "vector", 1))
    vector_ring(2)
    forward_modulation(3)
    for z_step, y_step in order:
        total = summed(0, z_step, y_step)
        copies.receive(("x", z_step, y_step))
        total = total + from_x[z_step, y_step].astype(FLOAT)
        if z_step < 3:
            copies.receive(("z", z_step + 1, y_step))
            total = total + from_z[z_step, y_step].astype(FLOAT)
        if z_step == 0 and y_step == 0:
            copies.receive(("y",))
            share_ref[...] = total + from_y[...].astype(FLOAT)
            continue
        own[0, z_step, y_step] = total.astype(HALF)
        if z_step > 0:
            copies.send(
                ("z", z_step, y_step), own.at[0, z_step, y_step], from_z.at[z_step - 1, y_step]
            )
        else:
            copies.send(("y",), own.at[0, 0, 1], from_y)
    copies.receive(("z", "vector", 2))
    total_ref[...] = (vector_z[0] + vector_z[1]) + (vector_z[2] + vector_z[3])
    for z_step in range(4):
        for x_step in range(2):
            copies.receive(("core", "modulation", z_step, x_step))
    copies.receive(("y", "strip"))
    copies.finish()


def tail(grad, half, vector, strip):
    slot = grad.shape[2:]
    count = grad.shape[1]
    images, columns = half.shape[1:]
    vmem = pl.BlockSpec(memory_space=pltpu.VMEM)
    anywhere = pl.BlockSpec(memory_space=pl.ANY)
    return pl.pallas_call(
        tail_kernel,
        out_shape=[
            jax.ShapeDtypeStruct(slot, FLOAT),
            jax.ShapeDtypeStruct((count, 2 * images, columns), HALF),
            jax.ShapeDtypeStruct(vector.shape, FLOAT),
            jax.ShapeDtypeStruct(strip.shape, HALF),
        ],
        in_specs=[anywhere, vmem, vmem, anywhere],
        out_specs=[vmem, vmem, vmem, anywhere],
        scratch_shapes=[
            pltpu.VMEM((2, 4, 2) + slot, HALF),
            pltpu.VMEM((2, 4, 2) + slot, HALF),
            pltpu.VMEM((4, 2) + slot, HALF),
            pltpu.VMEM((3, 2) + slot, HALF),
            pltpu.VMEM(slot, HALF),
            pltpu.VMEM(half.shape, FLOAT),
            pltpu.VMEM(half.shape[1:], FLOAT),
            pltpu.VMEM((2,) + vector.shape, FLOAT),
            pltpu.VMEM((3,) + vector.shape, FLOAT),
            pltpu.VMEM((4,) + vector.shape, FLOAT),
            pltpu.SemaphoreType.DMA((16,)),
            pltpu.SemaphoreType.DMA((64,)),
            pltpu.SemaphoreType.DMA((64,)),
        ],
        compiler_params=pltpu.CompilerParams(
            collective_id=2, has_side_effects=True, vmem_limit_bytes=48 * 2**20
        ),
        cost_estimate=pl.CostEstimate(flops=0, bytes_accessed=200 * 2**20, transcendentals=0),
        name="tail",
    )(grad, half, vector, strip)


def swap_blk(value):
    return lax.ppermute(value, "blk", [(0, 1), (1, 0)])


def gather_weight(shard):
    halves = lax.all_gather(shard, ("blk", "dp"), axis=0, tiled=True)
    rows = halves.shape[0] // 2
    return jnp.concatenate([halves[:rows], halves[rows:]], axis=1)


def share_columns(total, me_blk):
    half = total.shape[1] // 2
    keep = lax.dynamic_slice_in_dim(total, me_blk * half, half, 1)
    send = lax.dynamic_slice_in_dim(total, (1 - me_blk) * half, half, 1)
    return keep.astype(FLOAT) + swap_blk(send).astype(FLOAT)


def order_blk(first, mine, other, axis):
    return jnp.concatenate(
        [jnp.where(first, mine, other), jnp.where(first, other, mine)], axis=axis
    )


def pair_body(
    tokens,
    cotangent,
    condition,
    lengths,
    adaptive_weight,
    joint_weight,
    output_weight,
    up_weight,
    down_weight,
    adaptive_bias,
    query_bias,
    value_bias,
    output_bias,
    up_bias,
    down_bias,
):
    me_dp, me_blk = lax.axis_index("dp"), lax.axis_index("blk")
    first = me_blk == 0
    strip_rows, width = tokens.shape[2:]
    rows = 2 * strip_rows
    parts = strip_rows // 128
    images = lengths.shape[2]

    def mine_of(pair):
        return lax.dynamic_index_in_dim(pair, me_blk, 0, keepdims=False)

    def other_of(pair):
        return lax.dynamic_index_in_dim(pair, 1 - me_blk, 0, keepdims=False)

    cut = joint_weight.shape[1]
    halves, modulation, act_part, tokens_other = head(
        jnp.concatenate([joint_weight, output_weight], axis=1),
        condition[0],
        adaptive_weight,
        adaptive_bias,
        tokens[0],
    )
    modulation = jnp.concatenate([modulation[0], modulation[1]], axis=1)

    bias_mine = jnp.concatenate([query_bias, value_bias, output_bias, down_bias, up_bias])
    bias_other = swap_blk(bias_mine)
    small = width // 2

    def bias_of(begin, size):
        return order_blk(
            first, bias_mine[begin : begin + size], bias_other[begin : begin + size], 0
        ).astype(FLOAT)

    query_vector, value_vector = bias_of(0, small), bias_of(small, small)
    output_vector, down_vector = bias_of(2 * small, small), bias_of(3 * small, small)
    up_vector = bias_of(4 * small, up_bias.shape[0])

    halves, up_weight, down_weight = lax.optimization_barrier((halves, up_weight, down_weight))
    halves = halves.reshape(2, width, -1)
    joint = jnp.concatenate([halves[0, :, :cut], halves[1, :, :cut]], axis=1)
    output_matrix = jnp.concatenate([halves[0, :, cut:], halves[1, :, cut:]], axis=1)
    up_halves = lax.all_gather(up_weight, ("blk", "dp"), axis=0, tiled=True)
    up_halves = up_halves.reshape(2, width, -1)
    cotangent_other = swap_blk(other_of(cotangent[0]))

    strip = mine_of(lengths[0]) // 2
    ends = jnp.cumsum(strip)
    starts = ends - strip
    begin = jnp.arange(parts, dtype=jnp.int32)[:, None] * 128
    inside = (begin >= starts[None, :]) & (begin < ends[None, :])
    member = jnp.tile(inside.astype(FLOAT), (2, 1))
    long = strip == 512
    used = strip > 0
    rank = jnp.where(
        long,
        jnp.cumsum(long) - 1,
        jnp.where(used, jnp.sum(long) + jnp.cumsum(used & ~long) - 1, images + 8),
    )
    info = jnp.sum(
        jnp.where(rank[:, None] == jnp.arange(8)[None, :], starts[:, None], 0), axis=0
    )
    kinds = jnp.where(jnp.arange(8) < jnp.sum(long), 1, 0)
    info = jnp.concatenate([info, kinds]).astype(jnp.int32)

    per_part = jnp.dot(member, modulation, precision=HIGHEST, preferred_element_type=FLOAT)
    per_part = per_part.reshape(2 * parts, 1, 6, width)
    shift_one, scale_one, gate_one, shift_two, scale_two, gate_two = (
        per_part[:, :, index] for index in range(6)
    )

    inputs = jnp.concatenate([mine_of(tokens[0]), tokens_other], axis=0)
    joint_vector = jnp.concatenate([query_vector, jnp.zeros_like(query_vector), value_vector])
    hidden_one, query, keys, values = project_call(
        inputs, shift_one, scale_one, joint, joint_vector[None]
    )
    query, down_weight = lax.optimization_barrier((query, down_weight))
    down_matrix = gather_weight(down_weight)
    attended, total = attend_pack(info, query, keys, values)
    branch_one, hidden_two = mix_call(
        attended, inputs, gate_one, shift_two, scale_two, output_matrix, output_vector[None]
    )
    activated, slope = up_call(hidden_two, up_halves, up_vector[None])

    upstream = jnp.concatenate([mine_of(cotangent[0]), cotangent_other], axis=0)
    d_branch_two, d_pre, down_sum, up_sum = down_grad_call(
        upstream, gate_two, slope, down_matrix
    )
    d_pre, down_grad = lax.optimization_barrier(
        (d_pre, left_outer(activated, d_branch_two).astype(HALF))
    )
    down_total = lax.psum_scatter(down_grad, "dp", scatter_dimension=0, tiled=True)
    d_pre, up_grad = lax.optimization_barrier(
        (d_pre, left_outer(hidden_two, d_pre).astype(HALF))
    )
    up_total = lax.psum_scatter(up_grad, "dp", scatter_dimension=0, tiled=True)
    result, result_send, d_gate_two = finish_call(
        activated, inputs, branch_one, upstream, gate_one, gate_two, down_matrix, down_vector[None]
    )
    d_pre, result_send = lax.optimization_barrier((d_pre, result_send))
    result_other = swap_blk(result_send)
    d_middle, d_branch_one, d_attended, d_shift_two, d_scale_two, d_gate_one, output_sum = (
        mix_grad_call(
            d_pre, inputs, branch_one, upstream, gate_one, scale_two, up_halves, output_matrix
        )
    )
    d_attended, output_grad, down_total = lax.optimization_barrier(
        (d_attended, left_outer(attended, d_branch_one).astype(HALF), down_total)
    )
    down_share = share_columns(down_total, me_blk)
    d_query, d_keys, d_values = attend_pack_backward(
        info, query, keys, values, d_attended, total
    )
    d_query, up_total, result_other = lax.optimization_barrier((d_query, up_total, result_other))
    up_share = share_columns(up_total, me_blk)
    d_projected = jnp.concatenate([d_query, d_keys, d_values], axis=1)
    joint_grad = left_outer(hidden_one, d_projected).astype(HALF)
    d_inputs, d_inputs_send, d_shift_one, d_scale_one, query_sum, value_sum = project_grad_call(
        d_query, d_keys, d_values, inputs, d_middle, scale_one, joint
    )

    def part_rows(value):
        return value.reshape(2 * parts, width)

    d_parts = [d_shift_one, d_scale_one, d_gate_one, d_shift_two, d_scale_two, d_gate_two]
    d_parts = jnp.concatenate([part_rows(value) for value in d_parts], axis=1)
    d_modulation = lax.dot_general(
        member,
        d_parts,
        (((0,), (0,)), ((), ())),
        precision=HIGHEST,
        preferred_element_type=FLOAT,
    )
    vectors = [query_sum, value_sum, output_sum, down_sum, up_sum]
    sums = jnp.concatenate([jnp.sum(value, axis=(0, 1)) for value in vectors])
    narrow = output_weight.shape[1]
    grad_halves = jnp.stack(
        [
            jnp.concatenate([joint_grad[:, :cut], output_grad[:, :narrow]], axis=1),
            jnp.concatenate([joint_grad[:, cut:], output_grad[:, narrow:]], axis=1),
        ]
    )
    shard_rows = adaptive_weight.shape[0]
    share, d_mod_all, sums, d_inputs_other = tail(
        grad_halves.reshape(2, 16, shard_rows, -1),
        d_modulation.reshape(images, 2, -1).transpose(1, 0, 2),
        sums.reshape(-1, 128),
        d_inputs_send,
    )
    joint_share, output_share = share[:, :cut], share[:, cut:]
    sums = sums.reshape(-1)
    d_mod_all = d_mod_all.reshape(-1, d_mod_all.shape[2])
    adaptive_share = left_outer(act_part.reshape(-1, shard_rows), d_mod_all)
    adaptive_vector_share = jnp.sum(d_mod_all.astype(FLOAT), axis=0)
    d_act = right_outer(d_mod_all, adaptive_weight)
    d_act = d_act.reshape(16, 2 * images, shard_rows)
    d_act = lax.all_to_all(d_act, "dp", 0, 0)
    d_act = d_act + swap_blk(d_act)
    d_act = d_act.transpose(1, 0, 2).reshape(2, images, width)
    condition_full = condition[0].astype(FLOAT)
    sigmoid_cond = jax.nn.sigmoid(condition_full)
    d_condition = d_act * sigmoid_cond * (1.0 + condition_full * (1.0 - sigmoid_cond))

    def share_of(begin, size):
        return lax.dynamic_slice_in_dim(sums, begin + me_blk * (size // 2), size // 2, 0)

    def both(mine, other):
        return order_blk(first, mine[None], other.astype(FLOAT)[None], 0)[None]

    return (
        both(result, result_other),
        both(d_inputs, d_inputs_other),
        d_condition[None],
        adaptive_share,
        joint_share,
        output_share,
        up_share,
        down_share,
        adaptive_vector_share,
        share_of(0, width),
        share_of(width, width),
        share_of(2 * width, width),
        share_of(4 * width, 2 * up_bias.shape[0]),
        share_of(3 * width, width),
    )


def solution(mesh):
    in_specs = (
        P("dp", None, "blk", None),
        P("dp", None, "blk", None),
        P("dp", None, None, None),
        P("dp", None, None),
        P("dp", "blk"),
        P("dp", "blk"),
        P("dp", "blk"),
        P("dp", "blk"),
        P("dp", "blk"),
        P("blk"),
        P("blk"),
        P("blk"),
        P("blk"),
        P("blk"),
        P("blk"),
    )
    out_specs = (
        P("dp", None, "blk", None),
        P("dp", None, "blk", None),
        P("dp", None, None, None),
        P("dp", "blk"),
        P("dp", "blk"),
        P("dp", "blk"),
        P("dp", "blk"),
        P("dp", "blk"),
        P("blk"),
        P("blk"),
        P("blk"),
        P("blk"),
        P("blk"),
        P("blk"),
    )
    paired = mesh.shape["dp"] == 16 and mesh.shape["blk"] == 2
    body = pair_body if paired else general_body
    return jax.shard_map(body, mesh=mesh, in_specs=in_specs, out_specs=out_specs, check_vma=False)
```

```python
import functools

import jax
import jax.numpy as jnp
from jax import lax
from jax.experimental import pallas as pl
from jax.experimental.pallas import tpu as pltpu
from jax.sharding import PartitionSpec as P

HEADS = 16


EPSILON = 1e-06
GELU_SCALE = 0.7978845608028654
HIGHEST = lax.Precision.HIGHEST
FLOAT = jnp.float32
HALF = jnp.bfloat16


def matmul(left, right):
    return jnp.dot(left, right, preferred_element_type=FLOAT)


def left_outer(left, right):
    return lax.dot_general(left, right, (((0,), (0,)), ((), ())), preferred_element_type=FLOAT)


def right_outer(left, right):
    return lax.dot_general(left, right, (((1,), (1,)), ((), ())), preferred_element_type=FLOAT)


def normalize(values):
    center = values - jnp.mean(values, axis=-1, keepdims=True)
    inverse = lax.rsqrt(jnp.mean(center * center, axis=-1, keepdims=True) + EPSILON)
    return (center * inverse, inverse)


def norm_backward(normed, inverse, grad):
    mean_grad = jnp.mean(grad, axis=-1, keepdims=True)
    mean_cross = jnp.mean(grad * normed, axis=-1, keepdims=True)
    return inverse * (grad - mean_grad - normed * mean_cross)


def gelu_tanh(values):
    return (
        0.5 * values * (1.0 + jnp.tanh(GELU_SCALE * (values + 0.044715 * values * values * values)))
    )


def gelu_slope(values):
    bend = jnp.tanh(GELU_SCALE * (values + 0.044715 * values * values * values))
    return 0.5 * (1.0 + bend) + 0.5 * values * (1.0 - bend * bend) * GELU_SCALE * (
        1.0 + 3.0 * 0.044715 * values * values
    )


def block_size():
    return 512


def block_scores(query_heads, key_part, query_slots, slot_part, scale):
    scores = jnp.einsum("qhd,khd->hqk", query_heads, key_part, preferred_element_type=FLOAT) * scale
    allowed = query_slots[:, None] == slot_part[None, :]
    return jnp.where(allowed[None], scores, -1e30)


def split_blocks(key_all, value_all, key_slots):
    total, width = key_all.shape
    size = block_size()
    count = total // size
    shape = (count, size, HEADS, width // HEADS)
    return (key_all.reshape(shape), value_all.reshape(shape), key_slots.reshape(count, size))


def attend_forward(query, key_all, value_all, query_slots, key_slots, scale):
    rows, width = query.shape
    query_heads = query.reshape(rows, HEADS, width // HEADS)
    key_blocks, value_blocks, slot_blocks = split_blocks(key_all, value_all, key_slots)

    def statistics(carry, item):
        top, mass = carry
        key_part, slot_part = item
        scores = block_scores(query_heads, key_part, query_slots, slot_part, scale)
        new_top = jnp.maximum(top, jnp.max(scores, axis=-1))
        mass = mass * jnp.exp(top - new_top) + jnp.sum(
            jnp.exp(scores - new_top[..., None]), axis=-1
        )
        return ((new_top, mass), None)

    start = (jnp.full((HEADS, rows), -1e30, FLOAT), jnp.zeros((HEADS, rows), FLOAT))
    (top, mass), unused = lax.scan(statistics, start, (key_blocks, slot_blocks))
    log_total = top + jnp.log(mass)

    def accumulate(running, item):
        key_part, value_part, slot_part = item
        scores = block_scores(query_heads, key_part, query_slots, slot_part, scale)
        weights = jnp.exp(scores - log_total[..., None]).astype(HALF)
        return (
            running + jnp.einsum("hqk,khd->qhd", weights, value_part, preferred_element_type=FLOAT),
            None,
        )

    empty = jnp.zeros((rows, HEADS, width // HEADS), FLOAT)
    attended, unused = lax.scan(accumulate, empty, (key_blocks, value_blocks, slot_blocks))
    return (log_total, attended.reshape(rows, width))


def attention_delta(d_attended, attended):
    rows, width = attended.shape
    grad_heads = d_attended.reshape(rows, HEADS, width // HEADS).astype(FLOAT)
    return jnp.einsum("qhd,qhd->hq", grad_heads, attended.reshape(rows, HEADS, width // HEADS))


def attend_backward(
    query, key_all, value_all, query_slots, key_slots, log_total, delta, d_attended, scale
):
    rows, width = query.shape
    total = key_all.shape[0]
    query_heads = query.reshape(rows, HEADS, width // HEADS)
    grad_heads = d_attended.reshape(rows, HEADS, width // HEADS)
    key_blocks, value_blocks, slot_blocks = split_blocks(key_all, value_all, key_slots)

    def one_block(d_query, item):
        key_part, value_part, slot_part = item
        scores = block_scores(query_heads, key_part, query_slots, slot_part, scale)
        weights = jnp.exp(scores - log_total[..., None])
        d_weights = jnp.einsum("qhd,khd->hqk", grad_heads, value_part, preferred_element_type=FLOAT)
        d_scores = (weights * (d_weights - delta[..., None])).astype(HALF)
        d_query = (
            d_query
            + jnp.einsum("hqk,khd->qhd", d_scores, key_part, preferred_element_type=FLOAT) * scale
        )
        d_value_part = jnp.einsum(
            "hqk,qhd->khd", weights.astype(HALF), grad_heads, preferred_element_type=FLOAT
        )
        d_key_part = (
            jnp.einsum("hqk,qhd->khd", d_scores, query_heads, preferred_element_type=FLOAT) * scale
        )
        return (d_query, (d_key_part, d_value_part))

    empty = jnp.zeros((rows, HEADS, width // HEADS), FLOAT)
    d_query, key_parts = lax.scan(one_block, empty, (key_blocks, value_blocks, slot_blocks))
    d_keys, d_values = key_parts
    return (
        d_query.reshape(rows, width),
        d_keys.reshape(total, width),
        d_values.reshape(total, width),
    )


def run_pack(full, tokens_in, cotangent_in, condition_in, lengths_in, blocks, first_block):
    (
        adaptive_matrix,
        joint_matrix,
        output_matrix,
        up_matrix,
        down_matrix,
        adaptive_vector,
        query_vector,
        value_vector,
        output_vector,
        up_vector,
        down_vector,
    ) = full
    rows, width = tokens_in.shape
    scale = (width // HEADS) ** (-0.5)
    inputs = tokens_in.astype(FLOAT)
    strip = lengths_in // blocks
    ends = jnp.cumsum(strip)
    starts = ends - strip
    place = jnp.arange(rows, dtype=jnp.int32)[:, None]
    inside = (place >= starts[None, :]) & (place < ends[None, :])
    member = inside.astype(FLOAT)
    slot_ids = jnp.sum(
        inside.astype(jnp.int32) * jnp.arange(strip.shape[0], dtype=jnp.int32)[None, :], axis=1
    )
    key_slots = jnp.tile(slot_ids, blocks)
    condition_full = condition_in.astype(FLOAT)
    cond_act = jax.nn.silu(condition_full).astype(HALF)
    modulation = matmul(cond_act, adaptive_matrix) + adaptive_vector.astype(FLOAT)
    per_token = jnp.dot(member, modulation, precision=HIGHEST, preferred_element_type=FLOAT)
    shift_one, scale_one, gate_one, shift_two, scale_two, gate_two = jnp.split(per_token, 6, axis=1)
    normed_one, inverse_one = normalize(inputs)
    hidden_one = (normed_one * (1.0 + scale_one) + shift_one).astype(HALF)
    projected = matmul(hidden_one, joint_matrix)
    query = (projected[:, :width] + query_vector.astype(FLOAT)).astype(HALF)
    keys = projected[:, width : 2 * width].astype(HALF)
    values = (projected[:, 2 * width :] + value_vector.astype(FLOAT)).astype(HALF)
    key_all, value_all = (
        lax.all_gather(keys, "blk", axis=0, tiled=True),
        lax.all_gather(values, "blk", axis=0, tiled=True),
    )
    log_total, attended = attend_forward(query, key_all, value_all, slot_ids, key_slots, scale)
    attended_half = attended.astype(HALF)
    branch_one = matmul(attended_half, output_matrix) + output_vector.astype(FLOAT)
    middle = inputs + gate_one * branch_one
    normed_two, inverse_two = normalize(middle)
    hidden_two = (normed_two * (1.0 + scale_two) + shift_two).astype(HALF)
    pre_act = matmul(hidden_two, up_matrix) + up_vector.astype(FLOAT)
    activated = gelu_tanh(pre_act).astype(HALF)
    branch_two = matmul(activated, down_matrix) + down_vector.astype(FLOAT)
    result = middle + gate_two * branch_two
    upstream = cotangent_in.astype(FLOAT)
    d_gate_two = upstream * branch_two
    d_branch_two = (upstream * gate_two).astype(HALF)
    d_pre = (right_outer(d_branch_two, down_matrix) * gelu_slope(pre_act)).astype(HALF)
    d_hidden_two = right_outer(d_pre, up_matrix)
    d_scale_two = d_hidden_two * normed_two
    d_middle = upstream + norm_backward(normed_two, inverse_two, d_hidden_two * (1.0 + scale_two))
    d_gate_one = d_middle * branch_one
    d_branch_one = (d_middle * gate_one).astype(HALF)
    d_attended = right_outer(d_branch_one, output_matrix).astype(HALF)
    delta = attention_delta(d_attended, attended)
    d_query_full, d_key_all, d_value_all = attend_backward(
        query, key_all, value_all, slot_ids, key_slots, log_total, delta, d_attended, scale
    )
    d_key_full, d_value_full = (
        lax.psum_scatter(
            d_key_all.astype(jnp.bfloat16), "blk", scatter_dimension=0, tiled=True
        ).astype(jnp.float32),
        lax.psum_scatter(
            d_value_all.astype(jnp.bfloat16), "blk", scatter_dimension=0, tiled=True
        ).astype(jnp.float32),
    )
    d_query = d_query_full.astype(HALF)
    d_keys = d_key_full.astype(HALF)
    d_values = d_value_full.astype(HALF)
    d_projected = jnp.concatenate([d_query, d_keys, d_values], axis=1)
    d_hidden_one = right_outer(d_projected, joint_matrix)
    d_scale_one = d_hidden_one * normed_one
    d_inputs = d_middle + norm_backward(normed_one, inverse_one, d_hidden_one * (1.0 + scale_one))
    d_per_token = jnp.concatenate(
        [d_hidden_one, d_scale_one, d_gate_one, d_hidden_two, d_scale_two, d_gate_two], axis=1
    )
    d_mod_local = lax.dot_general(
        member,
        d_per_token,
        (((0,), (0,)), ((), ())),
        precision=HIGHEST,
        preferred_element_type=FLOAT,
    )
    d_modulation = lax.psum(d_mod_local.astype(jnp.bfloat16), "blk").astype(jnp.float32)
    sigmoid_cond = jax.nn.sigmoid(condition_full)
    adaptive_float = adaptive_matrix.astype(FLOAT)
    d_condition = (
        lax.dot_general(
            d_modulation,
            adaptive_float,
            (((1,), (1,)), ((), ())),
            precision=HIGHEST,
            preferred_element_type=FLOAT,
        )
        * sigmoid_cond
        * (1.0 + condition_full * (1.0 - sigmoid_cond))
    )
    adaptive_grad = lax.dot_general(
        cond_act.astype(FLOAT),
        d_modulation,
        (((0,), (0,)), ((), ())),
        precision=HIGHEST,
        preferred_element_type=FLOAT,
    )
    local = (
        adaptive_grad * first_block,
        left_outer(hidden_one, d_projected),
        left_outer(attended_half, d_branch_one),
        left_outer(hidden_two, d_pre),
        left_outer(activated, d_branch_two),
        jnp.sum(d_modulation, axis=0) * first_block,
        jnp.sum(d_query.astype(FLOAT), axis=0),
        jnp.sum(d_values.astype(FLOAT), axis=0),
        jnp.sum(d_branch_one.astype(FLOAT), axis=0),
        jnp.sum(d_pre.astype(FLOAT), axis=0),
        jnp.sum(d_branch_two.astype(FLOAT), axis=0),
    )
    return (result, d_inputs, d_condition, local)


def general_body(
    tokens,
    cotangent,
    condition,
    lengths,
    adaptive_weight,
    joint_weight,
    output_weight,
    up_weight,
    down_weight,
    adaptive_bias,
    query_bias,
    value_bias,
    output_bias,
    up_bias,
    down_bias,
):
    micro = tokens.shape[1]
    blocks = lax.axis_size("blk")
    first_block = jnp.where(lax.axis_index("blk") == 0, 1.0, 0.0).astype(FLOAT)
    results = []
    token_grads = []
    condition_grads = []
    sums = None
    for step in range(micro):
        columns = (
            lax.all_gather(adaptive_weight, "blk", axis=1, tiled=True),
            lax.all_gather(joint_weight, "blk", axis=1, tiled=True),
            lax.all_gather(output_weight, "blk", axis=1, tiled=True),
            lax.all_gather(up_weight, "blk", axis=1, tiled=True),
            lax.all_gather(down_weight, "blk", axis=1, tiled=True),
            lax.all_gather(adaptive_bias, "blk", axis=0, tiled=True),
            lax.all_gather(query_bias, "blk", axis=0, tiled=True),
            lax.all_gather(value_bias, "blk", axis=0, tiled=True),
            lax.all_gather(output_bias, "blk", axis=0, tiled=True),
            lax.all_gather(up_bias, "blk", axis=0, tiled=True),
            lax.all_gather(down_bias, "blk", axis=0, tiled=True),
        )
        whole = (
            lax.all_gather(columns[0], "dp", axis=0, tiled=True),
            lax.all_gather(columns[1], "dp", axis=0, tiled=True),
            lax.all_gather(columns[2], "dp", axis=0, tiled=True),
            lax.all_gather(columns[3], "dp", axis=0, tiled=True),
            lax.all_gather(columns[4], "dp", axis=0, tiled=True),
        )
        full = tuple(whole) + tuple(columns[5:])
        result, d_inputs, d_condition, local = run_pack(
            full,
            tokens[0, step],
            cotangent[0, step],
            condition[0, step],
            lengths[0, step],
            blocks,
            first_block,
        )
        results.append(result)
        token_grads.append(d_inputs)
        condition_grads.append(d_condition)
        shares = (
            lax.psum_scatter(
                lax.psum_scatter(
                    local[0].astype(jnp.bfloat16), "dp", scatter_dimension=0, tiled=True
                ),
                "blk",
                scatter_dimension=1,
                tiled=True,
            ).astype(jnp.float32),
            lax.psum_scatter(
                lax.psum_scatter(
                    local[1].astype(jnp.bfloat16), "dp", scatter_dimension=0, tiled=True
                ),
                "blk",
                scatter_dimension=1,
                tiled=True,
            ).astype(jnp.float32),
            lax.psum_scatter(
                lax.psum_scatter(
                    local[2].astype(jnp.bfloat16), "dp", scatter_dimension=0, tiled=True
                ),
                "blk",
                scatter_dimension=1,
                tiled=True,
            ).astype(jnp.float32),
            lax.psum_scatter(
                lax.psum_scatter(
                    local[3].astype(jnp.bfloat16), "dp", scatter_dimension=0, tiled=True
                ),
                "blk",
                scatter_dimension=1,
                tiled=True,
            ).astype(jnp.float32),
            lax.psum_scatter(
                lax.psum_scatter(
                    local[4].astype(jnp.bfloat16), "dp", scatter_dimension=0, tiled=True
                ),
                "blk",
                scatter_dimension=1,
                tiled=True,
            ).astype(jnp.float32),
            lax.psum_scatter(
                lax.psum(local[5].astype(jnp.bfloat16), "dp"),
                "blk",
                scatter_dimension=0,
                tiled=True,
            ).astype(jnp.float32),
            lax.psum_scatter(
                lax.psum(local[6].astype(jnp.bfloat16), "dp"),
                "blk",
                scatter_dimension=0,
                tiled=True,
            ).astype(jnp.float32),
            lax.psum_scatter(
                lax.psum(local[7].astype(jnp.bfloat16), "dp"),
                "blk",
                scatter_dimension=0,
                tiled=True,
            ).astype(jnp.float32),
            lax.psum_scatter(
                lax.psum(local[8].astype(jnp.bfloat16), "dp"),
                "blk",
                scatter_dimension=0,
                tiled=True,
            ).astype(jnp.float32),
            lax.psum_scatter(
                lax.psum(local[9].astype(jnp.bfloat16), "dp"),
                "blk",
                scatter_dimension=0,
                tiled=True,
            ).astype(jnp.float32),
            lax.psum_scatter(
                lax.psum(local[10].astype(jnp.bfloat16), "dp"),
                "blk",
                scatter_dimension=0,
                tiled=True,
            ).astype(jnp.float32),
        )
        sums = (
            shares
            if sums is None
            else tuple((first + second for first, second in zip(sums, shares)))
        )
    block_output = jnp.stack(results, axis=0)[None]
    tokens_grad = jnp.stack(token_grads, axis=0)[None]
    condition_grad = jnp.stack(condition_grads, axis=0)[None]
    return (
        block_output,
        tokens_grad,
        condition_grad,
        sums[0],
        sums[1],
        sums[2],
        sums[3],
        sums[4],
        sums[5],
        sums[6],
        sums[7],
        sums[8],
        sums[9],
        sums[10],
    )


HEAD = 72
EXPONENT = HEAD**-0.5 * 1.4426950408889634


WINDOW = 256


def head_window(head, width):
    start = jnp.minimum(lax.div(head * HEAD, 128) * 128, width - WINDOW)
    return pl.ds(pl.multiple_of(start, 128), WINDOW), head * HEAD - start


def head_windows(group):
    heads = []
    for pair in range(group // 2):
        pair = pl.program_id(1) * (group // 2) + pair
        late = jnp.where(pair >= HEADS // 4, 1, 0)
        for head, size in ((2 * pair + late, 128), (2 * pair + 1 - late, 256)):
            start = lax.div(head * HEAD, 128) * 128
            heads.append((head, pl.ds(pl.multiple_of(start, 128), size), head * HEAD - start, size))
    return heads


def head_lanes(offset, rows, size):
    lane = lax.broadcasted_iota(jnp.int32, (rows, size), 1)
    return (lane >= offset) & (lane < offset + HEAD)


def for_images(info, unit, image):
    @pl.when(info[8 + unit] == 1)
    def _():
        image(info[unit], 512, 256)

    @pl.when(info[8 + unit] == 0)
    def _():
        def step(index, carry):
            image(info[unit + index], 128, 128)
            return carry

        lax.fori_loop(0, 4, step, 0)


def image_rows(start, strip, half, index, block):
    place = index * block
    place = start + (place if place < strip else half + place - strip)
    return pl.ds(pl.multiple_of(place, 128), block)


def both_strips(ref, start, strip, half, window):
    return jnp.concatenate(
        [ref[pl.ds(start, strip), window], ref[pl.ds(half + start, strip), window]], axis=0
    )


def attend_forward_kernel(info, q_ref, k_ref, v_ref, o_ref, total_ref, *, group):
    half, width = q_ref.shape[0] // 2, q_ref.shape[1]

    def image(start, strip, block):
        start = pl.multiple_of(start, 128)
        work = []
        for member in range(group):
            head = pl.program_id(1) * group + member
            window, offset = head_window(head, width)
            keys = both_strips(k_ref, start, strip, half, window)
            keys = jnp.where(head_lanes(offset, 2 * strip, WINDOW), keys, jnp.zeros_like(keys))
            values = both_strips(v_ref, start, strip, half, window).T
            for index in range(2 * strip // block):
                rows = image_rows(start, strip, half, index, block)
                work.append((head, window, offset, keys, values, rows))

        def scores_of(item):
            return right_outer(item[3], q_ref[item[5], item[1]])

        coming = scores_of(work[0])
        for index, item in enumerate(work):
            head, window, offset, keys, values, rows = item
            scores = coming
            if index + 1 < len(work):
                coming = scores_of(work[index + 1])
            top = jnp.max(scores, axis=0, keepdims=True)
            expo = jnp.exp2((scores - top) * EXPONENT)
            mass = jnp.sum(expo, axis=0, keepdims=True)
            out = (matmul(values, expo.astype(HALF)) * (1.0 / mass)).T.astype(HALF)
            o_ref[rows, window] = jnp.where(head_lanes(offset, block, WINDOW), out, o_ref[rows, window])
            total_ref[head, :, rows] = top * EXPONENT + jnp.log2(mass)

    for_images(info, pl.program_id(0), image)


def attend_backward_kernel(
    info, q_ref, k_ref, v_ref, do_ref, total_ref, delta_ref, dq_ref, dk_ref, dv_ref, *, group
):
    half = q_ref.shape[0] // 2
    scale = HEAD**-0.5

    def image(start, strip, block):
        start = pl.multiple_of(start, 128)
        count = 2 * strip // block
        work = []
        for head, window, offset, size in head_windows(group):
            keys = both_strips(k_ref, start, strip, half, window)
            values = both_strips(v_ref, start, strip, half, window)
            inside = head_lanes(offset, 2 * strip, size)
            head_keys = jnp.where(inside, keys, jnp.zeros_like(keys))
            head_values = jnp.where(inside, values, jnp.zeros_like(values))
            turned = keys.T
            lanes = head_lanes(offset, block, size)
            for index in range(count):
                rows = image_rows(start, strip, half, index, block)
                work.append((head, window, lanes, head_keys, head_values, turned, rows))

        def begin(item):
            head, window, lanes, keys, values, turned, rows = item
            return (
                right_outer(keys, q_ref[rows, window]),
                right_outer(values, do_ref[rows, window]),
            )

        def middle(item, scores, d_weights):
            head, rows = item[0], item[6]
            weights = jnp.exp2(scores * EXPONENT - total_ref[head, :, rows])
            d_scores = weights * (d_weights - delta_ref[head, :, rows])
            return weights.astype(HALF), d_scores.astype(HALF)

        kept = []

        def finish(item, weights, d_scores):
            head, window, lanes, keys, values, turned, rows = item
            d_query = (matmul(turned, d_scores).T * scale).astype(HALF)
            dq_ref[rows, window] = jnp.where(lanes, d_query, dq_ref[rows, window])
            kept.append((weights, d_scores))
            if len(kept) < count:
                return
            weights = jnp.concatenate([part for part, _ in kept], axis=1)
            d_scores = jnp.concatenate([part for _, part in kept], axis=1)
            kept.clear()
            d_keys = matmul(d_scores, both_strips(q_ref, start, strip, half, window))
            d_values = matmul(weights, both_strips(do_ref, start, strip, half, window))
            for ref, value in (
                (dk_ref, (d_keys * scale).astype(HALF)),
                (dv_ref, d_values.astype(HALF)),
            ):
                for index in range(count):
                    rows = image_rows(start, strip, half, index, block)
                    part = value[index * block : (index + 1) * block]
                    ref[rows, window] = jnp.where(lanes, part, ref[rows, window])

        coming = begin(work[0])
        late = None
        for index, item in enumerate(work):
            now = coming
            if index + 1 < len(work):
                coming = begin(work[index + 1])
            if late is not None:
                finish(*late)
            late = (item,) + middle(item, *now)
        finish(*late)

    for_images(info, pl.program_id(0), image)


def attention_call(kernel, name, info, arrays, outputs, group, flops):
    def whole(array):
        return pl.BlockSpec(
            array.shape,
            lambda unit, head, info: (0,) * len(array.shape),
            pipeline_mode=pl.Buffered(1),
        )

    return pl.pallas_call(
        functools.partial(kernel, group=group),
        grid_spec=pltpu.PrefetchScalarGridSpec(
            num_scalar_prefetch=1,
            grid=(2, HEADS // group),
            in_specs=[whole(array) for array in arrays],
            out_specs=[whole(array) for array in outputs],
        ),
        out_shape=outputs,
        compiler_params=pltpu.CompilerParams(vmem_limit_bytes=60 * 2**20),
        cost_estimate=pl.CostEstimate(
            flops=flops, bytes_accessed=30 * 2**20, transcendentals=HEADS * 2**21
        ),
        name=name,
    )(info, *arrays)


def attend_pack(info, query, keys, values):
    rows, width = query.shape
    outputs = [
        jax.ShapeDtypeStruct((rows, width), HALF),
        jax.ShapeDtypeStruct((HEADS, 1, rows), FLOAT),
    ]
    return attention_call(
        attend_forward_kernel, "attend", info, [query, keys, values], outputs, 4, 70 * 10**9
    )


def attend_pack_backward(info, query, keys, values, grad, total, delta):
    outputs = [jax.ShapeDtypeStruct(query.shape, HALF)] * 3
    arrays = [query, keys, values, grad, total, delta]
    return attention_call(
        attend_backward_kernel, "attend_backward", info, arrays, outputs, 4, 140 * 10**9
    )


BLOCK = 256
PART = 128
STRIP = 32


def resident(array):
    return pl.BlockSpec(
        array.shape, lambda *step: (0,) * len(array.shape), pipeline_mode=pl.Buffered(1)
    )


def by_rows(array):
    size = BLOCK if len(array.shape) == 2 else BLOCK // PART
    zeros = (0,) * (len(array.shape) - 1)
    return pl.BlockSpec((size,) + array.shape[1:], lambda step, *scalars: (step,) + zeros)


def dense_call(kernel, name, rows, inputs, outputs, scratch=(), flops=0, strip=None):
    size = sum(array.size * array.dtype.itemsize for array, _ in inputs + outputs)
    scalars = [] if strip is None else [strip.reshape(1).astype(jnp.int32)]

    def run(*refs):
        kernel(*refs[len(scalars) :])

    return pl.pallas_call(
        run,
        grid_spec=pltpu.PrefetchScalarGridSpec(
            num_scalar_prefetch=len(scalars),
            grid=(rows // BLOCK,),
            in_specs=[spec for _, spec in inputs],
            out_specs=[spec for _, spec in outputs],
            scratch_shapes=list(scratch),
        ),
        out_shape=[shape for shape, _ in outputs],
        compiler_params=pltpu.CompilerParams(vmem_limit_bytes=60 * 2**20),
        cost_estimate=pl.CostEstimate(flops=flops, bytes_accessed=size, transcendentals=0),
        name=name,
    )(*scalars, *[array for array, _ in inputs])


def shape_of(*dims, kind=None):
    return jax.ShapeDtypeStruct(dims, kind or FLOAT)


def strips():
    return [
        (pl.ds(begin, STRIP), begin // PART, begin % PART == 0) for begin in range(0, BLOCK, STRIP)
    ]


def row_norm(values):
    center = values - jnp.mean(values, axis=1, keepdims=True)
    inverse = lax.rsqrt(jnp.mean(center * center, axis=1, keepdims=True) + EPSILON)
    return center * inverse, inverse


def fold(values):
    return jnp.sum(values.reshape(-1, 8, values.shape[1]), axis=0)


class Sums:
    def __init__(self):
        self.held = {}

    def add(self, ref, part, first, values):
        folded = fold(values)
        key = id(ref), part
        if not first:
            folded = self.held[key][1] + folded
        self.held[key] = (ref, folded)

    def store(self):
        for (_, part), (ref, value) in self.held.items():
            ref[part] = jnp.sum(value, axis=0, keepdims=True)


TILE_ROWS = 32
TILE_COLUMNS = 256


def tiles(rows, columns):
    return [
        (row, column)
        for row in range(0, rows, TILE_ROWS)
        for column in range(0, columns, TILE_COLUMNS)
    ]


def up_kernel(x_ref, w_ref, bias_ref, act_ref, slope_ref, *, chunk):
    x = x_ref[...]
    halves, _, columns = w_ref.shape
    work = [(half, begin) for half in range(halves) for begin in range(0, columns, chunk)]

    def product(item):
        return matmul(x, w_ref[item[0], :, pl.ds(item[1], chunk)])

    coming = product(work[0])
    for index, (half, begin) in enumerate(work):
        now = coming
        if index + 1 < len(work):
            coming = product(work[index + 1])
        for row, column in tiles(BLOCK, chunk):
            rows = pl.ds(row, TILE_ROWS)
            place = pl.ds(half * columns + begin + column, TILE_COLUMNS)
            value = now[row : row + TILE_ROWS, column : column + TILE_COLUMNS] + bias_ref[:, place]
            square = value * value
            gate = 0.5 + 0.5 * jnp.tanh(
                value * (GELU_SCALE + (GELU_SCALE * 0.044715) * square)
            )
            active = (value * gate).astype(HALF)
            gate, square = gate.astype(HALF), square.astype(HALF)
            bend = 2.0 * GELU_SCALE + (6.0 * GELU_SCALE * 0.044715) * square
            act_ref[rows, place] = active
            slope_ref[rows, place] = gate + active * (1.0 - gate) * bend


def up_call(hidden, weight, bias, chunk=768):
    rows, width = hidden.shape
    wide = 2 * weight.shape[2]
    out = shape_of(rows, wide, kind=HALF)
    return dense_call(
        functools.partial(up_kernel, chunk=chunk),
        "up",
        rows,
        [(hidden, by_rows(hidden)), (weight, resident(weight)), (bias, resident(bias))],
        [(out, by_rows(out)), (out, by_rows(out))],
        flops=2 * rows * width * wide,
    )


def down_grad_kernel(x_ref, slope_ref, w_ref, d_pre_ref, sum_ref, wide_ref, *, chunk):
    x = x_ref[...]
    sum_ref[0] = jnp.sum(fold(x.astype(FLOAT)), axis=0, keepdims=True)
    wide = w_ref.shape[0]
    work = list(range(0, wide, chunk))

    def product(begin):
        return right_outer(x, w_ref[pl.ds(begin, chunk), :])

    coming = product(work[0])
    for index, begin in enumerate(work):
        now = coming
        if index + 1 < len(work):
            coming = product(work[index + 1])
        for column in range(0, chunk, TILE_COLUMNS):
            place = pl.ds(begin + column, TILE_COLUMNS)
            total = None
            for row in range(0, BLOCK, TILE_ROWS):
                rows = pl.ds(row, TILE_ROWS)
                value = now[row : row + TILE_ROWS, column : column + TILE_COLUMNS]
                value = (value * slope_ref[rows, place].astype(FLOAT)).astype(HALF)
                d_pre_ref[rows, place] = value
                folded = fold(value.astype(FLOAT))
                total = folded if total is None else total + folded
            wide_ref[0, :, place] = jnp.sum(total, axis=0, keepdims=True)


def down_grad_call(d_branch, slope, weight, chunk=768):
    rows, width = d_branch.shape
    wide = weight.shape[0]
    steps = rows // BLOCK
    d_pre = shape_of(rows, wide, kind=HALF)
    total, wide_total = shape_of(steps, 1, width), shape_of(steps, 1, wide)

    def per_step(shape):
        return pl.BlockSpec((1,) + shape.shape[1:], lambda step, *scalars: (step, 0, 0))

    return dense_call(
        functools.partial(down_grad_kernel, chunk=chunk),
        "down_grad",
        rows,
        [
            (d_branch, by_rows(d_branch)),
            (slope, by_rows(slope)),
            (weight, resident(weight)),
        ],
        [
            (d_pre, by_rows(d_pre)),
            (total, per_step(total)),
            (wide_total, per_step(wide_total)),
        ],
        flops=2 * rows * width * wide,
    )


def project_kernel(x_ref, shift_ref, scale_ref, w_ref, bias_ref, hidden_ref, q_ref, k_ref, v_ref):
    for rows, part, _ in strips():
        normed, _ = row_norm(x_ref[rows, :].astype(FLOAT))
        hidden_ref[rows, :] = (normed * (1.0 + scale_ref[part]) + shift_ref[part]).astype(HALF)
    hidden = hidden_ref[...]
    width = hidden.shape[1]
    for index, ref in enumerate((q_ref, k_ref, v_ref)):
        place = pl.ds(index * width, width)
        ref[...] = (matmul(hidden, w_ref[:, place]) + bias_ref[:, place]).astype(HALF)


def project_call(tokens, shift, scale, weight, bias):
    rows, width = tokens.shape
    out = shape_of(rows, width, kind=HALF)
    return dense_call(
        project_kernel,
        "project",
        rows,
        [
            (tokens, by_rows(tokens)),
            (shift, by_rows(shift)),
            (scale, by_rows(scale)),
            (weight, resident(weight)),
            (bias, resident(bias)),
        ],
        [(out, by_rows(out))] * 4,
        flops=6 * rows * width * width,
    )


def mix_kernel(
    attended_ref, x_ref, gate_ref, shift_ref, scale_ref, w_ref, bias_ref, branch_ref, hidden_ref
):
    branch_ref[...] = matmul(attended_ref[...], w_ref[...]) + bias_ref[...]
    for rows, part, _ in strips():
        middle = x_ref[rows, :].astype(FLOAT) + gate_ref[part] * branch_ref[rows, :]
        normed, _ = row_norm(middle)
        hidden_ref[rows, :] = (normed * (1.0 + scale_ref[part]) + shift_ref[part]).astype(HALF)


def mix_call(attended, tokens, gate, shift, scale, weight, bias):
    rows, width = tokens.shape
    branch, hidden = shape_of(rows, width), shape_of(rows, width, kind=HALF)
    return dense_call(
        mix_kernel,
        "mix",
        rows,
        [
            (attended, by_rows(attended)),
            (tokens, by_rows(tokens)),
            (gate, by_rows(gate)),
            (shift, by_rows(shift)),
            (scale, by_rows(scale)),
            (weight, resident(weight)),
            (bias, resident(bias)),
        ],
        [(branch, by_rows(branch)), (hidden, by_rows(hidden))],
        flops=2 * rows * width * width,
    )


def finish_kernel(
    act_ref, x_ref, branch_ref, cot_ref, gate_one_ref, gate_two_ref, w_ref, bias_ref,
    own_ref, other_ref, sum_ref, branch_two,
):
    branch_two[...] = matmul(act_ref[...], w_ref[...]) + bias_ref[...]
    step = pl.program_id(0)
    sums = Sums()
    for rows, part, first in strips():
        middle = x_ref[rows, :].astype(FLOAT) + gate_one_ref[part] * branch_ref[rows, :]
        two = branch_two[rows, :]
        sums.add(sum_ref, part, first, cot_ref[rows, :].astype(FLOAT) * two)
        branch_two[rows, :] = middle + gate_two_ref[part] * two
    sums.store()
    store_strip(step, branch_two, own_ref, other_ref)


def store_strip(step, value_ref, own_ref, other_ref):
    half = pl.num_programs(0) // 2

    @pl.when(step < half)
    def _():
        own_ref[...] = value_ref[...]

    @pl.when(step >= half)
    def _():
        other_ref[...] = value_ref[...].astype(HALF)


def strip_specs(rows, width):
    half = rows // BLOCK // 2
    both, other = shape_of(2, rows // 2, width), shape_of(rows // 2, width, kind=HALF)

    def own_place(step, strip):
        return strip[0], jnp.minimum(step, half - 1), 0

    def other_place(step, strip):
        return jnp.maximum(step - half, 0), 0

    return [
        (both, pl.BlockSpec((None, BLOCK, width), own_place)),
        (other, pl.BlockSpec((BLOCK, width), other_place)),
    ]


def join_kernel(own_ref, other_ref, gate_ref, both_ref, d_branch_ref):
    first = pl.program_id(0) < pl.num_programs(0) // 2
    both_ref[...] = jnp.where(first, own_ref[...].astype(FLOAT), other_ref[...].astype(FLOAT)).astype(HALF)
    for rows, part, _ in strips():
        d_branch_ref[rows, :] = (both_ref[rows, :].astype(FLOAT) * gate_ref[part]).astype(HALF)


def join_call(pair, other, gate, strip):
    half, width = other.shape
    steps = half // BLOCK
    out = shape_of(2 * half, width, kind=HALF)
    own_spec = pl.BlockSpec(
        (None, BLOCK, width), lambda step, strip: (strip[0], jnp.minimum(step, steps - 1), 0)
    )
    other_spec = pl.BlockSpec(
        (BLOCK, width), lambda step, strip: (jnp.maximum(step - steps, 0), 0)
    )
    return dense_call(
        join_kernel,
        "join",
        2 * half,
        [(pair, own_spec), (other, other_spec), (gate, by_rows(gate))],
        [(out, by_rows(out)), (out, by_rows(out))],
        strip=strip,
    )


def fill_kernel(strip, both_ref, other_ref, out_ref):
    out_ref[...] = other_ref[...].astype(FLOAT)


def fill_call(both, other, strip):
    rows, width = other.shape
    return pl.pallas_call(
        fill_kernel,
        grid_spec=pltpu.PrefetchScalarGridSpec(
            num_scalar_prefetch=1,
            grid=(rows // BLOCK,),
            in_specs=[
                pl.BlockSpec(memory_space=pl.ANY),
                pl.BlockSpec((BLOCK, width), lambda step, strip: (step, 0)),
            ],
            out_specs=pl.BlockSpec(
                (None, BLOCK, width), lambda step, strip: (1 - strip[0], step, 0)
            ),
        ),
        out_shape=jax.ShapeDtypeStruct(both.shape, both.dtype),
        input_output_aliases={1: 0},
        cost_estimate=pl.CostEstimate(flops=0, bytes_accessed=8 * 2**20, transcendentals=0),
        name="fill",
    )(strip.reshape(1).astype(jnp.int32), both, other)


def finish_call(active, tokens, branch, cotangent, gate_one, gate_two, weight, bias, strip):
    rows, width = tokens.shape
    sums = shape_of(rows // PART, 1, width)
    return dense_call(
        finish_kernel,
        "finish",
        rows,
        [
            (active, by_rows(active)),
            (tokens, by_rows(tokens)),
            (branch, by_rows(branch)),
            (cotangent, by_rows(cotangent)),
            (gate_one, by_rows(gate_one)),
            (gate_two, by_rows(gate_two)),
            (weight, resident(weight)),
            (bias, resident(bias)),
        ],
        strip_specs(rows, width) + [(sums, by_rows(sums))],
        scratch=[pltpu.VMEM((BLOCK, width), FLOAT)],
        flops=2 * rows * active.shape[1] * width,
        strip=strip,
    )


def norm_pull(normed, inverse, grad):
    mean_grad = jnp.mean(grad, axis=1, keepdims=True)
    mean_cross = jnp.mean(grad * normed, axis=1, keepdims=True)
    return inverse * (grad - mean_grad - normed * mean_cross)


def mix_grad_kernel(
    d_pre_ref, attended_ref, x_ref, branch_ref, cot_ref, gate_ref, scale_ref, up_ref, out_ref,
    d_middle_ref, d_branch_ref, d_attended_ref, delta_ref, shift_sum, scale_sum, gate_sum, bias_sum, hidden,
):
    columns = up_ref.shape[2]
    hidden[...] = right_outer(d_pre_ref[:, :columns], up_ref[0]) + right_outer(
        d_pre_ref[:, columns:], up_ref[1]
    )
    sums = Sums()
    for rows, part, first in strips():
        branch, grad = branch_ref[rows, :], hidden[rows, :]
        gate = gate_ref[part]
        normed, inverse = row_norm(x_ref[rows, :].astype(FLOAT) + gate * branch)
        sums.add(shift_sum, part, first, grad)
        sums.add(scale_sum, part, first, grad * normed)
        d_middle = cot_ref[rows, :].astype(FLOAT) + norm_pull(
            normed, inverse, grad * (1.0 + scale_ref[part])
        )
        d_middle_ref[rows, :] = d_middle
        sums.add(gate_sum, part, first, d_middle * branch)
        d_branch = (d_middle * gate).astype(HALF)
        d_branch_ref[rows, :] = d_branch
        sums.add(bias_sum, part, first, d_branch.astype(FLOAT))
    sums.store()
    d_attended = right_outer(d_branch_ref[...], out_ref[...]).astype(HALF)
    d_attended_ref[...] = d_attended
    product = d_attended.astype(FLOAT) * attended_ref[...].astype(FLOAT)
    heads, width = HEADS, product.shape[1]
    lane = lax.broadcasted_iota(jnp.int32, (heads, width), 1)
    head = lax.broadcasted_iota(jnp.int32, (heads, width), 0) * HEAD
    member = jnp.where((lane >= head) & (lane < head + HEAD), 1.0, 0.0).astype(HALF)
    high = product.astype(HALF)
    low = (product - high.astype(FLOAT)).astype(HALF)
    delta = right_outer(member, high) + right_outer(member, low)
    for index in range(heads):
        delta_ref[index] = delta[index : index + 1]


def mix_grad_call(d_pre, attended, tokens, branch, cotangent, gate, scale, up, out):
    rows, width = tokens.shape
    half, sums = shape_of(rows, width, kind=HALF), shape_of(rows // PART, 1, width)
    d_middle, delta = shape_of(rows, width), shape_of(HEADS, 1, rows)
    return dense_call(
        mix_grad_kernel,
        "mix_grad",
        rows,
        [
            (d_pre, by_rows(d_pre)),
            (attended, by_rows(attended)),
            (tokens, by_rows(tokens)),
            (branch, by_rows(branch)),
            (cotangent, by_rows(cotangent)),
            (gate, by_rows(gate)),
            (scale, by_rows(scale)),
            (up, resident(up)),
            (out, resident(out)),
        ],
        [(d_middle, by_rows(d_middle)), (half, by_rows(half)), (half, by_rows(half))]
        + [(delta, pl.BlockSpec((HEADS, 1, BLOCK), lambda step, *scalars: (0, 0, step)))]
        + [(sums, by_rows(sums))] * 4,
        scratch=[pltpu.VMEM((BLOCK, width), FLOAT)],
        flops=2 * rows * width * (d_pre.shape[1] + width),
    )


def project_grad_kernel(
    dq_ref, dk_ref, dv_ref, x_ref, d_middle_ref, scale_ref, w_ref,
    own_ref, other_ref, shift_sum, scale_sum, query_sum, value_sum, hidden,
):
    grads = jnp.concatenate([dq_ref[...], dk_ref[...], dv_ref[...]], axis=1)
    hidden[...] = right_outer(grads, w_ref[...])
    sums = Sums()
    for rows, part, first in strips():
        grad = hidden[rows, :]
        normed, inverse = row_norm(x_ref[rows, :].astype(FLOAT))
        sums.add(shift_sum, part, first, grad)
        sums.add(scale_sum, part, first, grad * normed)
        sums.add(query_sum, part, first, dq_ref[rows, :].astype(FLOAT))
        sums.add(value_sum, part, first, dv_ref[rows, :].astype(FLOAT))
        hidden[rows, :] = d_middle_ref[rows, :] + norm_pull(
            normed, inverse, grad * (1.0 + scale_ref[part])
        )
    sums.store()
    store_strip(pl.program_id(0), hidden, own_ref, other_ref)


def project_grad_call(d_query, d_keys, d_values, tokens, d_middle, scale, weight, strip):
    rows, width = tokens.shape
    sums = shape_of(rows // PART, 1, width)
    return dense_call(
        project_grad_kernel,
        "project_grad",
        rows,
        [
            (d_query, by_rows(d_query)),
            (d_keys, by_rows(d_keys)),
            (d_values, by_rows(d_values)),
            (tokens, by_rows(tokens)),
            (d_middle, by_rows(d_middle)),
            (scale, by_rows(scale)),
            (weight, resident(weight)),
        ],
        strip_specs(rows, width) + [(sums, by_rows(sums))] * 4,
        scratch=[pltpu.VMEM((BLOCK, width), FLOAT)],
        flops=6 * rows * width * width,
        strip=strip,
    )


MESH = pl.DeviceIdType.MESH


class Place:
    def __init__(self):
        me = lax.axis_index("dp")
        self.me, self.y = me, lax.axis_index("blk")
        self.z, self.x, self.core = me // 4, (me // 2) % 2, me % 2

    def at(self, z_step, x_step, core_step):
        z = (self.z + 4 - z_step) % 4
        return z * 4 + ((self.x + x_step) % 2) * 2 + (self.core + core_step) % 2

    def half(self, y_step):
        return (self.y + y_step) % 2

    def partner(self, kind):
        if kind == "y":
            return {"blk": 1 - self.y}
        if kind == "z":
            return {"dp": (self.me + 4) % 16}
        if kind == "back":
            return {"dp": (self.me + 12) % 16}
        if kind == "x":
            return {"dp": self.at(0, 1, 0)}
        return {"dp": self.at(0, 0, 1)}

    def greet(self):
        barrier = pltpu.get_barrier_semaphore()
        for kind in ("y", "z", "back", "x", "core"):
            pl.semaphore_signal(
                barrier, inc=1, device_id=self.partner(kind), device_id_type=MESH
            )
        pl.semaphore_wait(barrier, 5)


class Copies:
    def __init__(self, place, send_sems, recv_sems):
        self.place, self.send_sems, self.recv_sems = place, send_sems, recv_sems
        self.made = {}

    def send(self, key, source, target):
        index = len(self.made)
        copy = pltpu.make_async_remote_copy(
            src_ref=source,
            dst_ref=target,
            send_sem=self.send_sems.at[index],
            recv_sem=self.recv_sems.at[index],
            device_id=self.place.partner(key[0]),
            device_id_type=MESH,
        )
        self.made[key] = copy
        copy.start()

    def receive(self, key):
        self.made[key].wait_recv()

    def finish(self):
        for copy in self.made.values():
            copy.wait_send()


def head_kernel(
    joint_ref,
    output_ref,
    condition_ref,
    adaptive_ref,
    bias_ref,
    tokens_ref,
    whole_joint_ref,
    whole_output_ref,
    modulation_ref,
    act_ref,
    other_ref,
    joint_from_y,
    output_from_y,
    joint_slot,
    output_slot,
    conditions,
    parts,
    from_core,
    from_x,
    from_z,
    share,
    from_y,
    local_sems,
    send_sems,
    recv_sems,
):
    place = Place()
    copies = Copies(place, send_sems, recv_sems)
    place.greet()
    conditions[place.me] = condition_ref[...]

    def condition(kind, z_step, x_step):
        slot = conditions.at[place.at(z_step, x_step, 0)]
        copies.send((kind, "condition", z_step, x_step), slot, slot)

    def weight(kind, z_step, x_step):
        for name, slot, whole in (
            ("joint", joint_slot, whole_joint_ref),
            ("output", output_slot, whole_output_ref),
        ):
            target = whole.at[place.at(z_step, x_step, 0)]
            mine = z_step == 0 and x_step == 0
            copies.send((kind, name, z_step, x_step), slot if mine else target, target)

    def arrived(kind, z_step, x_step):
        copies.receive((kind, "joint", z_step, x_step))
        copies.receive((kind, "output", z_step, x_step))

    def forward_condition(z_step):
        for x_step in range(2):
            copies.receive(("z", "condition", z_step - 1, x_step))
            if z_step < 3:
                condition("z", z_step, x_step)
            condition("core", z_step, x_step)

    def forward(z_step):
        arrived("z", z_step - 1, 0)
        if z_step < 3:
            weight("z", z_step, 0)
        weight("x", z_step, 0)
        weight("core", z_step, 0)

    copies.send(("y", "joint"), joint_ref, joint_from_y)
    copies.send(("y", "output"), output_ref, output_from_y)
    condition("x", 0, 0)
    condition("z", 0, 0)
    condition("core", 0, 0)
    copies.send(("y", "tokens"), tokens_ref.at[place.half(1)], other_ref)
    copies.receive(("x", "condition", 0, 0))
    condition("z", 0, 1)
    condition("core", 0, 1)
    forward_condition(1)

    owns = []
    for name, mine, other, slot, whole in (
        ("joint", joint_ref, joint_from_y, joint_slot, whole_joint_ref),
        ("output", output_ref, output_from_y, output_slot, whole_output_ref),
    ):
        copies.receive(("y", name))
        first, second = mine[...].astype(FLOAT), other[...].astype(FLOAT)
        low = place.y == 0
        slot[...] = jnp.concatenate(
            [jnp.where(low, first, second), jnp.where(low, second, first)], axis=1
        ).astype(HALF)
        own = pltpu.make_async_copy(slot, whole.at[place.me], local_sems.at[len(owns)])
        own.start()
        owns.append(own)
    weight("z", 0, 0)
    weight("x", 0, 0)
    weight("core", 0, 0)
    forward_condition(2)
    forward_condition(3)
    forward(1)
    for z_step in range(4):
        for x_step in range(2):
            copies.receive(("core", "condition", z_step, x_step))

    adaptive = adaptive_ref[...]
    count, rows = conditions.shape[0], conditions.shape[2]
    for index in range(count):
        values = conditions[index, place.me].astype(FLOAT)
        act_ref[index] = (values / (1.0 + jnp.exp(-values))).astype(HALF)

    def products(core_step):
        targets = [
            place.at((4 - z_step) % 4, x_step, core_step)
            for z_step in range(4)
            for x_step in range(2)
        ]
        acts = jnp.concatenate([act_ref[target] for target in targets], axis=0)
        product = matmul(acts, adaptive).astype(HALF)
        parts[core_step] = product.reshape(parts.shape[1:])

    def add(first, second):
        return first.astype(FLOAT) + second.astype(FLOAT)

    products(1)
    for z_step in (3, 2, 1, 0):
        copies.send(("core", "part", z_step), parts.at[1, z_step], from_core.at[z_step])
    products(0)
    forward(2)
    for z_step in (3, 2, 1, 0):
        copies.receive(("core", "part", z_step))
        total = add(parts[0, z_step], from_core[z_step])
        if z_step < 3:
            copies.receive(("z", "part", z_step + 1))
            total = total + from_z[z_step].astype(FLOAT)
        parts[0, z_step] = total.astype(HALF)
        if z_step > 0:
            copies.send(("z", "part", z_step), parts.at[0, z_step], from_z.at[z_step - 1])
        if z_step == 1:
            forward(3)
    copies.send(("x", "part"), parts.at[0, 0, 1], from_x)

    def last(z_step):
        arrived("x", z_step, 0)
        weight("core", z_step, 1)

    last(0)
    last(1)
    images = rows // 2
    copies.receive(("x", "part"))
    total = add(parts[0, 0, 0], from_x[...]) + bias_ref[...]
    share[0] = total[:images]
    share[1] = total[images:]
    copies.send(("y", "part"), share.at[place.half(1)], from_y)
    modulation_ref[place.half(0)] = share[place.half(0)]
    last(2)
    last(3)
    copies.receive(("y", "part"))
    modulation_ref[place.half(1)] = from_y[...]
    for z_step in range(4):
        for x_step in range(2):
            arrived("core", z_step, x_step)
    copies.receive(("y", "tokens"))
    for own in owns:
        own.wait()
    copies.finish()


def head(joint_weight, output_weight, condition, adaptive_weight, adaptive_bias, tokens):
    micro, images, width = condition.shape
    features, columns = adaptive_weight.shape
    rows = micro * images
    condition = condition.reshape(rows, width // features, features).transpose(1, 0, 2)
    count = 16
    vmem = pl.BlockSpec(memory_space=pltpu.VMEM)
    anywhere = pl.BlockSpec(memory_space=pl.ANY)
    slots = [(shard.shape[0], 2 * shard.shape[1]) for shard in (joint_weight, output_weight)]
    joint, output, modulation, act, other = pl.pallas_call(
        head_kernel,
        out_shape=[jax.ShapeDtypeStruct((count,) + slot, HALF) for slot in slots]
        + [
            jax.ShapeDtypeStruct((2, images, columns), FLOAT),
            jax.ShapeDtypeStruct((count, rows, features), HALF),
            jax.ShapeDtypeStruct(tokens.shape[1:], HALF),
        ],
        in_specs=[vmem] * 5 + [anywhere],
        out_specs=[anywhere, anywhere, vmem, vmem, anywhere],
        scratch_shapes=[
            pltpu.VMEM(joint_weight.shape, HALF),
            pltpu.VMEM(output_weight.shape, HALF),
            pltpu.VMEM(slots[0], HALF),
            pltpu.VMEM(slots[1], HALF),
            pltpu.VMEM((count,) + condition.shape, HALF),
            pltpu.VMEM((2, 4, 2, rows, columns), HALF),
            pltpu.VMEM((4, 2, rows, columns), HALF),
            pltpu.VMEM((rows, columns), HALF),
            pltpu.VMEM((3, 2, rows, columns), HALF),
            pltpu.VMEM((2, images, columns), FLOAT),
            pltpu.VMEM((images, columns), FLOAT),
            pltpu.SemaphoreType.DMA((2,)),
            pltpu.SemaphoreType.DMA((64,)),
            pltpu.SemaphoreType.DMA((64,)),
        ],
        compiler_params=pltpu.CompilerParams(
            collective_id=1, has_side_effects=True, vmem_limit_bytes=48 * 2**20
        ),
        cost_estimate=pl.CostEstimate(flops=0, bytes_accessed=200 * 2**20, transcendentals=0),
        name="head",
    )(
        joint_weight,
        output_weight,
        condition,
        adaptive_weight,
        adaptive_bias.astype(FLOAT)[None],
        tokens,
    )
    return (
        joint.reshape(-1, joint.shape[2]),
        output.reshape(-1, output.shape[2]),
        modulation,
        act,
        other,
    )


def tail_kernel(
    grad_ref,
    half_ref,
    vector_ref,
    strip_ref,
    share_ref,
    all_ref,
    total_ref,
    other_ref,
    own,
    from_core,
    from_x,
    from_z,
    half_sum,
    from_y,
    pair,
    pair_from_y,
    vector,
    vector_from,
    vector_z,
    local_sems,
    send_sems,
    recv_sems,
):
    place = Place()
    copies = Copies(place, send_sems, recv_sems)
    place.greet()

    def grad(z_step, x_step, core_step):
        return grad_ref.at[place.at((4 - z_step) % 4, x_step, core_step)]

    def modulation(kind, z_step, x_step):
        slot = all_ref.at[place.at(z_step, x_step, 0)]
        copies.send((kind, "modulation", z_step, x_step), slot, slot)

    copies.send(("y", "half"), half_ref.at[place.half(1)], pair_from_y)
    copies.send(("core", "vector"), vector_ref, vector_from.at[0])
    loads = {}
    for x_step in (1, 0):
        for z_step in (3, 2, 1, 0):
            copies.send(
                ("core", x_step, z_step),
                grad(z_step, x_step, 1),
                from_core.at[x_step, z_step],
            )
            load = pltpu.make_async_copy(
                grad(z_step, x_step, 0), own.at[x_step, z_step], local_sems.at[len(loads)]
            )
            load.start()
            loads[x_step, z_step] = load

    copies.receive(("core", "vector"))
    vector[0] = vector_ref[...] + vector_from[0]
    copies.send(("x", "vector"), vector.at[0], vector_from.at[1])
    pair[place.half(0)] = half_ref[place.half(0)]
    copies.receive(("y", "half"))
    pair[place.half(1)] = pair_from_y[...]
    all_ref[place.me] = pair[...].reshape(all_ref.shape[1:]).astype(HALF)
    modulation("x", 0, 0)
    modulation("z", 0, 0)
    modulation("core", 0, 0)

    def summed(x_step, z_step):
        loads[x_step, z_step].wait()
        copies.receive(("core", x_step, z_step))
        first = own[x_step, z_step].astype(FLOAT)
        return first + from_core[x_step, z_step].astype(FLOAT)

    def send_x(z_step):
        own[1, z_step] = summed(1, z_step).astype(HALF)
        copies.send(("x", z_step), own.at[1, z_step], from_x.at[z_step])

    def forward_modulation(z_step):
        for x_step in range(2):
            copies.receive(("z", "modulation", z_step - 1, x_step))
            if z_step < 3:
                modulation("z", z_step, x_step)
            modulation("core", z_step, x_step)

    def vector_ring(z_step):
        slot = vector_z.at[(place.z + 4 - z_step) % 4]
        copies.send(("z", "vector", z_step), slot, slot)

    send_x(3)
    copies.receive(("x", "vector"))
    vector[1] = vector[0] + vector_from[1]
    copies.send(("y", "vector"), vector.at[1], vector_from.at[2])
    copies.send(("y", "strip"), strip_ref, other_ref)
    copies.receive(("x", "modulation", 0, 0))
    modulation("z", 0, 1)
    modulation("core", 0, 1)
    send_x(2)
    copies.receive(("y", "vector"))
    vector_z[place.z] = vector[1] + vector_from[2]
    vector_ring(0)
    forward_modulation(1)
    send_x(1)
    copies.receive(("z", "vector", 0))
    vector_ring(1)
    forward_modulation(2)
    send_x(0)
    copies.receive(("z", "vector", 1))
    vector_ring(2)
    forward_modulation(3)
    for z_step in (3, 2, 1, 0):
        total = summed(0, z_step)
        copies.receive(("x", z_step))
        total = total + from_x[z_step].astype(FLOAT)
        if z_step < 3:
            copies.receive(("z", z_step + 1))
            total = total + from_z[z_step].astype(FLOAT)
        if z_step > 0:
            own[0, z_step] = total.astype(HALF)
            copies.send(("z", z_step), own.at[0, z_step], from_z.at[z_step - 1])
    cut = share_ref.shape[1]
    low, high = total[:, :cut], total[:, cut:]
    half_sum[...] = jnp.where(place.y == 0, high, low).astype(HALF)
    copies.send(("y",), half_sum, from_y)
    share_ref[...] = jnp.where(place.y == 0, low, high)
    copies.receive(("y",))
    share_ref[...] = share_ref[...] + from_y[...].astype(FLOAT)
    copies.receive(("z", "vector", 2))
    total_ref[...] = (vector_z[0] + vector_z[1]) + (vector_z[2] + vector_z[3])
    for z_step in range(4):
        for x_step in range(2):
            copies.receive(("core", "modulation", z_step, x_step))
    copies.receive(("y", "strip"))
    copies.finish()


def tail(grad, half, vector, strip):
    slot = grad.shape[1:]
    count = grad.shape[0]
    share = (slot[0], slot[1] // 2)
    images, columns = half.shape[1:]
    vmem = pl.BlockSpec(memory_space=pltpu.VMEM)
    anywhere = pl.BlockSpec(memory_space=pl.ANY)
    return pl.pallas_call(
        tail_kernel,
        out_shape=[
            jax.ShapeDtypeStruct(share, FLOAT),
            jax.ShapeDtypeStruct((count, 2 * images, columns), HALF),
            jax.ShapeDtypeStruct(vector.shape, FLOAT),
            jax.ShapeDtypeStruct(strip.shape, HALF),
        ],
        in_specs=[anywhere, vmem, vmem, anywhere],
        out_specs=[vmem, vmem, vmem, anywhere],
        scratch_shapes=[
            pltpu.VMEM((2, 4) + slot, HALF),
            pltpu.VMEM((2, 4) + slot, HALF),
            pltpu.VMEM((4,) + slot, HALF),
            pltpu.VMEM((3,) + slot, HALF),
            pltpu.VMEM(share, HALF),
            pltpu.VMEM(share, HALF),
            pltpu.VMEM(half.shape, FLOAT),
            pltpu.VMEM(half.shape[1:], FLOAT),
            pltpu.VMEM((2,) + vector.shape, FLOAT),
            pltpu.VMEM((3,) + vector.shape, FLOAT),
            pltpu.VMEM((4,) + vector.shape, FLOAT),
            pltpu.SemaphoreType.DMA((8,)),
            pltpu.SemaphoreType.DMA((64,)),
            pltpu.SemaphoreType.DMA((64,)),
        ],
        compiler_params=pltpu.CompilerParams(
            collective_id=2, has_side_effects=True, vmem_limit_bytes=48 * 2**20
        ),
        cost_estimate=pl.CostEstimate(flops=0, bytes_accessed=200 * 2**20, transcendentals=0),
        name="tail",
    )(grad, half, vector, strip)


def swap_blk(value):
    return lax.ppermute(value, "blk", [(0, 1), (1, 0)])


def share_columns(total, me_blk):
    half = total.shape[1] // 2
    keep = lax.dynamic_slice_in_dim(total, me_blk * half, half, 1)
    send = lax.dynamic_slice_in_dim(total, (1 - me_blk) * half, half, 1)
    return keep.astype(FLOAT) + swap_blk(send).astype(FLOAT)


def order_blk(first, mine, other, axis):
    return jnp.concatenate(
        [jnp.where(first, mine, other), jnp.where(first, other, mine)], axis=axis
    )


def pair_body(
    tokens,
    cotangent,
    condition,
    lengths,
    adaptive_weight,
    joint_weight,
    output_weight,
    up_weight,
    down_weight,
    adaptive_bias,
    query_bias,
    value_bias,
    output_bias,
    up_bias,
    down_bias,
):
    me_dp, me_blk = lax.axis_index("dp"), lax.axis_index("blk")
    first = me_blk == 0
    strip_rows, width = tokens.shape[2:]
    rows = 2 * strip_rows
    parts = strip_rows // 128
    images = lengths.shape[2]

    def mine_of(pair):
        return lax.dynamic_index_in_dim(pair, me_blk, 0, keepdims=False)

    def other_of(pair):
        return lax.dynamic_index_in_dim(pair, 1 - me_blk, 0, keepdims=False)

    joint, output_matrix, modulation, act_part, tokens_other = head(
        joint_weight, output_weight, condition[0], adaptive_weight, adaptive_bias, tokens[0]
    )
    modulation = jnp.concatenate([modulation[0], modulation[1]], axis=1)

    bias_mine = jnp.concatenate([query_bias, value_bias, output_bias, down_bias, up_bias])
    bias_other = swap_blk(bias_mine)
    small = width // 2

    def bias_of(begin, size):
        return order_blk(
            first, bias_mine[begin : begin + size], bias_other[begin : begin + size], 0
        ).astype(FLOAT)

    query_vector, value_vector = bias_of(0, small), bias_of(small, small)
    output_vector, down_vector = bias_of(2 * small, small), bias_of(3 * small, small)
    up_vector = bias_of(4 * small, up_bias.shape[0])

    joint, up_weight, down_weight = lax.optimization_barrier((joint, up_weight, down_weight))
    up_halves = lax.all_gather(up_weight, ("blk", "dp"), axis=0, tiled=True)
    up_halves = up_halves.reshape(2, width, -1)
    down_other = swap_blk(down_weight)
    cotangent_other = swap_blk(other_of(cotangent[0]))

    strip = mine_of(lengths[0]) // 2
    ends = jnp.cumsum(strip)
    starts = ends - strip
    begin = jnp.arange(parts, dtype=jnp.int32)[:, None] * 128
    inside = (begin >= starts[None, :]) & (begin < ends[None, :])
    member = jnp.tile(inside.astype(FLOAT), (2, 1))
    long = strip == 512
    used = strip > 0
    rank = jnp.where(
        long,
        jnp.cumsum(long) - 1,
        jnp.where(used, jnp.sum(long) + jnp.cumsum(used & ~long) - 1, images + 8),
    )
    info = jnp.sum(
        jnp.where(rank[:, None] == jnp.arange(8)[None, :], starts[:, None], 0), axis=0
    )
    kinds = jnp.where(jnp.arange(8) < jnp.sum(long), 1, 0)
    info = jnp.concatenate([info, kinds]).astype(jnp.int32)

    per_part = jnp.dot(member, modulation, precision=HIGHEST, preferred_element_type=FLOAT)
    per_part = per_part.reshape(2 * parts, 1, 6, width)
    shift_one, scale_one, gate_one, shift_two, scale_two, gate_two = (
        per_part[:, :, index] for index in range(6)
    )

    inputs = jnp.concatenate([mine_of(tokens[0]), tokens_other], axis=0)
    joint_vector = jnp.concatenate([query_vector, jnp.zeros_like(query_vector), value_vector])
    hidden_one, query, keys, values = project_call(
        inputs, shift_one, scale_one, joint, joint_vector[None]
    )
    query, down_weight = lax.optimization_barrier((query, down_weight))
    down_rows = order_blk(first, down_weight, down_other, 1)
    down_matrix = lax.all_gather(down_rows, "dp", axis=0, tiled=True)
    attended, total = attend_pack(info, query, keys, values)
    branch_one, hidden_two = mix_call(
        attended, inputs, gate_one, shift_two, scale_two, output_matrix, output_vector[None]
    )
    activated, slope = up_call(hidden_two, up_halves, up_vector[None])

    upstream, d_branch_two = join_call(cotangent[0], cotangent_other, gate_two, me_blk)
    d_branch_two, down_grad = lax.optimization_barrier(
        (d_branch_two, left_outer(activated, d_branch_two).astype(HALF))
    )
    down_total = lax.psum_scatter(down_grad, "dp", scatter_dimension=0, tiled=True)
    d_pre, down_sum, up_sum = down_grad_call(d_branch_two, slope, down_matrix)
    d_pre, up_grad = lax.optimization_barrier(
        (d_pre, left_outer(hidden_two, d_pre).astype(HALF))
    )
    up_total = lax.psum_scatter(up_grad, "dp", scatter_dimension=0, tiled=True)
    result, result_send, d_gate_two = finish_call(
        activated,
        inputs,
        branch_one,
        upstream,
        gate_one,
        gate_two,
        down_matrix,
        down_vector[None],
        me_blk,
    )
    d_pre, result_send = lax.optimization_barrier((d_pre, result_send))
    result_other = swap_blk(result_send)
    d_middle, d_branch_one, d_attended, delta, *part_totals = (
        mix_grad_call(
            d_pre, attended, inputs, branch_one, upstream, gate_one, scale_two, up_halves, output_matrix
        )
    )
    d_shift_two, d_scale_two, d_gate_one, output_sum = part_totals
    d_attended, output_grad, down_total = lax.optimization_barrier(
        (d_attended, left_outer(attended, d_branch_one).astype(HALF), down_total)
    )
    output_total = lax.psum_scatter(output_grad, "dp", scatter_dimension=0, tiled=True)
    down_share = share_columns(down_total, me_blk)
    d_query, d_keys, d_values = attend_pack_backward(
        info, query, keys, values, d_attended, total, delta
    )
    d_query, up_total, result_other = lax.optimization_barrier((d_query, up_total, result_other))
    up_share = share_columns(up_total, me_blk)
    result = fill_call(result, result_other, me_blk)
    d_projected = jnp.concatenate([d_query, d_keys, d_values], axis=1)
    joint_grad = left_outer(hidden_one, d_projected).astype(HALF)
    d_inputs, d_inputs_send, d_shift_one, d_scale_one, query_sum, value_sum = project_grad_call(
        d_query, d_keys, d_values, inputs, d_middle, scale_one, joint, me_blk
    )

    def part_rows(value):
        return value.reshape(2 * parts, width)

    d_parts = [d_shift_one, d_scale_one, d_gate_one, d_shift_two, d_scale_two, d_gate_two]
    d_parts = jnp.concatenate([part_rows(value) for value in d_parts], axis=1)
    d_modulation = lax.dot_general(
        member,
        d_parts,
        (((0,), (0,)), ((), ())),
        precision=HIGHEST,
        preferred_element_type=FLOAT,
    )
    vectors = [query_sum, value_sum, output_sum, down_sum, up_sum]
    sums = jnp.concatenate([jnp.sum(value, axis=(0, 1)) for value in vectors])
    joint_grad, output_total = lax.optimization_barrier((joint_grad, output_total))
    output_share = share_columns(output_total, me_blk)
    shard_rows = adaptive_weight.shape[0]
    joint_share, d_mod_all, sums, d_inputs_other = tail(
        joint_grad.reshape(16, shard_rows, -1),
        d_modulation.reshape(images, 2, -1).transpose(1, 0, 2),
        sums.reshape(-1, 128),
        d_inputs_send,
    )
    d_inputs = fill_call(d_inputs, d_inputs_other, me_blk)
    sums = sums.reshape(-1)
    d_mod_all = d_mod_all.reshape(-1, d_mod_all.shape[2])
    adaptive_share = left_outer(act_part.reshape(-1, shard_rows), d_mod_all)
    adaptive_vector_share = jnp.sum(d_mod_all.astype(FLOAT), axis=0)
    d_act = right_outer(d_mod_all, adaptive_weight)
    d_act = d_act.reshape(16, 2 * images, shard_rows)
    d_act = lax.all_to_all(d_act, "dp", 0, 0)
    d_act = d_act + swap_blk(d_act)
    d_act = d_act.transpose(1, 0, 2).reshape(2, images, width)
    condition_full = condition[0].astype(FLOAT)
    sigmoid_cond = jax.nn.sigmoid(condition_full)
    d_condition = d_act * sigmoid_cond * (1.0 + condition_full * (1.0 - sigmoid_cond))

    def share_of(begin, size):
        return lax.dynamic_slice_in_dim(sums, begin + me_blk * (size // 2), size // 2, 0)

    return (
        result[None],
        d_inputs[None],
        d_condition[None],
        adaptive_share,
        joint_share,
        output_share,
        up_share,
        down_share,
        adaptive_vector_share,
        share_of(0, width),
        share_of(width, width),
        share_of(2 * width, width),
        share_of(4 * width, 2 * up_bias.shape[0]),
        share_of(3 * width, width),
    )


def solution(mesh):
    in_specs = (
        P("dp", None, "blk", None),
        P("dp", None, "blk", None),
        P("dp", None, None, None),
        P("dp", None, None),
        P("dp", "blk"),
        P("dp", "blk"),
        P("dp", "blk"),
        P("dp", "blk"),
        P("dp", "blk"),
        P("blk"),
        P("blk"),
        P("blk"),
        P("blk"),
        P("blk"),
        P("blk"),
    )
    out_specs = (
        P("dp", None, "blk", None),
        P("dp", None, "blk", None),
        P("dp", None, None, None),
        P("dp", "blk"),
        P("dp", "blk"),
        P("dp", "blk"),
        P("dp", "blk"),
        P("dp", "blk"),
        P("blk"),
        P("blk"),
        P("blk"),
        P("blk"),
        P("blk"),
        P("blk"),
    )
    paired = mesh.shape["dp"] == 16 and mesh.shape["blk"] == 2
    body = pair_body if paired else general_body
    return jax.shard_map(body, mesh=mesh, in_specs=in_specs, out_specs=out_specs, check_vma=False)
```

```python
import functools

import jax
import jax.numpy as jnp
from jax import lax
from jax.experimental import pallas as pl
from jax.experimental.pallas import tpu as pltpu
from jax.sharding import PartitionSpec as P

HEADS = 16


EPSILON = 1e-06
GELU_SCALE = 0.7978845608028654
HIGHEST = lax.Precision.HIGHEST
FLOAT = jnp.float32
HALF = jnp.bfloat16


def matmul(left, right):
    return jnp.dot(left, right, preferred_element_type=FLOAT)


def left_outer(left, right):
    return lax.dot_general(left, right, (((0,), (0,)), ((), ())), preferred_element_type=FLOAT)


def right_outer(left, right):
    return lax.dot_general(left, right, (((1,), (1,)), ((), ())), preferred_element_type=FLOAT)


def normalize(values):
    center = values - jnp.mean(values, axis=-1, keepdims=True)
    inverse = lax.rsqrt(jnp.mean(center * center, axis=-1, keepdims=True) + EPSILON)
    return (center * inverse, inverse)


def norm_backward(normed, inverse, grad):
    mean_grad = jnp.mean(grad, axis=-1, keepdims=True)
    mean_cross = jnp.mean(grad * normed, axis=-1, keepdims=True)
    return inverse * (grad - mean_grad - normed * mean_cross)


def gelu_tanh(values):
    return (
        0.5 * values * (1.0 + jnp.tanh(GELU_SCALE * (values + 0.044715 * values * values * values)))
    )


def gelu_slope(values):
    bend = jnp.tanh(GELU_SCALE * (values + 0.044715 * values * values * values))
    return 0.5 * (1.0 + bend) + 0.5 * values * (1.0 - bend * bend) * GELU_SCALE * (
        1.0 + 3.0 * 0.044715 * values * values
    )


def block_size():
    return 512


def block_scores(query_heads, key_part, query_slots, slot_part, scale):
    scores = jnp.einsum("qhd,khd->hqk", query_heads, key_part, preferred_element_type=FLOAT) * scale
    allowed = query_slots[:, None] == slot_part[None, :]
    return jnp.where(allowed[None], scores, -1e30)


def split_blocks(key_all, value_all, key_slots):
    total, width = key_all.shape
    size = block_size()
    count = total // size
    shape = (count, size, HEADS, width // HEADS)
    return (key_all.reshape(shape), value_all.reshape(shape), key_slots.reshape(count, size))


def attend_forward(query, key_all, value_all, query_slots, key_slots, scale):
    rows, width = query.shape
    query_heads = query.reshape(rows, HEADS, width // HEADS)
    key_blocks, value_blocks, slot_blocks = split_blocks(key_all, value_all, key_slots)

    def statistics(carry, item):
        top, mass = carry
        key_part, slot_part = item
        scores = block_scores(query_heads, key_part, query_slots, slot_part, scale)
        new_top = jnp.maximum(top, jnp.max(scores, axis=-1))
        mass = mass * jnp.exp(top - new_top) + jnp.sum(
            jnp.exp(scores - new_top[..., None]), axis=-1
        )
        return ((new_top, mass), None)

    start = (jnp.full((HEADS, rows), -1e30, FLOAT), jnp.zeros((HEADS, rows), FLOAT))
    (top, mass), unused = lax.scan(statistics, start, (key_blocks, slot_blocks))
    log_total = top + jnp.log(mass)

    def accumulate(running, item):
        key_part, value_part, slot_part = item
        scores = block_scores(query_heads, key_part, query_slots, slot_part, scale)
        weights = jnp.exp(scores - log_total[..., None]).astype(HALF)
        return (
            running + jnp.einsum("hqk,khd->qhd", weights, value_part, preferred_element_type=FLOAT),
            None,
        )

    empty = jnp.zeros((rows, HEADS, width // HEADS), FLOAT)
    attended, unused = lax.scan(accumulate, empty, (key_blocks, value_blocks, slot_blocks))
    return (log_total, attended.reshape(rows, width))


def attention_delta(d_attended, attended):
    rows, width = attended.shape
    grad_heads = d_attended.reshape(rows, HEADS, width // HEADS).astype(FLOAT)
    return jnp.einsum("qhd,qhd->hq", grad_heads, attended.reshape(rows, HEADS, width // HEADS))


def attend_backward(
    query, key_all, value_all, query_slots, key_slots, log_total, delta, d_attended, scale
):
    rows, width = query.shape
    total = key_all.shape[0]
    query_heads = query.reshape(rows, HEADS, width // HEADS)
    grad_heads = d_attended.reshape(rows, HEADS, width // HEADS)
    key_blocks, value_blocks, slot_blocks = split_blocks(key_all, value_all, key_slots)

    def one_block(d_query, item):
        key_part, value_part, slot_part = item
        scores = block_scores(query_heads, key_part, query_slots, slot_part, scale)
        weights = jnp.exp(scores - log_total[..., None])
        d_weights = jnp.einsum("qhd,khd->hqk", grad_heads, value_part, preferred_element_type=FLOAT)
        d_scores = (weights * (d_weights - delta[..., None])).astype(HALF)
        d_query = (
            d_query
            + jnp.einsum("hqk,khd->qhd", d_scores, key_part, preferred_element_type=FLOAT) * scale
        )
        d_value_part = jnp.einsum(
            "hqk,qhd->khd", weights.astype(HALF), grad_heads, preferred_element_type=FLOAT
        )
        d_key_part = (
            jnp.einsum("hqk,qhd->khd", d_scores, query_heads, preferred_element_type=FLOAT) * scale
        )
        return (d_query, (d_key_part, d_value_part))

    empty = jnp.zeros((rows, HEADS, width // HEADS), FLOAT)
    d_query, key_parts = lax.scan(one_block, empty, (key_blocks, value_blocks, slot_blocks))
    d_keys, d_values = key_parts
    return (
        d_query.reshape(rows, width),
        d_keys.reshape(total, width),
        d_values.reshape(total, width),
    )


def run_pack(full, tokens_in, cotangent_in, condition_in, lengths_in, blocks, first_block):
    (
        adaptive_matrix,
        joint_matrix,
        output_matrix,
        up_matrix,
        down_matrix,
        adaptive_vector,
        query_vector,
        value_vector,
        output_vector,
        up_vector,
        down_vector,
    ) = full
    rows, width = tokens_in.shape
    scale = (width // HEADS) ** (-0.5)
    inputs = tokens_in.astype(FLOAT)
    strip = lengths_in // blocks
    ends = jnp.cumsum(strip)
    starts = ends - strip
    place = jnp.arange(rows, dtype=jnp.int32)[:, None]
    inside = (place >= starts[None, :]) & (place < ends[None, :])
    member = inside.astype(FLOAT)
    slot_ids = jnp.sum(
        inside.astype(jnp.int32) * jnp.arange(strip.shape[0], dtype=jnp.int32)[None, :], axis=1
    )
    key_slots = jnp.tile(slot_ids, blocks)
    condition_full = condition_in.astype(FLOAT)
    cond_act = jax.nn.silu(condition_full).astype(HALF)
    modulation = matmul(cond_act, adaptive_matrix) + adaptive_vector.astype(FLOAT)
    per_token = jnp.dot(member, modulation, precision=HIGHEST, preferred_element_type=FLOAT)
    shift_one, scale_one, gate_one, shift_two, scale_two, gate_two = jnp.split(per_token, 6, axis=1)
    normed_one, inverse_one = normalize(inputs)
    hidden_one = (normed_one * (1.0 + scale_one) + shift_one).astype(HALF)
    projected = matmul(hidden_one, joint_matrix)
    query = (projected[:, :width] + query_vector.astype(FLOAT)).astype(HALF)
    keys = projected[:, width : 2 * width].astype(HALF)
    values = (projected[:, 2 * width :] + value_vector.astype(FLOAT)).astype(HALF)
    key_all, value_all = (
        lax.all_gather(keys, "blk", axis=0, tiled=True),
        lax.all_gather(values, "blk", axis=0, tiled=True),
    )
    log_total, attended = attend_forward(query, key_all, value_all, slot_ids, key_slots, scale)
    attended_half = attended.astype(HALF)
    branch_one = matmul(attended_half, output_matrix) + output_vector.astype(FLOAT)
    middle = inputs + gate_one * branch_one
    normed_two, inverse_two = normalize(middle)
    hidden_two = (normed_two * (1.0 + scale_two) + shift_two).astype(HALF)
    pre_act = matmul(hidden_two, up_matrix) + up_vector.astype(FLOAT)
    activated = gelu_tanh(pre_act).astype(HALF)
    branch_two = matmul(activated, down_matrix) + down_vector.astype(FLOAT)
    result = middle + gate_two * branch_two
    upstream = cotangent_in.astype(FLOAT)
    d_gate_two = upstream * branch_two
    d_branch_two = (upstream * gate_two).astype(HALF)
    d_pre = (right_outer(d_branch_two, down_matrix) * gelu_slope(pre_act)).astype(HALF)
    d_hidden_two = right_outer(d_pre, up_matrix)
    d_scale_two = d_hidden_two * normed_two
    d_middle = upstream + norm_backward(normed_two, inverse_two, d_hidden_two * (1.0 + scale_two))
    d_gate_one = d_middle * branch_one
    d_branch_one = (d_middle * gate_one).astype(HALF)
    d_attended = right_outer(d_branch_one, output_matrix).astype(HALF)
    delta = attention_delta(d_attended, attended)
    d_query_full, d_key_all, d_value_all = attend_backward(
        query, key_all, value_all, slot_ids, key_slots, log_total, delta, d_attended, scale
    )
    d_key_full, d_value_full = (
        lax.psum_scatter(
            d_key_all.astype(jnp.bfloat16), "blk", scatter_dimension=0, tiled=True
        ).astype(jnp.float32),
        lax.psum_scatter(
            d_value_all.astype(jnp.bfloat16), "blk", scatter_dimension=0, tiled=True
        ).astype(jnp.float32),
    )
    d_query = d_query_full.astype(HALF)
    d_keys = d_key_full.astype(HALF)
    d_values = d_value_full.astype(HALF)
    d_projected = jnp.concatenate([d_query, d_keys, d_values], axis=1)
    d_hidden_one = right_outer(d_projected, joint_matrix)
    d_scale_one = d_hidden_one * normed_one
    d_inputs = d_middle + norm_backward(normed_one, inverse_one, d_hidden_one * (1.0 + scale_one))
    d_per_token = jnp.concatenate(
        [d_hidden_one, d_scale_one, d_gate_one, d_hidden_two, d_scale_two, d_gate_two], axis=1
    )
    d_mod_local = lax.dot_general(
        member,
        d_per_token,
        (((0,), (0,)), ((), ())),
        precision=HIGHEST,
        preferred_element_type=FLOAT,
    )
    d_modulation = lax.psum(d_mod_local.astype(jnp.bfloat16), "blk").astype(jnp.float32)
    sigmoid_cond = jax.nn.sigmoid(condition_full)
    adaptive_float = adaptive_matrix.astype(FLOAT)
    d_condition = (
        lax.dot_general(
            d_modulation,
            adaptive_float,
            (((1,), (1,)), ((), ())),
            precision=HIGHEST,
            preferred_element_type=FLOAT,
        )
        * sigmoid_cond
        * (1.0 + condition_full * (1.0 - sigmoid_cond))
    )
    adaptive_grad = lax.dot_general(
        cond_act.astype(FLOAT),
        d_modulation,
        (((0,), (0,)), ((), ())),
        precision=HIGHEST,
        preferred_element_type=FLOAT,
    )
    local = (
        adaptive_grad * first_block,
        left_outer(hidden_one, d_projected),
        left_outer(attended_half, d_branch_one),
        left_outer(hidden_two, d_pre),
        left_outer(activated, d_branch_two),
        jnp.sum(d_modulation, axis=0) * first_block,
        jnp.sum(d_query.astype(FLOAT), axis=0),
        jnp.sum(d_values.astype(FLOAT), axis=0),
        jnp.sum(d_branch_one.astype(FLOAT), axis=0),
        jnp.sum(d_pre.astype(FLOAT), axis=0),
        jnp.sum(d_branch_two.astype(FLOAT), axis=0),
    )
    return (result, d_inputs, d_condition, local)


def general_body(
    tokens,
    cotangent,
    condition,
    lengths,
    adaptive_weight,
    joint_weight,
    output_weight,
    up_weight,
    down_weight,
    adaptive_bias,
    query_bias,
    value_bias,
    output_bias,
    up_bias,
    down_bias,
):
    micro = tokens.shape[1]
    blocks = lax.axis_size("blk")
    first_block = jnp.where(lax.axis_index("blk") == 0, 1.0, 0.0).astype(FLOAT)
    results = []
    token_grads = []
    condition_grads = []
    sums = None
    for step in range(micro):
        columns = (
            lax.all_gather(adaptive_weight, "blk", axis=1, tiled=True),
            lax.all_gather(joint_weight, "blk", axis=1, tiled=True),
            lax.all_gather(output_weight, "blk", axis=1, tiled=True),
            lax.all_gather(up_weight, "blk", axis=1, tiled=True),
            lax.all_gather(down_weight, "blk", axis=1, tiled=True),
            lax.all_gather(adaptive_bias, "blk", axis=0, tiled=True),
            lax.all_gather(query_bias, "blk", axis=0, tiled=True),
            lax.all_gather(value_bias, "blk", axis=0, tiled=True),
            lax.all_gather(output_bias, "blk", axis=0, tiled=True),
            lax.all_gather(up_bias, "blk", axis=0, tiled=True),
            lax.all_gather(down_bias, "blk", axis=0, tiled=True),
        )
        whole = (
            lax.all_gather(columns[0], "dp", axis=0, tiled=True),
            lax.all_gather(columns[1], "dp", axis=0, tiled=True),
            lax.all_gather(columns[2], "dp", axis=0, tiled=True),
            lax.all_gather(columns[3], "dp", axis=0, tiled=True),
            lax.all_gather(columns[4], "dp", axis=0, tiled=True),
        )
        full = tuple(whole) + tuple(columns[5:])
        result, d_inputs, d_condition, local = run_pack(
            full,
            tokens[0, step],
            cotangent[0, step],
            condition[0, step],
            lengths[0, step],
            blocks,
            first_block,
        )
        results.append(result)
        token_grads.append(d_inputs)
        condition_grads.append(d_condition)
        shares = (
            lax.psum_scatter(
                lax.psum_scatter(
                    local[0].astype(jnp.bfloat16), "dp", scatter_dimension=0, tiled=True
                ),
                "blk",
                scatter_dimension=1,
                tiled=True,
            ).astype(jnp.float32),
            lax.psum_scatter(
                lax.psum_scatter(
                    local[1].astype(jnp.bfloat16), "dp", scatter_dimension=0, tiled=True
                ),
                "blk",
                scatter_dimension=1,
                tiled=True,
            ).astype(jnp.float32),
            lax.psum_scatter(
                lax.psum_scatter(
                    local[2].astype(jnp.bfloat16), "dp", scatter_dimension=0, tiled=True
                ),
                "blk",
                scatter_dimension=1,
                tiled=True,
            ).astype(jnp.float32),
            lax.psum_scatter(
                lax.psum_scatter(
                    local[3].astype(jnp.bfloat16), "dp", scatter_dimension=0, tiled=True
                ),
                "blk",
                scatter_dimension=1,
                tiled=True,
            ).astype(jnp.float32),
            lax.psum_scatter(
                lax.psum_scatter(
                    local[4].astype(jnp.bfloat16), "dp", scatter_dimension=0, tiled=True
                ),
                "blk",
                scatter_dimension=1,
                tiled=True,
            ).astype(jnp.float32),
            lax.psum_scatter(
                lax.psum(local[5].astype(jnp.bfloat16), "dp"),
                "blk",
                scatter_dimension=0,
                tiled=True,
            ).astype(jnp.float32),
            lax.psum_scatter(
                lax.psum(local[6].astype(jnp.bfloat16), "dp"),
                "blk",
                scatter_dimension=0,
                tiled=True,
            ).astype(jnp.float32),
            lax.psum_scatter(
                lax.psum(local[7].astype(jnp.bfloat16), "dp"),
                "blk",
                scatter_dimension=0,
                tiled=True,
            ).astype(jnp.float32),
            lax.psum_scatter(
                lax.psum(local[8].astype(jnp.bfloat16), "dp"),
                "blk",
                scatter_dimension=0,
                tiled=True,
            ).astype(jnp.float32),
            lax.psum_scatter(
                lax.psum(local[9].astype(jnp.bfloat16), "dp"),
                "blk",
                scatter_dimension=0,
                tiled=True,
            ).astype(jnp.float32),
            lax.psum_scatter(
                lax.psum(local[10].astype(jnp.bfloat16), "dp"),
                "blk",
                scatter_dimension=0,
                tiled=True,
            ).astype(jnp.float32),
        )
        sums = (
            shares
            if sums is None
            else tuple((first + second for first, second in zip(sums, shares)))
        )
    block_output = jnp.stack(results, axis=0)[None]
    tokens_grad = jnp.stack(token_grads, axis=0)[None]
    condition_grad = jnp.stack(condition_grads, axis=0)[None]
    return (
        block_output,
        tokens_grad,
        condition_grad,
        sums[0],
        sums[1],
        sums[2],
        sums[3],
        sums[4],
        sums[5],
        sums[6],
        sums[7],
        sums[8],
        sums[9],
        sums[10],
    )


HEAD = 72
EXPONENT = HEAD**-0.5 * 1.4426950408889634


WINDOW = 256


def head_window(head, width):
    start = jnp.minimum(lax.div(head * HEAD, 128) * 128, width - WINDOW)
    return pl.ds(pl.multiple_of(start, 128), WINDOW), head * HEAD - start


def head_windows(group):
    heads = []
    for pair in range(group // 2):
        pair = pl.program_id(1) * (group // 2) + pair
        late = jnp.where(pair >= HEADS // 4, 1, 0)
        for head, size in ((2 * pair + late, 128), (2 * pair + 1 - late, 256)):
            start = lax.div(head * HEAD, 128) * 128
            heads.append((head, pl.ds(pl.multiple_of(start, 128), size), head * HEAD - start, size))
    return heads


def head_lanes(offset, rows, size):
    lane = lax.broadcasted_iota(jnp.int32, (rows, size), 1)
    return (lane >= offset) & (lane < offset + HEAD)


def for_images(info, unit, image):
    @pl.when(info[8 + unit] == 1)
    def _():
        image(info[unit], 512, 256)

    @pl.when(info[8 + unit] == 0)
    def _():
        def step(index, carry):
            image(info[unit + index], 128, 128)
            return carry

        lax.fori_loop(0, 4, step, 0)


def image_rows(start, strip, half, index, block):
    place = index * block
    place = start + (place if place < strip else half + place - strip)
    return pl.ds(pl.multiple_of(place, 128), block)


def both_strips(ref, start, strip, half, window):
    return jnp.concatenate(
        [ref[pl.ds(start, strip), window], ref[pl.ds(half + start, strip), window]], axis=0
    )


def attend_forward_kernel(info, q_ref, k_ref, v_ref, o_ref, total_ref, *, group):
    half, width = q_ref.shape[0] // 2, q_ref.shape[1]

    def image(start, strip, block):
        start = pl.multiple_of(start, 128)
        work = []
        for member in range(group):
            head = pl.program_id(1) * group + member
            window, offset = head_window(head, width)
            keys = both_strips(k_ref, start, strip, half, window)
            keys = jnp.where(head_lanes(offset, 2 * strip, WINDOW), keys, jnp.zeros_like(keys))
            values = both_strips(v_ref, start, strip, half, window).T
            for index in range(2 * strip // block):
                rows = image_rows(start, strip, half, index, block)
                work.append((head, window, offset, keys, values, rows))

        def scores_of(item):
            return right_outer(item[3], q_ref[item[5], item[1]])

        coming = scores_of(work[0])
        for index, item in enumerate(work):
            head, window, offset, keys, values, rows = item
            scores = coming
            if index + 1 < len(work):
                coming = scores_of(work[index + 1])
            top = jnp.max(scores, axis=0, keepdims=True)
            expo = jnp.exp2((scores - top) * EXPONENT)
            mass = jnp.sum(expo, axis=0, keepdims=True)
            out = (matmul(values, expo.astype(HALF)) * (1.0 / mass)).T.astype(HALF)
            o_ref[rows, window] = jnp.where(head_lanes(offset, block, WINDOW), out, o_ref[rows, window])
            total_ref[head, :, rows] = top * EXPONENT + jnp.log2(mass)

    for_images(info, pl.program_id(0), image)


def attend_backward_kernel(
    info, q_ref, k_ref, v_ref, do_ref, total_ref, delta_ref, dq_ref, dk_ref, dv_ref, *, group
):
    half = q_ref.shape[0] // 2
    scale = HEAD**-0.5

    def image(start, strip, block):
        start = pl.multiple_of(start, 128)
        count = 2 * strip // block
        work = []
        for head, window, offset, size in head_windows(group):
            keys = both_strips(k_ref, start, strip, half, window)
            values = both_strips(v_ref, start, strip, half, window)
            inside = head_lanes(offset, 2 * strip, size)
            head_keys = jnp.where(inside, keys, jnp.zeros_like(keys))
            head_values = jnp.where(inside, values, jnp.zeros_like(values))
            turned = keys.T
            lanes = head_lanes(offset, block, size)
            for index in range(count):
                rows = image_rows(start, strip, half, index, block)
                work.append((head, window, lanes, head_keys, head_values, turned, rows))

        def begin(item):
            head, window, lanes, keys, values, turned, rows = item
            return (
                right_outer(keys, q_ref[rows, window]),
                right_outer(values, do_ref[rows, window]),
            )

        def middle(item, scores, d_weights):
            head, rows = item[0], item[6]
            weights = jnp.exp2(scores * EXPONENT - total_ref[head, :, rows])
            d_scores = weights * (d_weights - delta_ref[head, :, rows])
            return weights.astype(HALF), d_scores.astype(HALF)

        kept = []

        def finish(item, weights, d_scores):
            head, window, lanes, keys, values, turned, rows = item
            d_query = (matmul(turned, d_scores).T * scale).astype(HALF)
            dq_ref[rows, window] = jnp.where(lanes, d_query, dq_ref[rows, window])
            kept.append((weights, d_scores))
            if len(kept) < count:
                return
            weights = jnp.concatenate([part for part, _ in kept], axis=1)
            d_scores = jnp.concatenate([part for _, part in kept], axis=1)
            kept.clear()
            d_keys = matmul(d_scores, both_strips(q_ref, start, strip, half, window))
            d_values = matmul(weights, both_strips(do_ref, start, strip, half, window))
            for ref, value in (
                (dk_ref, (d_keys * scale).astype(HALF)),
                (dv_ref, d_values.astype(HALF)),
            ):
                for index in range(count):
                    rows = image_rows(start, strip, half, index, block)
                    part = value[index * block : (index + 1) * block]
                    ref[rows, window] = jnp.where(lanes, part, ref[rows, window])

        coming = begin(work[0])
        late = None
        for index, item in enumerate(work):
            now = coming
            if index + 1 < len(work):
                coming = begin(work[index + 1])
            if late is not None:
                finish(*late)
            late = (item,) + middle(item, *now)
        finish(*late)

    for_images(info, pl.program_id(0), image)


def attention_call(kernel, name, info, arrays, outputs, group, flops):
    def whole(array):
        return pl.BlockSpec(
            array.shape,
            lambda unit, head, info: (0,) * len(array.shape),
            pipeline_mode=pl.Buffered(1),
        )

    return pl.pallas_call(
        functools.partial(kernel, group=group),
        grid_spec=pltpu.PrefetchScalarGridSpec(
            num_scalar_prefetch=1,
            grid=(2, HEADS // group),
            in_specs=[whole(array) for array in arrays],
            out_specs=[whole(array) for array in outputs],
        ),
        out_shape=outputs,
        compiler_params=pltpu.CompilerParams(vmem_limit_bytes=60 * 2**20),
        cost_estimate=pl.CostEstimate(
            flops=flops, bytes_accessed=30 * 2**20, transcendentals=HEADS * 2**21
        ),
        name=name,
    )(info, *arrays)


def attend_pack(info, query, keys, values):
    rows, width = query.shape
    outputs = [
        jax.ShapeDtypeStruct((rows, width), HALF),
        jax.ShapeDtypeStruct((HEADS, 1, rows), FLOAT),
    ]
    return attention_call(
        attend_forward_kernel, "attend", info, [query, keys, values], outputs, 4, 70 * 10**9
    )


def attend_pack_backward(info, query, keys, values, grad, total, delta):
    outputs = [jax.ShapeDtypeStruct(query.shape, HALF)] * 3
    arrays = [query, keys, values, grad, total, delta]
    return attention_call(
        attend_backward_kernel, "attend_backward", info, arrays, outputs, 4, 140 * 10**9
    )


BLOCK = 256
PART = 128
STRIP = 32


def resident(array):
    return pl.BlockSpec(
        array.shape, lambda *step: (0,) * len(array.shape), pipeline_mode=pl.Buffered(1)
    )


def by_rows(array):
    size = BLOCK if len(array.shape) == 2 else BLOCK // PART
    zeros = (0,) * (len(array.shape) - 1)
    return pl.BlockSpec((size,) + array.shape[1:], lambda step, *scalars: (step,) + zeros)


def dense_call(kernel, name, rows, inputs, outputs, scratch=(), flops=0, strip=None):
    size = sum(array.size * array.dtype.itemsize for array, _ in inputs + outputs)
    scalars = [] if strip is None else [strip.reshape(1).astype(jnp.int32)]

    def run(*refs):
        kernel(*refs[len(scalars) :])

    return pl.pallas_call(
        run,
        grid_spec=pltpu.PrefetchScalarGridSpec(
            num_scalar_prefetch=len(scalars),
            grid=(rows // BLOCK,),
            in_specs=[spec for _, spec in inputs],
            out_specs=[spec for _, spec in outputs],
            scratch_shapes=list(scratch),
        ),
        out_shape=[shape for shape, _ in outputs],
        compiler_params=pltpu.CompilerParams(vmem_limit_bytes=60 * 2**20),
        cost_estimate=pl.CostEstimate(flops=flops, bytes_accessed=size, transcendentals=0),
        name=name,
    )(*scalars, *[array for array, _ in inputs])


def shape_of(*dims, kind=None):
    return jax.ShapeDtypeStruct(dims, kind or FLOAT)


def strips():
    return [
        (pl.ds(begin, STRIP), begin // PART, begin % PART == 0) for begin in range(0, BLOCK, STRIP)
    ]


def row_norm(values):
    center = values - jnp.mean(values, axis=1, keepdims=True)
    inverse = lax.rsqrt(jnp.mean(center * center, axis=1, keepdims=True) + EPSILON)
    return center * inverse, inverse


def fold(values):
    return jnp.sum(values.reshape(-1, 8, values.shape[1]), axis=0)


class Sums:
    def __init__(self):
        self.held = {}

    def add(self, ref, part, first, values):
        folded = fold(values)
        key = id(ref), part
        if not first:
            folded = self.held[key][1] + folded
        self.held[key] = (ref, folded)

    def store(self):
        for (_, part), (ref, value) in self.held.items():
            ref[part] = jnp.sum(value, axis=0, keepdims=True)


TILE_ROWS = 32
TILE_COLUMNS = 256


def tiles(rows, columns):
    return [
        (row, column)
        for row in range(0, rows, TILE_ROWS)
        for column in range(0, columns, TILE_COLUMNS)
    ]


def up_kernel(x_ref, w_ref, bias_ref, act_ref, slope_ref, *, chunk):
    x = x_ref[...]
    halves, _, columns = w_ref.shape
    work = [(half, begin) for half in range(halves) for begin in range(0, columns, chunk)]

    def product(item):
        return matmul(x, w_ref[item[0], :, pl.ds(item[1], chunk)])

    coming = product(work[0])
    for index, (half, begin) in enumerate(work):
        now = coming
        if index + 1 < len(work):
            coming = product(work[index + 1])
        for row, column in tiles(BLOCK, chunk):
            rows = pl.ds(row, TILE_ROWS)
            place = pl.ds(half * columns + begin + column, TILE_COLUMNS)
            value = now[row : row + TILE_ROWS, column : column + TILE_COLUMNS] + bias_ref[:, place]
            square = value * value
            gate = 0.5 + 0.5 * jnp.tanh(
                value * (GELU_SCALE + (GELU_SCALE * 0.044715) * square)
            )
            active = (value * gate).astype(HALF)
            gate, square = gate.astype(HALF), square.astype(HALF)
            bend = 2.0 * GELU_SCALE + (6.0 * GELU_SCALE * 0.044715) * square
            act_ref[rows, place] = active
            slope_ref[rows, place] = gate + active * (1.0 - gate) * bend


def up_call(hidden, weight, bias, chunk=768):
    rows, width = hidden.shape
    wide = 2 * weight.shape[2]
    out = shape_of(rows, wide, kind=HALF)
    return dense_call(
        functools.partial(up_kernel, chunk=chunk),
        "up",
        rows,
        [(hidden, by_rows(hidden)), (weight, resident(weight)), (bias, resident(bias))],
        [(out, by_rows(out)), (out, by_rows(out))],
        flops=2 * rows * width * wide,
    )


def down_grad_kernel(x_ref, slope_ref, w_ref, d_pre_ref, sum_ref, wide_ref, *, chunk):
    x = x_ref[...]
    sum_ref[0] = jnp.sum(fold(x.astype(FLOAT)), axis=0, keepdims=True)
    wide = w_ref.shape[0]
    work = list(range(0, wide, chunk))

    def product(begin):
        return right_outer(x, w_ref[pl.ds(begin, chunk), :])

    coming = product(work[0])
    for index, begin in enumerate(work):
        now = coming
        if index + 1 < len(work):
            coming = product(work[index + 1])
        for column in range(0, chunk, TILE_COLUMNS):
            place = pl.ds(begin + column, TILE_COLUMNS)
            total = None
            for row in range(0, BLOCK, TILE_ROWS):
                rows = pl.ds(row, TILE_ROWS)
                value = now[row : row + TILE_ROWS, column : column + TILE_COLUMNS]
                value = (value * slope_ref[rows, place].astype(FLOAT)).astype(HALF)
                d_pre_ref[rows, place] = value
                folded = fold(value.astype(FLOAT))
                total = folded if total is None else total + folded
            wide_ref[0, :, place] = jnp.sum(total, axis=0, keepdims=True)


def down_grad_call(d_branch, slope, weight, chunk=768):
    rows, width = d_branch.shape
    wide = weight.shape[0]
    steps = rows // BLOCK
    d_pre = shape_of(rows, wide, kind=HALF)
    total, wide_total = shape_of(steps, 1, width), shape_of(steps, 1, wide)

    def per_step(shape):
        return pl.BlockSpec((1,) + shape.shape[1:], lambda step, *scalars: (step, 0, 0))

    return dense_call(
        functools.partial(down_grad_kernel, chunk=chunk),
        "down_grad",
        rows,
        [
            (d_branch, by_rows(d_branch)),
            (slope, by_rows(slope)),
            (weight, resident(weight)),
        ],
        [
            (d_pre, by_rows(d_pre)),
            (total, per_step(total)),
            (wide_total, per_step(wide_total)),
        ],
        flops=2 * rows * width * wide,
    )


def project_kernel(x_ref, shift_ref, scale_ref, w_ref, bias_ref, hidden_ref, q_ref, k_ref, v_ref):
    for rows, part, _ in strips():
        normed, _ = row_norm(x_ref[rows, :].astype(FLOAT))
        hidden_ref[rows, :] = (normed * (1.0 + scale_ref[part]) + shift_ref[part]).astype(HALF)
    hidden = hidden_ref[...]
    width = hidden.shape[1]
    for index, ref in enumerate((q_ref, k_ref, v_ref)):
        place = pl.ds(index * width, width)
        ref[...] = (matmul(hidden, w_ref[:, place]) + bias_ref[:, place]).astype(HALF)


def project_call(tokens, shift, scale, weight, bias):
    rows, width = tokens.shape
    out = shape_of(rows, width, kind=HALF)
    return dense_call(
        project_kernel,
        "project",
        rows,
        [
            (tokens, by_rows(tokens)),
            (shift, by_rows(shift)),
            (scale, by_rows(scale)),
            (weight, resident(weight)),
            (bias, resident(bias)),
        ],
        [(out, by_rows(out))] * 4,
        flops=6 * rows * width * width,
    )


def mix_kernel(
    attended_ref, x_ref, gate_ref, shift_ref, scale_ref, w_ref, bias_ref, branch_ref, hidden_ref
):
    branch_ref[...] = matmul(attended_ref[...], w_ref[...]) + bias_ref[...]
    for rows, part, _ in strips():
        middle = x_ref[rows, :].astype(FLOAT) + gate_ref[part] * branch_ref[rows, :]
        normed, _ = row_norm(middle)
        hidden_ref[rows, :] = (normed * (1.0 + scale_ref[part]) + shift_ref[part]).astype(HALF)


def mix_call(attended, tokens, gate, shift, scale, weight, bias):
    rows, width = tokens.shape
    branch, hidden = shape_of(rows, width), shape_of(rows, width, kind=HALF)
    return dense_call(
        mix_kernel,
        "mix",
        rows,
        [
            (attended, by_rows(attended)),
            (tokens, by_rows(tokens)),
            (gate, by_rows(gate)),
            (shift, by_rows(shift)),
            (scale, by_rows(scale)),
            (weight, resident(weight)),
            (bias, resident(bias)),
        ],
        [(branch, by_rows(branch)), (hidden, by_rows(hidden))],
        flops=2 * rows * width * width,
    )


def finish_kernel(
    act_ref, x_ref, branch_ref, cot_ref, gate_one_ref, gate_two_ref, w_ref, bias_ref,
    own_ref, other_ref, sum_ref, branch_two,
):
    branch_two[...] = matmul(act_ref[...], w_ref[...]) + bias_ref[...]
    step = pl.program_id(0)
    sums = Sums()
    for rows, part, first in strips():
        middle = x_ref[rows, :].astype(FLOAT) + gate_one_ref[part] * branch_ref[rows, :]
        two = branch_two[rows, :]
        sums.add(sum_ref, part, first, cot_ref[rows, :].astype(FLOAT) * two)
        branch_two[rows, :] = middle + gate_two_ref[part] * two
    sums.store()
    store_strip(step, branch_two, own_ref, other_ref)


def store_strip(step, value_ref, own_ref, other_ref):
    half = pl.num_programs(0) // 2

    @pl.when(step < half)
    def _():
        own_ref[...] = value_ref[...]

    @pl.when(step >= half)
    def _():
        other_ref[...] = value_ref[...].astype(HALF)


def strip_specs(rows, width):
    half = rows // BLOCK // 2
    both, other = shape_of(2, rows // 2, width), shape_of(rows // 2, width, kind=HALF)

    def own_place(step, strip):
        return strip[0], jnp.minimum(step, half - 1), 0

    def other_place(step, strip):
        return jnp.maximum(step - half, 0), 0

    return [
        (both, pl.BlockSpec((None, BLOCK, width), own_place)),
        (other, pl.BlockSpec((BLOCK, width), other_place)),
    ]


def join_kernel(own_ref, other_ref, gate_ref, both_ref, d_branch_ref):
    first = pl.program_id(0) < pl.num_programs(0) // 2
    both_ref[...] = jnp.where(first, own_ref[...].astype(FLOAT), other_ref[...].astype(FLOAT)).astype(HALF)
    for rows, part, _ in strips():
        d_branch_ref[rows, :] = (both_ref[rows, :].astype(FLOAT) * gate_ref[part]).astype(HALF)


def join_call(pair, other, gate, strip):
    half, width = other.shape
    steps = half // BLOCK
    out = shape_of(2 * half, width, kind=HALF)
    own_spec = pl.BlockSpec(
        (None, BLOCK, width), lambda step, strip: (strip[0], jnp.minimum(step, steps - 1), 0)
    )
    other_spec = pl.BlockSpec(
        (BLOCK, width), lambda step, strip: (jnp.maximum(step - steps, 0), 0)
    )
    return dense_call(
        join_kernel,
        "join",
        2 * half,
        [(pair, own_spec), (other, other_spec), (gate, by_rows(gate))],
        [(out, by_rows(out)), (out, by_rows(out))],
        strip=strip,
    )


def fill_kernel(strip, both_ref, other_ref, out_ref):
    out_ref[...] = other_ref[...].astype(FLOAT)


def fill_call(both, other, strip):
    rows, width = other.shape
    return pl.pallas_call(
        fill_kernel,
        grid_spec=pltpu.PrefetchScalarGridSpec(
            num_scalar_prefetch=1,
            grid=(rows // BLOCK,),
            in_specs=[
                pl.BlockSpec(memory_space=pl.ANY),
                pl.BlockSpec((BLOCK, width), lambda step, strip: (step, 0)),
            ],
            out_specs=pl.BlockSpec(
                (None, BLOCK, width), lambda step, strip: (1 - strip[0], step, 0)
            ),
        ),
        out_shape=jax.ShapeDtypeStruct(both.shape, both.dtype),
        input_output_aliases={1: 0},
        cost_estimate=pl.CostEstimate(flops=0, bytes_accessed=8 * 2**20, transcendentals=0),
        name="fill",
    )(strip.reshape(1).astype(jnp.int32), both, other)


def finish_call(active, tokens, branch, cotangent, gate_one, gate_two, weight, bias, strip):
    rows, width = tokens.shape
    sums = shape_of(rows // PART, 1, width)
    return dense_call(
        finish_kernel,
        "finish",
        rows,
        [
            (active, by_rows(active)),
            (tokens, by_rows(tokens)),
            (branch, by_rows(branch)),
            (cotangent, by_rows(cotangent)),
            (gate_one, by_rows(gate_one)),
            (gate_two, by_rows(gate_two)),
            (weight, resident(weight)),
            (bias, resident(bias)),
        ],
        strip_specs(rows, width) + [(sums, by_rows(sums))],
        scratch=[pltpu.VMEM((BLOCK, width), FLOAT)],
        flops=2 * rows * active.shape[1] * width,
        strip=strip,
    )


def norm_pull(normed, inverse, grad):
    mean_grad = jnp.mean(grad, axis=1, keepdims=True)
    mean_cross = jnp.mean(grad * normed, axis=1, keepdims=True)
    return inverse * (grad - mean_grad - normed * mean_cross)


def mix_grad_kernel(
    d_pre_ref, attended_ref, x_ref, branch_ref, cot_ref, gate_ref, scale_ref, up_ref, out_ref,
    d_middle_ref, d_branch_ref, d_attended_ref, delta_ref, shift_sum, scale_sum, gate_sum, bias_sum, hidden,
):
    columns = up_ref.shape[2]
    hidden[...] = right_outer(d_pre_ref[:, :columns], up_ref[0]) + right_outer(
        d_pre_ref[:, columns:], up_ref[1]
    )
    sums = Sums()
    for rows, part, first in strips():
        branch, grad = branch_ref[rows, :], hidden[rows, :]
        gate = gate_ref[part]
        normed, inverse = row_norm(x_ref[rows, :].astype(FLOAT) + gate * branch)
        sums.add(shift_sum, part, first, grad)
        sums.add(scale_sum, part, first, grad * normed)
        d_middle = cot_ref[rows, :].astype(FLOAT) + norm_pull(
            normed, inverse, grad * (1.0 + scale_ref[part])
        )
        d_middle_ref[rows, :] = d_middle
        sums.add(gate_sum, part, first, d_middle * branch)
        d_branch = (d_middle * gate).astype(HALF)
        d_branch_ref[rows, :] = d_branch
        sums.add(bias_sum, part, first, d_branch.astype(FLOAT))
    sums.store()
    d_attended = right_outer(d_branch_ref[...], out_ref[...]).astype(HALF)
    d_attended_ref[...] = d_attended
    product = d_attended.astype(FLOAT) * attended_ref[...].astype(FLOAT)
    heads, width = HEADS, product.shape[1]
    lane = lax.broadcasted_iota(jnp.int32, (heads, width), 1)
    head = lax.broadcasted_iota(jnp.int32, (heads, width), 0) * HEAD
    member = jnp.where((lane >= head) & (lane < head + HEAD), 1.0, 0.0).astype(HALF)
    high = product.astype(HALF)
    low = (product - high.astype(FLOAT)).astype(HALF)
    delta = right_outer(member, high) + right_outer(member, low)
    for index in range(heads):
        delta_ref[index] = delta[index : index + 1]


def mix_grad_call(d_pre, attended, tokens, branch, cotangent, gate, scale, up, out):
    rows, width = tokens.shape
    half, sums = shape_of(rows, width, kind=HALF), shape_of(rows // PART, 1, width)
    d_middle, delta = shape_of(rows, width), shape_of(HEADS, 1, rows)
    return dense_call(
        mix_grad_kernel,
        "mix_grad",
        rows,
        [
            (d_pre, by_rows(d_pre)),
            (attended, by_rows(attended)),
            (tokens, by_rows(tokens)),
            (branch, by_rows(branch)),
            (cotangent, by_rows(cotangent)),
            (gate, by_rows(gate)),
            (scale, by_rows(scale)),
            (up, resident(up)),
            (out, resident(out)),
        ],
        [(d_middle, by_rows(d_middle)), (half, by_rows(half)), (half, by_rows(half))]
        + [(delta, pl.BlockSpec((HEADS, 1, BLOCK), lambda step, *scalars: (0, 0, step)))]
        + [(sums, by_rows(sums))] * 4,
        scratch=[pltpu.VMEM((BLOCK, width), FLOAT)],
        flops=2 * rows * width * (d_pre.shape[1] + width),
    )


def project_grad_kernel(
    dq_ref, dk_ref, dv_ref, x_ref, d_middle_ref, scale_ref, w_ref,
    own_ref, other_ref, shift_sum, scale_sum, query_sum, value_sum, hidden,
):
    grads = jnp.concatenate([dq_ref[...], dk_ref[...], dv_ref[...]], axis=1)
    hidden[...] = right_outer(grads, w_ref[...])
    sums = Sums()
    for rows, part, first in strips():
        grad = hidden[rows, :]
        normed, inverse = row_norm(x_ref[rows, :].astype(FLOAT))
        sums.add(shift_sum, part, first, grad)
        sums.add(scale_sum, part, first, grad * normed)
        sums.add(query_sum, part, first, dq_ref[rows, :].astype(FLOAT))
        sums.add(value_sum, part, first, dv_ref[rows, :].astype(FLOAT))
        hidden[rows, :] = d_middle_ref[rows, :] + norm_pull(
            normed, inverse, grad * (1.0 + scale_ref[part])
        )
    sums.store()
    store_strip(pl.program_id(0), hidden, own_ref, other_ref)


def project_grad_call(d_query, d_keys, d_values, tokens, d_middle, scale, weight, strip):
    rows, width = tokens.shape
    sums = shape_of(rows // PART, 1, width)
    return dense_call(
        project_grad_kernel,
        "project_grad",
        rows,
        [
            (d_query, by_rows(d_query)),
            (d_keys, by_rows(d_keys)),
            (d_values, by_rows(d_values)),
            (tokens, by_rows(tokens)),
            (d_middle, by_rows(d_middle)),
            (scale, by_rows(scale)),
            (weight, resident(weight)),
        ],
        strip_specs(rows, width) + [(sums, by_rows(sums))] * 4,
        scratch=[pltpu.VMEM((BLOCK, width), FLOAT)],
        flops=6 * rows * width * width,
        strip=strip,
    )


MESH = pl.DeviceIdType.MESH


class Place:
    def __init__(self):
        me = lax.axis_index("dp")
        self.me, self.y = me, lax.axis_index("blk")
        self.z, self.x, self.core = me // 4, (me // 2) % 2, me % 2

    def at(self, z_step, x_step, core_step):
        z = (self.z + 4 - z_step) % 4
        return z * 4 + ((self.x + x_step) % 2) * 2 + (self.core + core_step) % 2

    def half(self, y_step):
        return (self.y + y_step) % 2

    def partner(self, kind):
        if kind == "y":
            return {"blk": 1 - self.y}
        if kind == "z":
            return {"dp": (self.me + 4) % 16}
        if kind == "back":
            return {"dp": (self.me + 12) % 16}
        if kind == "x":
            return {"dp": self.at(0, 1, 0)}
        return {"dp": self.at(0, 0, 1)}

    def greet(self):
        barrier = pltpu.get_barrier_semaphore()
        for kind in ("y", "z", "back", "x", "core"):
            pl.semaphore_signal(
                barrier, inc=1, device_id=self.partner(kind), device_id_type=MESH
            )
        pl.semaphore_wait(barrier, 5)


class Copies:
    def __init__(self, place, send_sems, recv_sems):
        self.place, self.send_sems, self.recv_sems = place, send_sems, recv_sems
        self.made = {}

    def send(self, key, source, target):
        index = len(self.made)
        copy = pltpu.make_async_remote_copy(
            src_ref=source,
            dst_ref=target,
            send_sem=self.send_sems.at[index],
            recv_sem=self.recv_sems.at[index],
            device_id=self.place.partner(key[0]),
            device_id_type=MESH,
        )
        self.made[key] = copy
        copy.start()

    def receive(self, key):
        self.made[key].wait_recv()

    def finish(self):
        for copy in self.made.values():
            copy.wait_send()


def head_kernel(
    joint_ref,
    output_ref,
    condition_ref,
    adaptive_ref,
    bias_ref,
    tokens_ref,
    whole_joint_ref,
    whole_output_ref,
    modulation_ref,
    act_ref,
    other_ref,
    joint_from_y,
    output_from_y,
    joint_slot,
    output_slot,
    conditions,
    parts,
    from_core,
    from_x,
    from_z,
    share,
    from_y,
    local_sems,
    send_sems,
    recv_sems,
):
    place = Place()
    copies = Copies(place, send_sems, recv_sems)
    place.greet()
    conditions[place.me] = condition_ref[...]

    def condition(kind, z_step, x_step):
        slot = conditions.at[place.at(z_step, x_step, 0)]
        copies.send((kind, "condition", z_step, x_step), slot, slot)

    def weight(kind, z_step, x_step):
        for name, slot, whole in (
            ("joint", joint_slot, whole_joint_ref),
            ("output", output_slot, whole_output_ref),
        ):
            target = whole.at[place.at(z_step, x_step, 0)]
            mine = z_step == 0 and x_step == 0
            copies.send((kind, name, z_step, x_step), slot if mine else target, target)

    def arrived(kind, z_step, x_step):
        copies.receive((kind, "joint", z_step, x_step))
        copies.receive((kind, "output", z_step, x_step))

    def forward_condition(z_step):
        for x_step in range(2):
            copies.receive(("z", "condition", z_step - 1, x_step))
            if z_step < 3:
                condition("z", z_step, x_step)
            condition("core", z_step, x_step)

    def forward(z_step):
        arrived("z", z_step - 1, 0)
        if z_step < 3:
            weight("z", z_step, 0)
        weight("x", z_step, 0)
        weight("core", z_step, 0)

    copies.send(("y", "joint"), joint_ref, joint_from_y)
    copies.send(("y", "output"), output_ref, output_from_y)
    condition("x", 0, 0)
    condition("z", 0, 0)
    condition("core", 0, 0)
    copies.send(("y", "tokens"), tokens_ref.at[place.half(1)], other_ref)
    copies.receive(("x", "condition", 0, 0))
    condition("z", 0, 1)
    condition("core", 0, 1)
    forward_condition(1)

    owns = []
    for name, mine, other, slot, whole in (
        ("joint", joint_ref, joint_from_y, joint_slot, whole_joint_ref),
        ("output", output_ref, output_from_y, output_slot, whole_output_ref),
    ):
        copies.receive(("y", name))
        first, second = mine[...].astype(FLOAT), other[...].astype(FLOAT)
        low = place.y == 0
        slot[...] = jnp.concatenate(
            [jnp.where(low, first, second), jnp.where(low, second, first)], axis=1
        ).astype(HALF)
        own = pltpu.make_async_copy(slot, whole.at[place.me], local_sems.at[len(owns)])
        own.start()
        owns.append(own)
    weight("z", 0, 0)
    weight("x", 0, 0)
    weight("core", 0, 0)
    forward_condition(2)
    forward_condition(3)
    forward(1)
    for z_step in range(4):
        for x_step in range(2):
            copies.receive(("core", "condition", z_step, x_step))

    adaptive = adaptive_ref[...]
    count, rows = conditions.shape[0], conditions.shape[2]
    for index in range(count):
        values = conditions[index, place.me].astype(FLOAT)
        act_ref[index] = (values / (1.0 + jnp.exp(-values))).astype(HALF)

    def products(core_step):
        targets = [
            place.at((4 - z_step) % 4, x_step, core_step)
            for z_step in range(4)
            for x_step in range(2)
        ]
        acts = jnp.concatenate([act_ref[target] for target in targets], axis=0)
        product = matmul(acts, adaptive).astype(HALF)
        parts[core_step] = product.reshape(parts.shape[1:])

    def add(first, second):
        return first.astype(FLOAT) + second.astype(FLOAT)

    products(1)
    for z_step in (3, 2, 1, 0):
        copies.send(("core", "part", z_step), parts.at[1, z_step], from_core.at[z_step])
    products(0)
    for z_step in (3, 2, 1, 0):
        copies.receive(("core", "part", z_step))
        total = add(parts[0, z_step], from_core[z_step])
        if z_step < 3:
            copies.receive(("z", "part", z_step + 1))
            total = total + from_z[z_step].astype(FLOAT)
        parts[0, z_step] = total.astype(HALF)
        if z_step > 0:
            copies.send(("z", "part", z_step), parts.at[0, z_step], from_z.at[z_step - 1])
        if z_step == 3:
            forward(2)
        if z_step == 2:
            forward(3)
    copies.send(("x", "part"), parts.at[0, 0, 1], from_x)

    def last(z_step):
        arrived("x", z_step, 0)
        weight("core", z_step, 1)

    last(0)
    last(1)
    images = rows // 2
    copies.receive(("x", "part"))
    total = add(parts[0, 0, 0], from_x[...]) + bias_ref[...]
    share[0] = total[:images]
    share[1] = total[images:]
    copies.send(("y", "part"), share.at[place.half(1)], from_y)
    modulation_ref[place.half(0)] = share[place.half(0)]
    last(2)
    last(3)
    copies.receive(("y", "part"))
    modulation_ref[place.half(1)] = from_y[...]
    for z_step in range(4):
        for x_step in range(2):
            arrived("core", z_step, x_step)
    copies.receive(("y", "tokens"))
    for own in owns:
        own.wait()
    copies.finish()


def head(joint_weight, output_weight, condition, adaptive_weight, adaptive_bias, tokens):
    micro, images, width = condition.shape
    features, columns = adaptive_weight.shape
    rows = micro * images
    condition = condition.reshape(rows, width // features, features).transpose(1, 0, 2)
    count = 16
    vmem = pl.BlockSpec(memory_space=pltpu.VMEM)
    anywhere = pl.BlockSpec(memory_space=pl.ANY)
    slots = [(shard.shape[0], 2 * shard.shape[1]) for shard in (joint_weight, output_weight)]
    joint, output, modulation, act, other = pl.pallas_call(
        head_kernel,
        out_shape=[jax.ShapeDtypeStruct((count,) + slot, HALF) for slot in slots]
        + [
            jax.ShapeDtypeStruct((2, images, columns), FLOAT),
            jax.ShapeDtypeStruct((count, rows, features), HALF),
            jax.ShapeDtypeStruct(tokens.shape[1:], HALF),
        ],
        in_specs=[vmem] * 5 + [anywhere],
        out_specs=[anywhere, anywhere, vmem, vmem, anywhere],
        scratch_shapes=[
            pltpu.VMEM(joint_weight.shape, HALF),
            pltpu.VMEM(output_weight.shape, HALF),
            pltpu.VMEM(slots[0], HALF),
            pltpu.VMEM(slots[1], HALF),
            pltpu.VMEM((count,) + condition.shape, HALF),
            pltpu.VMEM((2, 4, 2, rows, columns), HALF),
            pltpu.VMEM((4, 2, rows, columns), HALF),
            pltpu.VMEM((rows, columns), HALF),
            pltpu.VMEM((3, 2, rows, columns), HALF),
            pltpu.VMEM((2, images, columns), FLOAT),
            pltpu.VMEM((images, columns), FLOAT),
            pltpu.SemaphoreType.DMA((2,)),
            pltpu.SemaphoreType.DMA((64,)),
            pltpu.SemaphoreType.DMA((64,)),
        ],
        compiler_params=pltpu.CompilerParams(
            collective_id=1, has_side_effects=True, vmem_limit_bytes=48 * 2**20
        ),
        cost_estimate=pl.CostEstimate(flops=0, bytes_accessed=200 * 2**20, transcendentals=0),
        name="head",
    )(
        joint_weight,
        output_weight,
        condition,
        adaptive_weight,
        adaptive_bias.astype(FLOAT)[None],
        tokens,
    )
    return (
        joint.reshape(-1, joint.shape[2]),
        output.reshape(-1, output.shape[2]),
        modulation,
        act,
        other,
    )


def tail_kernel(
    grad_ref,
    half_ref,
    vector_ref,
    strip_ref,
    share_ref,
    all_ref,
    total_ref,
    other_ref,
    own,
    from_core,
    from_x,
    from_z,
    half_sum,
    from_y,
    pair,
    pair_from_y,
    vector,
    vector_from,
    vector_z,
    local_sems,
    send_sems,
    recv_sems,
):
    place = Place()
    copies = Copies(place, send_sems, recv_sems)
    place.greet()

    def grad(z_step, x_step, core_step):
        return grad_ref.at[place.at((4 - z_step) % 4, x_step, core_step)]

    def modulation(kind, z_step, x_step):
        slot = all_ref.at[place.at(z_step, x_step, 0)]
        copies.send((kind, "modulation", z_step, x_step), slot, slot)

    copies.send(("y", "half"), half_ref.at[place.half(1)], pair_from_y)
    copies.send(("core", "vector"), vector_ref, vector_from.at[0])
    loads = {}
    for x_step in (1, 0):
        for z_step in (3, 2, 1, 0):
            copies.send(
                ("core", x_step, z_step),
                grad(z_step, x_step, 1),
                from_core.at[x_step, z_step],
            )
            load = pltpu.make_async_copy(
                grad(z_step, x_step, 0), own.at[x_step, z_step], local_sems.at[len(loads)]
            )
            load.start()
            loads[x_step, z_step] = load

    copies.receive(("core", "vector"))
    vector[0] = vector_ref[...] + vector_from[0]
    copies.send(("x", "vector"), vector.at[0], vector_from.at[1])
    pair[place.half(0)] = half_ref[place.half(0)]
    copies.receive(("y", "half"))
    pair[place.half(1)] = pair_from_y[...]
    all_ref[place.me] = pair[...].reshape(all_ref.shape[1:]).astype(HALF)
    modulation("x", 0, 0)
    modulation("z", 0, 0)
    modulation("core", 0, 0)

    def summed(x_step, z_step):
        loads[x_step, z_step].wait()
        copies.receive(("core", x_step, z_step))
        first = own[x_step, z_step].astype(FLOAT)
        return first + from_core[x_step, z_step].astype(FLOAT)

    def send_x(z_step):
        own[1, z_step] = summed(1, z_step).astype(HALF)
        copies.send(("x", z_step), own.at[1, z_step], from_x.at[z_step])

    def forward_modulation(z_step):
        for x_step in range(2):
            copies.receive(("z", "modulation", z_step - 1, x_step))
            if z_step < 3:
                modulation("z", z_step, x_step)
            modulation("core", z_step, x_step)

    def vector_ring(z_step):
        slot = vector_z.at[(place.z + 4 - z_step) % 4]
        copies.send(("z", "vector", z_step), slot, slot)

    send_x(3)
    copies.receive(("x", "vector"))
    vector[1] = vector[0] + vector_from[1]
    copies.send(("y", "vector"), vector.at[1], vector_from.at[2])
    copies.send(("y", "strip"), strip_ref, other_ref)
    copies.receive(("x", "modulation", 0, 0))
    modulation("z", 0, 1)
    modulation("core", 0, 1)
    send_x(2)
    copies.receive(("y", "vector"))
    vector_z[place.z] = vector[1] + vector_from[2]
    vector_ring(0)
    forward_modulation(1)
    send_x(1)
    copies.receive(("z", "vector", 0))
    vector_ring(1)
    forward_modulation(2)
    send_x(0)
    copies.receive(("z", "vector", 1))
    vector_ring(2)
    forward_modulation(3)
    for z_step in (3, 2, 1, 0):
        total = summed(0, z_step)
        copies.receive(("x", z_step))
        total = total + from_x[z_step].astype(FLOAT)
        if z_step < 3:
            copies.receive(("z", z_step + 1))
            total = total + from_z[z_step].astype(FLOAT)
        if z_step > 0:
            own[0, z_step] = total.astype(HALF)
            copies.send(("z", z_step), own.at[0, z_step], from_z.at[z_step - 1])
    cut = share_ref.shape[1]
    low, high = total[:, :cut], total[:, cut:]
    half_sum[...] = jnp.where(place.y == 0, high, low).astype(HALF)
    copies.send(("y",), half_sum, from_y)
    share_ref[...] = jnp.where(place.y == 0, low, high)
    copies.receive(("y",))
    share_ref[...] = share_ref[...] + from_y[...].astype(FLOAT)
    copies.receive(("z", "vector", 2))
    total_ref[...] = (vector_z[0] + vector_z[1]) + (vector_z[2] + vector_z[3])
    for z_step in range(4):
        for x_step in range(2):
            copies.receive(("core", "modulation", z_step, x_step))
    copies.receive(("y", "strip"))
    copies.finish()


def tail(grad, half, vector, strip):
    slot = grad.shape[1:]
    count = grad.shape[0]
    share = (slot[0], slot[1] // 2)
    images, columns = half.shape[1:]
    vmem = pl.BlockSpec(memory_space=pltpu.VMEM)
    anywhere = pl.BlockSpec(memory_space=pl.ANY)
    return pl.pallas_call(
        tail_kernel,
        out_shape=[
            jax.ShapeDtypeStruct(share, FLOAT),
            jax.ShapeDtypeStruct((count, 2 * images, columns), HALF),
            jax.ShapeDtypeStruct(vector.shape, FLOAT),
            jax.ShapeDtypeStruct(strip.shape, HALF),
        ],
        in_specs=[anywhere, vmem, vmem, anywhere],
        out_specs=[vmem, vmem, vmem, anywhere],
        scratch_shapes=[
            pltpu.VMEM((2, 4) + slot, HALF),
            pltpu.VMEM((2, 4) + slot, HALF),
            pltpu.VMEM((4,) + slot, HALF),
            pltpu.VMEM((3,) + slot, HALF),
            pltpu.VMEM(share, HALF),
            pltpu.VMEM(share, HALF),
            pltpu.VMEM(half.shape, FLOAT),
            pltpu.VMEM(half.shape[1:], FLOAT),
            pltpu.VMEM((2,) + vector.shape, FLOAT),
            pltpu.VMEM((3,) + vector.shape, FLOAT),
            pltpu.VMEM((4,) + vector.shape, FLOAT),
            pltpu.SemaphoreType.DMA((8,)),
            pltpu.SemaphoreType.DMA((64,)),
            pltpu.SemaphoreType.DMA((64,)),
        ],
        compiler_params=pltpu.CompilerParams(
            collective_id=2, has_side_effects=True, vmem_limit_bytes=48 * 2**20
        ),
        cost_estimate=pl.CostEstimate(flops=0, bytes_accessed=200 * 2**20, transcendentals=0),
        name="tail",
    )(grad, half, vector, strip)


def swap_blk(value):
    return lax.ppermute(value, "blk", [(0, 1), (1, 0)])


def share_columns(total, me_blk):
    half = total.shape[1] // 2
    keep = lax.dynamic_slice_in_dim(total, me_blk * half, half, 1)
    send = lax.dynamic_slice_in_dim(total, (1 - me_blk) * half, half, 1)
    return keep.astype(FLOAT) + swap_blk(send).astype(FLOAT)


def order_blk(first, mine, other, axis):
    return jnp.concatenate(
        [jnp.where(first, mine, other), jnp.where(first, other, mine)], axis=axis
    )


def pair_body(
    tokens,
    cotangent,
    condition,
    lengths,
    adaptive_weight,
    joint_weight,
    output_weight,
    up_weight,
    down_weight,
    adaptive_bias,
    query_bias,
    value_bias,
    output_bias,
    up_bias,
    down_bias,
):
    me_dp, me_blk = lax.axis_index("dp"), lax.axis_index("blk")
    first = me_blk == 0
    strip_rows, width = tokens.shape[2:]
    rows = 2 * strip_rows
    parts = strip_rows // 128
    images = lengths.shape[2]

    def mine_of(pair):
        return lax.dynamic_index_in_dim(pair, me_blk, 0, keepdims=False)

    def other_of(pair):
        return lax.dynamic_index_in_dim(pair, 1 - me_blk, 0, keepdims=False)

    joint, output_matrix, modulation, act_part, tokens_other = head(
        joint_weight, output_weight, condition[0], adaptive_weight, adaptive_bias, tokens[0]
    )
    modulation = jnp.concatenate([modulation[0], modulation[1]], axis=1)

    bias_mine = jnp.concatenate([query_bias, value_bias, output_bias, down_bias, up_bias])
    bias_other = swap_blk(bias_mine)
    small = width // 2

    def bias_of(begin, size):
        return order_blk(
            first, bias_mine[begin : begin + size], bias_other[begin : begin + size], 0
        ).astype(FLOAT)

    query_vector, value_vector = bias_of(0, small), bias_of(small, small)
    output_vector, down_vector = bias_of(2 * small, small), bias_of(3 * small, small)
    up_vector = bias_of(4 * small, up_bias.shape[0])

    joint, up_weight, down_weight = lax.optimization_barrier((joint, up_weight, down_weight))
    up_halves = lax.all_gather(up_weight, ("blk", "dp"), axis=0, tiled=True)
    up_halves = up_halves.reshape(2, width, -1)
    down_other = swap_blk(down_weight)
    cotangent_other = swap_blk(other_of(cotangent[0]))

    strip = mine_of(lengths[0]) // 2
    ends = jnp.cumsum(strip)
    starts = ends - strip
    begin = jnp.arange(parts, dtype=jnp.int32)[:, None] * 128
    inside = (begin >= starts[None, :]) & (begin < ends[None, :])
    member = jnp.tile(inside.astype(FLOAT), (2, 1))
    long = strip == 512
    used = strip > 0
    rank = jnp.where(
        long,
        jnp.cumsum(long) - 1,
        jnp.where(used, jnp.sum(long) + jnp.cumsum(used & ~long) - 1, images + 8),
    )
    info = jnp.sum(
        jnp.where(rank[:, None] == jnp.arange(8)[None, :], starts[:, None], 0), axis=0
    )
    kinds = jnp.where(jnp.arange(8) < jnp.sum(long), 1, 0)
    info = jnp.concatenate([info, kinds]).astype(jnp.int32)

    per_part = jnp.dot(member, modulation, precision=HIGHEST, preferred_element_type=FLOAT)
    per_part = per_part.reshape(2 * parts, 1, 6, width)
    shift_one, scale_one, gate_one, shift_two, scale_two, gate_two = (
        per_part[:, :, index] for index in range(6)
    )

    inputs = jnp.concatenate([mine_of(tokens[0]), tokens_other], axis=0)
    joint_vector = jnp.concatenate([query_vector, jnp.zeros_like(query_vector), value_vector])
    hidden_one, query, keys, values = project_call(
        inputs, shift_one, scale_one, joint, joint_vector[None]
    )
    query, down_weight = lax.optimization_barrier((query, down_weight))
    down_rows = order_blk(first, down_weight, down_other, 1)
    down_matrix = lax.all_gather(down_rows, "dp", axis=0, tiled=True)
    attended, total = attend_pack(info, query, keys, values)
    branch_one, hidden_two = mix_call(
        attended, inputs, gate_one, shift_two, scale_two, output_matrix, output_vector[None]
    )
    activated, slope = up_call(hidden_two, up_halves, up_vector[None])

    upstream, d_branch_two = join_call(cotangent[0], cotangent_other, gate_two, me_blk)
    d_branch_two, down_grad = lax.optimization_barrier(
        (d_branch_two, left_outer(activated, d_branch_two).astype(HALF))
    )
    down_total = lax.psum_scatter(down_grad, "dp", scatter_dimension=0, tiled=True)
    d_pre, down_sum, up_sum = down_grad_call(d_branch_two, slope, down_matrix)
    d_pre, up_grad = lax.optimization_barrier(
        (d_pre, left_outer(hidden_two, d_pre).astype(HALF))
    )
    up_total = lax.psum_scatter(up_grad, "dp", scatter_dimension=0, tiled=True)
    result, result_send, d_gate_two = finish_call(
        activated,
        inputs,
        branch_one,
        upstream,
        gate_one,
        gate_two,
        down_matrix,
        down_vector[None],
        me_blk,
    )
    d_pre, result_send = lax.optimization_barrier((d_pre, result_send))
    result_other = swap_blk(result_send)
    d_middle, d_branch_one, d_attended, delta, *part_totals = (
        mix_grad_call(
            d_pre, attended, inputs, branch_one, upstream, gate_one, scale_two, up_halves, output_matrix
        )
    )
    d_shift_two, d_scale_two, d_gate_one, output_sum = part_totals
    d_attended, output_grad, down_total = lax.optimization_barrier(
        (d_attended, left_outer(attended, d_branch_one).astype(HALF), down_total)
    )
    output_total = lax.psum_scatter(output_grad, "dp", scatter_dimension=0, tiled=True)
    down_share = share_columns(down_total, me_blk)
    d_query, d_keys, d_values = attend_pack_backward(
        info, query, keys, values, d_attended, total, delta
    )
    d_query, up_total, result_other = lax.optimization_barrier((d_query, up_total, result_other))
    up_share = share_columns(up_total, me_blk)
    result = fill_call(result, result_other, me_blk)
    d_projected = jnp.concatenate([d_query, d_keys, d_values], axis=1)
    joint_grad = left_outer(hidden_one, d_projected).astype(HALF)
    d_inputs, d_inputs_send, d_shift_one, d_scale_one, query_sum, value_sum = project_grad_call(
        d_query, d_keys, d_values, inputs, d_middle, scale_one, joint, me_blk
    )

    def part_rows(value):
        return value.reshape(2 * parts, width)

    d_parts = [d_shift_one, d_scale_one, d_gate_one, d_shift_two, d_scale_two, d_gate_two]
    d_parts = jnp.concatenate([part_rows(value) for value in d_parts], axis=1)
    d_modulation = lax.dot_general(
        member,
        d_parts,
        (((0,), (0,)), ((), ())),
        precision=HIGHEST,
        preferred_element_type=FLOAT,
    )
    vectors = [query_sum, value_sum, output_sum, down_sum, up_sum]
    sums = jnp.concatenate([jnp.sum(value, axis=(0, 1)) for value in vectors])
    joint_grad, output_total = lax.optimization_barrier((joint_grad, output_total))
    output_share = share_columns(output_total, me_blk)
    shard_rows = adaptive_weight.shape[0]
    joint_share, d_mod_all, sums, d_inputs_other = tail(
        joint_grad.reshape(16, shard_rows, -1),
        d_modulation.reshape(images, 2, -1).transpose(1, 0, 2),
        sums.reshape(-1, 128),
        d_inputs_send,
    )
    d_inputs = fill_call(d_inputs, d_inputs_other, me_blk)
    sums = sums.reshape(-1)
    d_mod_all = d_mod_all.reshape(-1, d_mod_all.shape[2])
    adaptive_share = left_outer(act_part.reshape(-1, shard_rows), d_mod_all)
    adaptive_vector_share = jnp.sum(d_mod_all.astype(FLOAT), axis=0)
    d_act = right_outer(d_mod_all, adaptive_weight)
    d_act = d_act.reshape(16, 2 * images, shard_rows)
    d_act = lax.all_to_all(d_act, "dp", 0, 0)
    d_act = d_act + swap_blk(d_act)
    d_act = d_act.transpose(1, 0, 2).reshape(2, images, width)
    condition_full = condition[0].astype(FLOAT)
    sigmoid_cond = jax.nn.sigmoid(condition_full)
    d_condition = d_act * sigmoid_cond * (1.0 + condition_full * (1.0 - sigmoid_cond))

    def share_of(begin, size):
        return lax.dynamic_slice_in_dim(sums, begin + me_blk * (size // 2), size // 2, 0)

    return (
        result[None],
        d_inputs[None],
        d_condition[None],
        adaptive_share,
        joint_share,
        output_share,
        up_share,
        down_share,
        adaptive_vector_share,
        share_of(0, width),
        share_of(width, width),
        share_of(2 * width, width),
        share_of(4 * width, 2 * up_bias.shape[0]),
        share_of(3 * width, width),
    )


def solution(mesh):
    in_specs = (
        P("dp", None, "blk", None),
        P("dp", None, "blk", None),
        P("dp", None, None, None),
        P("dp", None, None),
        P("dp", "blk"),
        P("dp", "blk"),
        P("dp", "blk"),
        P("dp", "blk"),
        P("dp", "blk"),
        P("blk"),
        P("blk"),
        P("blk"),
        P("blk"),
        P("blk"),
        P("blk"),
    )
    out_specs = (
        P("dp", None, "blk", None),
        P("dp", None, "blk", None),
        P("dp", None, None, None),
        P("dp", "blk"),
        P("dp", "blk"),
        P("dp", "blk"),
        P("dp", "blk"),
        P("dp", "blk"),
        P("blk"),
        P("blk"),
        P("blk"),
        P("blk"),
        P("blk"),
        P("blk"),
    )
    paired = mesh.shape["dp"] == 16 and mesh.shape["blk"] == 2
    body = pair_body if paired else general_body
    return jax.shard_map(body, mesh=mesh, in_specs=in_specs, out_specs=out_specs, check_vma=False)
```
